32 devices in a mesh: grp: 2 (over x), tile: 16 (over z, y, core).
Axes of the slice: x: 2, y: 2, z: 4, core: 2. Of those that a mesh axis runs over, the one named last changes fastest.
Arguments:
- features: bfloat16 [768, 48, 48, 128], P(('grp', 'tile')), parts along dimension 0, may hold values from -6 to 6
- edge_table: int32 [384, 4, 2], replicated, may hold values from 0 to 383, as said below
- w_enc0: bfloat16 [3, 3, 128, 128], replicated, may hold values from -0.25 to 0.25
- w_enc1: bfloat16 [3, 3, 128, 128], replicated, may hold values from -0.25 to 0.25
- w_enc2: bfloat16 [3, 3, 128, 128], replicated, may hold values from -0.25 to 0.25
- w_mid: bfloat16 [3, 3, 128, 128], replicated, may hold values from -0.25 to 0.25
- w_dec2: bfloat16 [3, 3, 256, 128], replicated, may hold values from -0.1875 to 0.1875
- w_dec1: bfloat16 [3, 3, 256, 128], replicated, may hold values from -0.1875 to 0.1875
- w_dec0: bfloat16 [3, 3, 256, 128], replicated, may hold values from -0.1875 to 0.1875
Outputs:
- decoded: bfloat16 [768, 48, 48, 128], P(('grp', 'tile')), parts along dimension 0
The draws below stay inside these ranges and needn't reach their ends.
There are 2 independent parts, one for each index of `grp`. The reference program is written for one: setup_inputs(seed, part) draws one part's arguments, and reference() takes and returns one part's arrays. A program takes and returns all parts, laid end to end along the dimension named above; an argument that names none is the same for every part. Nothing has to cross between parts.
Inputs may be any that keep to these rules, and one draw needn't show every extreme that they name: `edge_table`: edges are numbered 0 for row 0, 1 for the last column, 2 for the last row, 3 for column 0 of a tile; pairs are symmetric, with the same reversal flag on both sides. The tiles are those of a cube with 8 x 8 tiles a face, numbered face by face (faces +x, -x, +y, -y, +z, -z; on the face of axis k, rows run along axis k+1 and columns along axis k+2, modulo 3) and row by row within a face; blocks of 24 consecutive tiles of that numbering are placed on the devices in an order drawn at random, and the arrays hold the tiles in device order.
All inputs are finite; a program needn't handle non-finite values.
Results may differ from the reference program's by a relative error of at most 0.0053.
Values may be sent and summed in bfloat16 or wider, within the bound.
No kernel may reach another device: no remote copies, remote signals or barrier semaphores. Data moves between devices by JAX's collectives and lax.ppermute only.
A program may use at most 128 MiB of HBM per device.

```python
import jax
import jax.numpy as jnp
import numpy as np
from jax import lax

C = 128
FACE_TILES = 8
TILE = 48
TILES = 384
TILES_DEV = 24


def same_vector(first, second):
    return int(np.sum(np.abs(first - second))) == 0


def cube_links(tiles_side):
    basis = np.eye(3, dtype=np.int64)
    frames = []
    for axis_id in range(3):
        for orient in (1, -1):
            frames.append((orient * basis[axis_id], basis[(axis_id + 1) % 3], basis[(axis_id + 2) % 3]))
    per_face = tiles_side * tiles_side
    tile_total = 6 * per_face
    centres = np.zeros((tile_total, 3), np.int64)
    lookup = {}
    for face_id in range(6):
        normal, row_axis, col_axis = frames[face_id]
        for row_id in range(tiles_side):
            for col_id in range(tiles_side):
                slot_id = face_id * per_face + row_id * tiles_side + col_id
                centre = tiles_side * normal + (2 * row_id + 1 - tiles_side) * row_axis + (2 * col_id + 1 - tiles_side) * col_axis
                centres[slot_id] = centre
                lookup[tuple((int(entry) for entry in centre))] = slot_id
    partner = np.zeros((tile_total, 4), np.int64)
    matching = np.zeros((tile_total, 4), np.int64)
    flipped = np.zeros((tile_total, 4), np.int64)
    for slot_id in range(tile_total):
        normal, row_axis, col_axis = frames[slot_id // per_face]
        outward = (-row_axis, col_axis, row_axis, -col_axis)
        running = (col_axis, row_axis, col_axis, row_axis)
        for edge_id in range(4):
            beyond = tuple((int(entry) for entry in centres[slot_id] + 2 * outward[edge_id]))
            if beyond in lookup:
                other_slot = lookup[beyond]
                facing = -outward[edge_id]
            else:
                other_slot = lookup[tuple((int(entry) for entry in centres[slot_id] + outward[edge_id] - normal))]
                facing = normal
            other_normal, other_rows, other_cols = frames[other_slot // per_face]
            other_out = (-other_rows, other_cols, other_rows, -other_cols)
            other_run = (other_cols, other_rows, other_cols, other_rows)
            for candidate in range(4):
                if same_vector(other_out[candidate], facing):
                    matching[slot_id, edge_id] = candidate
                    flipped[slot_id, edge_id] = 0 if same_vector(other_run[candidate], running[edge_id]) else 1
            partner[slot_id, edge_id] = other_slot
    return (partner, matching, flipped)


def draw_edge_table(key, part):
    partner_slot, edge_slot, flip_slot = cube_links(FACE_TILES)
    blocks = TILES // TILES_DEV
    placing = jax.random.permutation(key, blocks).astype(jnp.int32)
    inverse = jnp.zeros((blocks,), jnp.int32).at[placing].set(jnp.arange(blocks, dtype=jnp.int32))
    labels = jnp.arange(TILES, dtype=jnp.int32)
    slot_of = placing[labels // TILES_DEV] * TILES_DEV + labels % TILES_DEV
    neighbour = jnp.asarray(partner_slot, jnp.int32)[slot_of]
    partner = inverse[neighbour // TILES_DEV] * TILES_DEV + neighbour % TILES_DEV
    codes = jnp.asarray(edge_slot * 2 + flip_slot, jnp.int32)[slot_of]
    return jnp.stack([partner, codes], axis=2).astype(jnp.int32)


def block_scale(key, extent, shards, least, high):
    def one(dim, parts):
        steps = jax.random.uniform(jax.random.fold_in(jax.random.fold_in(key, 6), dim), (parts,), jnp.float32, least / len(shards), high / len(shards))
        return jnp.repeat(jnp.exp(steps), extent[dim] // parts).reshape((-1,) + (1,) * (len(extent) - dim - 1))

    factor_of = one(*shards[0])
    for cut in shards[1:]:
        factor_of = factor_of * one(*cut)
    return factor_of


def scatter_about(stream_key, extent, spread, most, shards=(), kind=jnp.bfloat16):
    entries = jax.random.normal(stream_key, extent, jnp.float32) * spread
    if len(shards) > 0:
        entries = block_scale(stream_key, extent, shards, -0.22, 0.18) * entries
    return jnp.clip(entries, min=-most, max=most).astype(kind)


def setup_inputs(seed: int = 0, part: int = 0) -> dict:
    key_list = jax.random.split(jax.random.key(seed), 10)
    part_splits = jax.random.split(jax.random.fold_in(key_list[9], part), 10)
    return {
        "features": scatter_about(part_splits[0], (TILES, TILE, TILE, C), 1.0, 6.0, ((0, 16),)),
        "edge_table": draw_edge_table(jax.random.fold_in(key_list[9], 71), part),
        "w_enc0": scatter_about(key_list[2], (3, 3, C, C), (4 * C) ** -0.5, 0.25),
        "w_enc1": scatter_about(key_list[3], (3, 3, C, C), (4 * C) ** -0.5, 0.25),
        "w_enc2": scatter_about(key_list[4], (3, 3, C, C), (4 * C) ** -0.5, 0.25),
        "w_mid": scatter_about(key_list[5], (3, 3, C, C), (4 * C) ** -0.5, 0.25),
        "w_dec2": scatter_about(key_list[6], (3, 3, 2 * C, C), (8 * C) ** -0.5, 0.1875),
        "w_dec1": scatter_about(key_list[7], (3, 3, 2 * C, C), (8 * C) ** -0.5, 0.1875),
        "w_dec0": scatter_about(key_list[8], (3, 3, 2 * C, C), (8 * C) ** -0.5, 0.1875),
    }


def edge_rims(field):
    return jnp.stack([field[:, 0], field[:, :, -1], field[:, -1], field[:, :, 0]], axis=1)


def assemble(field, halo_rows):
    upper_side = halo_rows[:, 0]
    right_side = halo_rows[:, 1]
    lower_side = halo_rows[:, 2]
    left_side = halo_rows[:, 3]

    def corner(one_side, other_side):
        return ((one_side.astype(jnp.float32) + other_side.astype(jnp.float32)) * 0.5).astype(field.dtype)[:, None]

    upper_row = jnp.concatenate([corner(upper_side[:, 0], left_side[:, 0]), upper_side, corner(upper_side[:, -1], right_side[:, 0])], axis=1)
    lower_row = jnp.concatenate([corner(lower_side[:, 0], left_side[:, -1]), lower_side, corner(lower_side[:, -1], right_side[:, -1])], axis=1)
    middle_rows = jnp.concatenate([left_side[:, :, None], field, right_side[:, :, None]], axis=2)
    return jnp.concatenate([upper_row[:, None], middle_rows, lower_row[:, None]], axis=1)


def conv_layer(padded, weight):
    summed = lax.conv_general_dilated(padded.astype(jnp.float32), weight.astype(jnp.float32), (1, 1), "VALID", dimension_numbers=("NHWC", "HWIO", "NHWC"), precision=lax.Precision.HIGHEST)
    return jax.nn.silu(summed).astype(jnp.bfloat16)


def shrink(field):
    count, length, _, channels = field.shape
    blocks = field.astype(jnp.float32).reshape(count, length // 2, 2, length // 2, 2, channels)
    return (jnp.sum(blocks, axis=(2, 4)) * 0.25).astype(jnp.bfloat16)


def enlarge(field):
    return jnp.repeat(jnp.repeat(field, 2, axis=1), 2, axis=2)


def reference(features, edge_table, w_enc0, w_enc1, w_enc2, w_mid, w_dec2, w_dec1, w_dec0):
    partner = edge_table[:, :, 0]
    matching = edge_table[:, :, 1] // 2
    reversal = edge_table[:, :, 1] % 2 == 1

    def surround(field):
        strips = edge_rims(field)
        arrived = strips[partner, matching]
        arrived = jnp.where(reversal[:, :, None, None], arrived[:, :, ::-1], arrived)
        return assemble(field, arrived)

    enc0 = conv_layer(surround(features), w_enc0)
    enc1 = conv_layer(surround(shrink(enc0)), w_enc1)
    enc2 = conv_layer(surround(shrink(enc1)), w_enc2)
    middle = conv_layer(surround(shrink(enc2)), w_mid)
    dec2 = conv_layer(surround(jnp.concatenate([enlarge(middle), enc2], axis=3)), w_dec2)
    dec1 = conv_layer(surround(jnp.concatenate([enlarge(dec2), enc1], axis=3)), w_dec1)
    return conv_layer(surround(jnp.concatenate([enlarge(dec1), enc0], axis=3)), w_dec0)
```

```python
import jax
import jax.numpy as jnp
import numpy as np
from jax import lax
from jax.experimental import pallas as pl
from jax.experimental.pallas import tpu as pltpu
from jax.sharding import PartitionSpec as P

FACE_TILES = 8
VMEM_LIMIT = 50 * 2**20
BF = jnp.bfloat16
F32 = jnp.float32


def cube_links(tiles_side):
    basis = np.eye(3, dtype=np.int64)
    frames = []
    for axis_id in range(3):
        for orient in (1, -1):
            frames.append(
                (orient * basis[axis_id], basis[(axis_id + 1) % 3], basis[(axis_id + 2) % 3])
            )
    per_face = tiles_side * tiles_side
    tile_total = 6 * per_face
    centres = np.zeros((tile_total, 3), np.int64)
    lookup = {}
    for face_id in range(6):
        normal, row_axis, col_axis = frames[face_id]
        for row_id in range(tiles_side):
            for col_id in range(tiles_side):
                slot_id = face_id * per_face + row_id * tiles_side + col_id
                centre = (
                    tiles_side * normal
                    + (2 * row_id + 1 - tiles_side) * row_axis
                    + (2 * col_id + 1 - tiles_side) * col_axis
                )
                centres[slot_id] = centre
                lookup[tuple((int(entry) for entry in centre))] = slot_id
    partner = np.zeros((tile_total, 4), np.int64)
    for slot_id in range(tile_total):
        normal, row_axis, col_axis = frames[slot_id // per_face]
        outward = (-row_axis, col_axis, row_axis, -col_axis)
        for edge_id in range(4):
            beyond = tuple((int(entry) for entry in centres[slot_id] + 2 * outward[edge_id]))
            if beyond in lookup:
                partner[slot_id, edge_id] = lookup[beyond]
            else:
                partner[slot_id, edge_id] = lookup[
                    tuple((int(entry) for entry in centres[slot_id] + outward[edge_id] - normal))
                ]
    return partner


def pair_capacity(tiles_side, tiles_here):
    partner = cube_links(tiles_side)
    tile_total = partner.shape[0]
    blocks = tile_total // tiles_here
    source = np.repeat(np.arange(tile_total) // tiles_here, 4)
    target = partner.reshape(-1) // tiles_here
    identity = np.eye(blocks, dtype=np.int64)
    shared = identity[source].T @ identity[target]
    shared = shared * (1 - identity)
    return max(int(shared.max()), 1)


def routing_plan(edge_table, position, tiles_here, slot_count, devices):
    strip_count = tiles_here * 4
    own_rows = lax.dynamic_slice_in_dim(edge_table, position * tiles_here, tiles_here, 0).reshape(
        strip_count, 2
    )
    partner = own_rows[:, 0]
    matching = own_rows[:, 1] // 2
    reversed_rows = own_rows[:, 1] % 2
    target = partner // tiles_here
    order = jnp.arange(strip_count, dtype=jnp.int32)
    earlier = (order[None, :] < order[:, None]) & (target[None, :] == target[:, None])
    slot_rank = jnp.sum(earlier.astype(jnp.int32), axis=1)
    remote = target != position
    slot_row = jnp.where(remote, target * slot_count + slot_rank, -1)
    source_tiles = target[:, None] * tiles_here + jnp.arange(tiles_here, dtype=jnp.int32)[None, :]
    their_partners = jnp.take(edge_table[:, :, 0], source_tiles, axis=0).reshape(
        strip_count, strip_count
    )
    toward_me = their_partners // tiles_here == position
    wanted = partner % tiles_here * 4 + matching
    before_wanted = order[None, :] < wanted[:, None]
    recv_rank = jnp.sum((toward_me & before_wanted).astype(jnp.int32), axis=1)
    pick_row = jnp.where(remote, target * slot_count + recv_rank, devices * slot_count + wanted)
    return (slot_row, pick_row, reversed_rows)


def edge_rims(field):
    return jnp.stack([field[:, 0], field[:, :, -1], field[:, -1], field[:, :, 0]], axis=1)


def assemble(field, halo_rows):
    upper_side = halo_rows[:, 0]
    right_side = halo_rows[:, 1]
    lower_side = halo_rows[:, 2]
    left_side = halo_rows[:, 3]

    def corner(one_side, other_side):
        return ((one_side.astype(F32) + other_side.astype(F32)) * 0.5).astype(field.dtype)[:, None]

    upper_row = jnp.concatenate(
        [
            corner(upper_side[:, 0], left_side[:, 0]),
            upper_side,
            corner(upper_side[:, -1], right_side[:, 0]),
        ],
        axis=1,
    )
    lower_row = jnp.concatenate(
        [
            corner(lower_side[:, 0], left_side[:, -1]),
            lower_side,
            corner(lower_side[:, -1], right_side[:, -1]),
        ],
        axis=1,
    )
    middle_rows = jnp.concatenate([left_side[:, :, None], field, right_side[:, :, None]], axis=2)
    return jnp.concatenate([upper_row[:, None], middle_rows, lower_row[:, None]], axis=1)


def conv_layer(padded, weight):
    summed = lax.conv_general_dilated(
        padded,
        weight,
        (1, 1),
        "VALID",
        dimension_numbers=("NHWC", "HWIO", "NHWC"),
        preferred_element_type=F32,
    )
    return jax.nn.silu(summed).astype(BF)


def shrink(field):
    count, length, _, channels = field.shape
    blocks = field.astype(F32).reshape(count, length // 2, 2, length // 2, 2, channels)
    return (jnp.sum(blocks, axis=(2, 4)) * 0.25).astype(BF)


def enlarge(field):
    return jnp.repeat(jnp.repeat(field, 2, axis=1), 2, axis=2)


def up16(n):
    return (n + 15) // 16 * 16


def params():
    return pltpu.CompilerParams(vmem_limit_bytes=VMEM_LIMIT)


def column_strips(read_cols, n, colbuf):
    colbuf[...] = read_cols(0).reshape(n * 8, 128)
    left = colbuf[pl.ds(0, n, 8), :]
    colbuf[...] = read_cols(n - 8).reshape(n * 8, 128)
    right = colbuf[pl.ds(7, n, 8), :]
    return left, right


def rims_kernel(x_ref, out_ref, colbuf):
    n = x_ref.shape[1]
    left, right = column_strips(lambda lo: x_ref[0, :, lo : lo + 8, :].astype(F32), n, colbuf)
    out_ref[0, 0] = x_ref[0, 0]
    out_ref[0, 1] = right.astype(BF)
    out_ref[0, 2] = x_ref[0, n - 1]
    out_ref[0, 3] = left.astype(BF)


def tile_rims(x):
    tiles, n, _, c = x.shape
    return pl.pallas_call(
        rims_kernel,
        grid=(tiles,),
        in_specs=[pl.BlockSpec((1, n, n, c), lambda i: (i, 0, 0, 0))],
        out_specs=pl.BlockSpec((1, 4, n, c), lambda i: (i, 0, 0, 0)),
        out_shape=jax.ShapeDtypeStruct((tiles, 4, n, c), BF),
        scratch_shapes=[pltpu.VMEM((n * 8, 128), F32)],
        compiler_params=params(),
        name="tile_rims",
    )(x)


def pack_kernel(slot_ref, rims_ref, send_ref):
    def step(i, carry):
        slot = slot_ref[i]

        @pl.when(slot >= 0)
        def _():
            send_ref[slot] = rims_ref[i]

        return carry

    lax.fori_loop(0, rims_ref.shape[0], step, 0)


def pack_strips(slot_row, rims, rows):
    strips, length, c = rims.shape
    return pl.pallas_call(
        pack_kernel,
        in_specs=[
            pl.BlockSpec(memory_space=pltpu.SMEM),
            pl.BlockSpec(memory_space=pltpu.VMEM),
        ],
        out_specs=pl.BlockSpec(memory_space=pltpu.VMEM),
        out_shape=jax.ShapeDtypeStruct((rows, length, c), BF),
        compiler_params=params(),
        name="pack_strips",
    )(slot_row, rims)


def route_kernel(pick_ref, rev_ref, recv_ref, own_ref, out_ref):
    rows = recv_ref.shape[0]
    length = recv_ref.shape[1]
    ri = lax.broadcasted_iota(jnp.int32, (length, length), 0)
    ci = lax.broadcasted_iota(jnp.int32, (length, length), 1)
    flip = (ri + ci == length - 1).astype(F32).astype(BF)

    def step(i, carry):
        pick = pick_ref[i]

        @pl.when(pick < rows)
        def _():
            out_ref[i] = recv_ref[jnp.minimum(pick, rows - 1)]

        @pl.when(pick >= rows)
        def _():
            out_ref[i] = own_ref[jnp.maximum(pick - rows, 0)]

        @pl.when(rev_ref[i] == 1)
        def _():
            out_ref[i] = jnp.dot(flip, out_ref[i], preferred_element_type=F32).astype(BF)

        return carry

    lax.fori_loop(0, out_ref.shape[0], step, 0)


def route_strips(pick_row, rev, recv, own):
    strips, length, c = own.shape
    smem = pl.BlockSpec(memory_space=pltpu.SMEM)
    vmem = pl.BlockSpec(memory_space=pltpu.VMEM)
    return pl.pallas_call(
        route_kernel,
        in_specs=[smem, smem, vmem, vmem],
        out_specs=vmem,
        out_shape=jax.ShapeDtypeStruct((strips, length, c), BF),
        compiler_params=params(),
        name="route_strips",
    )(pick_row, rev, recv, own)


def corner_cell(a, b):
    return ((a + b) * 0.5).astype(BF).astype(F32)


def shifted(x, n, first, last):
    axis = x.ndim - 2
    sub = lax.broadcasted_iota(jnp.int32, first.shape, axis)
    down = pltpu.roll(x, 1, axis)
    up = pltpu.roll(x, n - 1, axis)
    head = jnp.where(sub == 0, first, lax.slice_in_dim(down, 0, 8, axis=axis))
    tail = jnp.where(sub == 7, last, lax.slice_in_dim(up, n - 8, n, axis=axis))
    down = jnp.concatenate([head, lax.slice_in_dim(down, 8, n, axis=axis)], axis=axis)
    up = jnp.concatenate([lax.slice_in_dim(up, 0, n - 8, axis=axis), tail], axis=axis)
    return down, up


def spread_columns(strip, n, sublane, buf):
    buf[pl.ds(sublane, n, 8), :] = strip
    return buf[...].reshape(n, 8, 128)


def cell8(cell):
    return jnp.broadcast_to(cell, (8, 128))


def padded_rows(x, halo, n, buf_l, buf_r):
    top, right, bottom, left = halo
    first = spread_columns(left, n, 0, buf_l)
    last = spread_columns(right, n, 7, buf_r)
    body_d, body_u = shifted(x, n, first, last)
    tl = corner_cell(top[0:1], left[0:1])
    tr = corner_cell(top[n - 1 : n], right[0:1])
    bl = corner_cell(bottom[0:1], left[n - 1 : n])
    br = corner_cell(bottom[n - 1 : n], right[n - 1 : n])
    top_d, top_u = shifted(top, n, cell8(tl), cell8(tr))
    bot_d, bot_u = shifted(bottom, n, cell8(bl), cell8(br))
    return (top_d, top, top_u), (body_d, x, body_u), (bot_d, bottom, bot_u)


def fill_pairs(y_ref, x, halo, n, buf_l, buf_r):
    half = n // 2
    top, body, bottom = padded_rows(x, halo, n, buf_l, buf_r)
    for s in range(3):
        b = body[s].astype(BF).reshape(half, 2, n, 128)
        y_ref[0, 0:n, s * 128 : s * 128 + 128] = top[s].astype(BF)
        y_ref[0:half, 0:n, 384 + s * 128 : 384 + s * 128 + 128] = b[:, 0]
        y_ref[1 : half + 1, 0:n, s * 128 : s * 128 + 128] = b[:, 1]
        y_ref[half, 0:n, 384 + s * 128 : 384 + s * 128 + 128] = bottom[s].astype(BF)


def fill_rows(u_ref, x, halo, n, buf_l, buf_r):
    top, body, bottom = padded_rows(x, halo, n, buf_l, buf_r)
    for s in range(3):
        lanes = slice(s * 128, s * 128 + 128)
        u_ref[0, 0:n, lanes] = top[s].astype(BF)
        u_ref[1 : n + 1, 0:n, lanes] = body[s].astype(BF)
        u_ref[n + 1, 0:n, lanes] = bottom[s].astype(BF)


def silu(s):
    return s / (1.0 + jnp.exp(-s))


def conv_pairs(y_ref, w_ref, q0, m, extra):
    n_p = y_ref.shape[1]
    a = y_ref[q0 : q0 + m].reshape(m * n_p, 768)
    b = y_ref[q0 + 1 : q0 + 1 + m].reshape(m * n_p, 768)
    acc = jnp.dot(a, w_ref[0:768, :], preferred_element_type=F32)
    acc = acc + jnp.dot(b, w_ref[768:1536, :], preferred_element_type=F32)
    acc = acc.reshape(m, n_p, 256)
    if extra is not None:
        acc = acc + extra
    return silu(acc)


def pair_chunks(n):
    half = n // 2
    m = 6 if half % 6 == 0 else half
    return [(q, m) for q in range(0, half, m)]


def emit_rims(y_ref, rims_ref, g, n, colbuf):
    def read(lo):
        return y_ref[g, :, :, lo : lo + 8, :].astype(F32).reshape(n, 8, 128)

    left, right = column_strips(read, n, colbuf)
    rims_ref[g, 0] = y_ref[g, 0, 0]
    rims_ref[g, 1] = right.astype(BF)
    rims_ref[g, 2] = y_ref[g, n // 2 - 1, 1]
    rims_ref[g, 3] = left.astype(BF)


def enc_kernel(x_ref, halo_ref, w_ref, y_ref, rims_ref, s_ref, pairs, buf_l, buf_r, colbuf, sumbuf):
    group, n = x_ref.shape[0], x_ref.shape[1]
    half = n // 2

    def one(g):
        halo = [halo_ref[g, e].astype(F32) for e in range(4)]
        fill_pairs(pairs, x_ref[g].astype(F32), halo, n, buf_l, buf_r)
        for q0, m in pair_chunks(n):
            out = conv_pairs(pairs, w_ref, q0, m, None).astype(BF)[:, 0:n]
            y_ref[g, q0 : q0 + m, 0] = out[:, :, 0:128]
            y_ref[g, q0 : q0 + m, 1] = out[:, :, 128:256]
            both = out[:, :, 0:128].astype(F32) + out[:, :, 128:256].astype(F32)
            sumbuf[...] = both.reshape(m * n, 128)
            small = sumbuf[pl.ds(0, m * half, 2), :] + sumbuf[pl.ds(1, m * half, 2), :]
            s_ref[g, q0 : q0 + m] = (small * 0.25).reshape(m, half, 128).astype(BF)
        emit_rims(y_ref, rims_ref, g, n, colbuf)

    for g in range(group):
        one(g)


def dec_kernel(
    x_ref, halo_ref, u_ref, uhalo_ref, w_ref, wu_ref, y_ref, rims_ref,
    pairs, rows, buf_l, buf_r, cbuf_l, cbuf_r, colbuf, acc_ref,
):
    group, n = x_ref.shape[0], x_ref.shape[1]
    half = n // 2
    hp = rows.shape[1]

    def one(g):
        halo = [halo_ref[g, e].astype(F32) for e in range(4)]
        uhalo = [uhalo_ref[g, e].astype(F32) for e in range(4)]
        fill_rows(rows, u_ref[g].astype(F32), uhalo, half, cbuf_l, cbuf_r)
        fill_pairs(pairs, x_ref[g].astype(F32), halo, n, buf_l, buf_r)
        for q0, m in pair_chunks(n):
            for b in range(2):
                acc = None
                for k in range(3):
                    lhs = rows[q0 + k : q0 + k + m, :, b * 128 : b * 128 + 256].reshape(m * hp, 256)
                    part = jnp.dot(lhs, wu_ref[b, k], preferred_element_type=F32)
                    acc = part if acc is None else acc + part
                acc = acc.reshape(m, hp, 256)
                for i in range(m):
                    for p in range(2):
                        acc_ref[p, i, pl.ds(b, half, 2), :] = acc[i, 0:half, p * 128 : p * 128 + 128]
            extra = jnp.concatenate([acc_ref[0], acc_ref[1]], axis=2)
            out = conv_pairs(pairs, w_ref, q0, m, extra).astype(BF)[:, 0:n]
            y_ref[g, q0 : q0 + m, 0] = out[:, :, 0:128]
            y_ref[g, q0 : q0 + m, 1] = out[:, :, 128:256]
        if rims_ref is not None:
            emit_rims(y_ref, rims_ref, g, n, colbuf)

    for g in range(group):
        one(g)


def group_of(tiles, want):
    return max(g for g in range(1, want + 1) if tiles % g == 0)


def pair_weights(w):
    zero = jnp.zeros((1,) + w.shape[1:], w.dtype)
    first = jnp.concatenate([w, zero], axis=0)
    second = jnp.concatenate([zero, w], axis=0)
    return jnp.concatenate([first.reshape(1536, 128), second.reshape(1536, 128)], axis=1)


def coarse_weights(w):
    w = w.astype(F32)
    zero = jnp.zeros_like(w[0])
    even = jnp.stack([w[0], w[1] + w[2], zero])
    odd = jnp.stack([zero, w[0] + w[1], w[2]])
    both = jnp.stack([even, odd], axis=3)
    left = jnp.stack([both[:, 0], both[:, 1] + both[:, 2]], axis=1)
    right = jnp.stack([both[:, 0] + both[:, 1], both[:, 2]], axis=1)
    return jnp.stack([left, right]).reshape(2, 3, 256, 256).astype(BF)


def tile_spec(group, *dims):
    return pl.BlockSpec((group,) + dims, lambda i: (i,) + (0,) * len(dims))


def whole_spec(shape):
    return pl.BlockSpec(shape, lambda i: (0,) * len(shape))


def enc_conv(x, halo, w, want):
    tiles, n, _, c = x.shape
    half, n_p = n // 2, up16(n)
    g = group_of(tiles, want)
    m = pair_chunks(n)[0][1]
    y, rims, s = pl.pallas_call(
        enc_kernel,
        grid=(tiles // g,),
        in_specs=[tile_spec(g, n, n, c), tile_spec(g, 4, n, c), whole_spec((1536, 256))],
        out_specs=[tile_spec(g, half, 2, n, c), tile_spec(g, 4, n, c), tile_spec(g, half, half, c)],
        out_shape=[
            jax.ShapeDtypeStruct((tiles, half, 2, n, c), BF),
            jax.ShapeDtypeStruct((tiles, 4, n, c), BF),
            jax.ShapeDtypeStruct((tiles, half, half, c), BF),
        ],
        scratch_shapes=[
            pltpu.VMEM((half + 1, n_p, 768), BF),
            pltpu.VMEM((n * 8, 128), F32),
            pltpu.VMEM((n * 8, 128), F32),
            pltpu.VMEM((n * 8, 128), F32),
            pltpu.VMEM((m * n, 128), F32),
        ],
        compiler_params=params(),
        cost_estimate=pl.CostEstimate(
            flops=tiles * n * n * 2 * 1536 * 128, bytes_accessed=tiles * n * n * 600, transcendentals=tiles * n * n * 128
        ),
        name="enc_conv",
    )(x, halo, pair_weights(w))
    return y.reshape(tiles, n, n, c), rims, s


def dec_conv(x, halo, u, uhalo, w, want, with_rims):
    tiles, n, _, c = x.shape
    half, n_p, h_p = n // 2, up16(n), up16(n // 2)
    g = group_of(tiles, want)
    m = pair_chunks(n)[0][1]
    kernel = dec_kernel if with_rims else (lambda *r: dec_kernel(*r[:7], None, *r[7:]))
    out = pl.pallas_call(
        kernel,
        grid=(tiles // g,),
        in_specs=[
            tile_spec(g, n, n, c), tile_spec(g, 4, n, c), tile_spec(g, half, half, c), tile_spec(g, 4, half, c),
            whole_spec((1536, 256)), whole_spec((2, 3, 256, 256)),
        ],
        out_specs=[tile_spec(g, half, 2, n, c)] + [tile_spec(g, 4, n, c)] * with_rims,
        out_shape=[jax.ShapeDtypeStruct((tiles, half, 2, n, c), BF)]
        + [jax.ShapeDtypeStruct((tiles, 4, n, c), BF)] * with_rims,
        scratch_shapes=[
            pltpu.VMEM((half + 1, n_p, 768), BF),
            pltpu.VMEM((half + 2, h_p, 384), BF),
            pltpu.VMEM((n * 8, 128), F32),
            pltpu.VMEM((n * 8, 128), F32),
            pltpu.VMEM((half * 8, 128), F32),
            pltpu.VMEM((half * 8, 128), F32),
            pltpu.VMEM((n * 8, 128), F32),
            pltpu.VMEM((2, m, n_p, 128), F32),
        ],
        compiler_params=params(),
        cost_estimate=pl.CostEstimate(
            flops=tiles * n * n * 2 * 2300 * 128, bytes_accessed=tiles * n * n * 600, transcendentals=tiles * n * n * 128
        ),
        name="dec_conv",
    )(x, halo, u, uhalo, pair_weights(w[:, :, c:]), coarse_weights(w[:, :, :c]))
    y = out[0].reshape(tiles, n, n, c)
    return (y, out[1]) if with_rims else y


def per_device(features, edge_table, w_enc0, w_enc1, w_enc2, w_mid, w_dec2, w_dec1, w_dec0):
    tiles = features.shape[0]
    devices = lax.axis_size("tile")
    position = lax.axis_index("tile")
    cap = pair_capacity(FACE_TILES, tiles)
    rows = devices * cap
    slot_row, pick_row, rev = routing_plan(edge_table, position, tiles, cap, devices)
    strip_count = tiles * 4
    buffer_rows = jnp.arange(rows, dtype=jnp.int32)
    send_map = (slot_row[None, :] == buffer_rows[:, None]).astype(BF)
    pick_columns = jnp.arange(rows + strip_count, dtype=jnp.int32)
    pick_map = (pick_row[:, None] == pick_columns[None, :]).astype(BF)

    def trade(strips):
        length = strips.shape[1]
        out = lax.all_to_all(
            strips.reshape(devices, cap * length, 128), "tile", split_axis=0, concat_axis=0, tiled=True
        )
        return out.reshape(rows, length, 128)

    def halo_big(rims):
        length = rims.shape[2]
        own = rims.reshape(strip_count, length, 128)
        recv = trade(pack_strips(slot_row, own, rows))
        return route_strips(pick_row, rev, recv, own).reshape(tiles, 4, length, 128)

    def halo_small(rims):
        length = rims.shape[2]
        flat = rims.reshape(strip_count, length * 128)
        outgoing = jnp.dot(send_map, flat, preferred_element_type=F32).astype(BF)
        incoming = trade(outgoing.reshape(rows, length, 128)).reshape(rows, length * 128)
        gathered = jnp.concatenate([incoming, flat], axis=0)
        halo = jnp.dot(pick_map, gathered, preferred_element_type=F32).astype(BF)
        halo = halo.reshape(strip_count, length, 128)
        halo = jnp.where(rev[:, None, None] == 1, halo[:, ::-1, :], halo)
        return halo.reshape(tiles, 4, length, 128)

    x0_rims = tile_rims(features)
    enc0, enc0_rims, x1 = enc_conv(features, halo_big(x0_rims), w_enc0, 1)
    x1_halo = halo_big(tile_rims(x1))
    enc0_halo = halo_big(enc0_rims)
    enc1, enc1_rims, x2 = enc_conv(x1, x1_halo, w_enc1, 4)
    x2_halo = halo_small(edge_rims(x2))
    enc1_halo = halo_big(enc1_rims)
    enc2 = conv_layer(assemble(x2, x2_halo), w_enc2)
    x3 = shrink(enc2)
    x3_halo = halo_small(edge_rims(x3))
    enc2_halo = halo_small(edge_rims(enc2))
    middle = conv_layer(assemble(x3, x3_halo), w_mid)
    mid_halo = halo_small(edge_rims(middle))
    upper = assemble(enlarge(middle), jnp.repeat(mid_halo, 2, axis=2))
    lower = assemble(enc2, enc2_halo)
    dec2 = conv_layer(jnp.concatenate([upper, lower], axis=3), w_dec2)
    dec2_halo = halo_small(edge_rims(dec2))
    dec1, dec1_rims = dec_conv(enc1, enc1_halo, dec2, dec2_halo, w_dec1, 4, True)
    dec1_halo = halo_big(dec1_rims)
    return dec_conv(enc0, enc0_halo, dec1, dec1_halo, w_dec0, 1, False)


def solution(mesh):
    return jax.shard_map(
        per_device,
        mesh=mesh,
        in_specs=(P(("grp", "tile"), None, None, None), P(), P(), P(), P(), P(), P(), P(), P()),
        out_specs=P(("grp", "tile"), None, None, None),
        check_vma=False,
    )
```

```python
import jax
import jax.numpy as jnp
import numpy as np
from jax import lax
from jax.experimental import pallas as pl
from jax.experimental.pallas import tpu as pltpu
from jax.sharding import PartitionSpec as P

FACE_TILES = 8
VMEM_LIMIT = 50 * 2**20
BF = jnp.bfloat16
F32 = jnp.float32


def cube_links(tiles_side):
    basis = np.eye(3, dtype=np.int64)
    frames = []
    for axis_id in range(3):
        for orient in (1, -1):
            frames.append(
                (orient * basis[axis_id], basis[(axis_id + 1) % 3], basis[(axis_id + 2) % 3])
            )
    per_face = tiles_side * tiles_side
    tile_total = 6 * per_face
    centres = np.zeros((tile_total, 3), np.int64)
    lookup = {}
    for face_id in range(6):
        normal, row_axis, col_axis = frames[face_id]
        for row_id in range(tiles_side):
            for col_id in range(tiles_side):
                slot_id = face_id * per_face + row_id * tiles_side + col_id
                centre = (
                    tiles_side * normal
                    + (2 * row_id + 1 - tiles_side) * row_axis
                    + (2 * col_id + 1 - tiles_side) * col_axis
                )
                centres[slot_id] = centre
                lookup[tuple((int(entry) for entry in centre))] = slot_id
    partner = np.zeros((tile_total, 4), np.int64)
    for slot_id in range(tile_total):
        normal, row_axis, col_axis = frames[slot_id // per_face]
        outward = (-row_axis, col_axis, row_axis, -col_axis)
        for edge_id in range(4):
            beyond = tuple((int(entry) for entry in centres[slot_id] + 2 * outward[edge_id]))
            if beyond in lookup:
                partner[slot_id, edge_id] = lookup[beyond]
            else:
                partner[slot_id, edge_id] = lookup[
                    tuple((int(entry) for entry in centres[slot_id] + outward[edge_id] - normal))
                ]
    return partner


def pair_capacity(tiles_side, tiles_here):
    partner = cube_links(tiles_side)
    tile_total = partner.shape[0]
    blocks = tile_total // tiles_here
    source = np.repeat(np.arange(tile_total) // tiles_here, 4)
    target = partner.reshape(-1) // tiles_here
    identity = np.eye(blocks, dtype=np.int64)
    shared = identity[source].T @ identity[target]
    shared = shared * (1 - identity)
    return max(int(shared.max()), 1)


def routing_plan(edge_table, position, tiles_here, slot_count, devices):
    strip_count = tiles_here * 4
    own_rows = lax.dynamic_slice_in_dim(edge_table, position * tiles_here, tiles_here, 0).reshape(
        strip_count, 2
    )
    partner = own_rows[:, 0]
    matching = own_rows[:, 1] // 2
    reversed_rows = own_rows[:, 1] % 2
    target = partner // tiles_here
    order = jnp.arange(strip_count, dtype=jnp.int32)
    earlier = (order[None, :] < order[:, None]) & (target[None, :] == target[:, None])
    slot_rank = jnp.sum(earlier.astype(jnp.int32), axis=1)
    remote = target != position
    slot_row = jnp.where(remote, target * slot_count + slot_rank, -1)
    source_tiles = target[:, None] * tiles_here + jnp.arange(tiles_here, dtype=jnp.int32)[None, :]
    their_partners = jnp.take(edge_table[:, :, 0], source_tiles, axis=0).reshape(
        strip_count, strip_count
    )
    toward_me = their_partners // tiles_here == position
    wanted = partner % tiles_here * 4 + matching
    before_wanted = order[None, :] < wanted[:, None]
    recv_rank = jnp.sum((toward_me & before_wanted).astype(jnp.int32), axis=1)
    pick_row = jnp.where(remote, target * slot_count + recv_rank, devices * slot_count + wanted)
    return (pick_row, reversed_rows, slot_row, matching)


def up16(n):
    return (n + 15) // 16 * 16


def strip_rows(n):
    return {6: 8, 12: 16}.get(n, n)


def params():
    return pltpu.CompilerParams(vmem_limit_bytes=VMEM_LIMIT)


def rims_kernel(lo_ref, hi_ref, top_ref, bottom_ref, out_ref, colbuf):
    group, n = lo_ref.shape[0], lo_ref.shape[1]
    for g in range(group):
        colbuf[...] = lo_ref[g, :, 0:8, :].astype(F32).reshape(n * 8, 128)
        left = colbuf[pl.ds(0, n, 8), :]
        colbuf[...] = hi_ref[g, :, 8:16, :].astype(F32).reshape(n * 8, 128)
        right = colbuf[pl.ds(7, n, 8), :]
        out_ref[g, 0] = top_ref[g, 0]
        out_ref[g, 1] = right.astype(BF)
        out_ref[g, 2] = bottom_ref[g, 0]
        out_ref[g, 3] = left.astype(BF)


def tile_rims(x):
    tiles, n, _, c = x.shape
    g = group_of(tiles, 4)
    last = n // 16 - 1
    return pl.pallas_call(
        rims_kernel,
        grid=(tiles // g,),
        in_specs=[
            pl.BlockSpec((g, n, 16, c), lambda i: (i, 0, 0, 0)),
            pl.BlockSpec((g, n, 16, c), lambda i: (i, 0, last, 0)),
            pl.BlockSpec((g, 1, n, c), lambda i: (i, 0, 0, 0)),
            pl.BlockSpec((g, 1, n, c), lambda i: (i, n - 1, 0, 0)),
        ],
        out_specs=pl.BlockSpec((g, 4, n, c), lambda i: (i, 0, 0, 0)),
        out_shape=jax.ShapeDtypeStruct((tiles, 4, n, c), BF),
        scratch_shapes=[pltpu.VMEM((n * 8, 128), F32)],
        compiler_params=params(),
        name="tile_rims",
    )(x, x, x, x)


def pack_kernel(slot_ref, rims_ref, send_ref):
    def step(i, carry):
        slot = slot_ref[i]

        @pl.when(slot >= 0)
        def _():
            send_ref[slot] = rims_ref[i]

        return carry

    lax.fori_loop(0, rims_ref.shape[0], step, 0)


def pack_strips(slot_row, rims, rows):
    strips, length, c = rims.shape
    return pl.pallas_call(
        pack_kernel,
        in_specs=[
            pl.BlockSpec(memory_space=pltpu.SMEM),
            pl.BlockSpec(memory_space=pltpu.VMEM),
        ],
        out_specs=pl.BlockSpec(memory_space=pltpu.VMEM),
        out_shape=jax.ShapeDtypeStruct((rows, length, c), BF),
        compiler_params=params(),
        name="pack_strips",
    )(slot_row, rims)


def silu(s):
    return s / (1.0 + jnp.exp(-s))


def strip_shifts(h, n):
    rows = h.shape[0]
    row = lax.broadcasted_iota(jnp.int32, h.shape, 0)
    half = h * 0.5
    down = jnp.where(row == 0, half, pltpu.roll(h, 1, 0))
    up = jnp.where(row == n - 1, half, pltpu.roll(h, rows - 1, 0))
    return down, up


def flip_matrix(rows, n):
    ri = lax.broadcasted_iota(jnp.int32, (rows, rows), 0)
    ci = lax.broadcasted_iota(jnp.int32, (rows, rows), 1)
    return (ri + ci == n - 1).astype(F32).astype(BF)


def put_shifts(ref, index, lane, h, n):
    down, up = strip_shifts(h, n)
    for s, part in enumerate((down, h, up)):
        ref[index + (slice(None), slice(lane + s * 128, lane + s * 128 + 128))] = part.astype(ref.dtype)


def rim_kernel(n, shrunk, strips_in, nxt, refs):
    it = iter(refs)
    pick_ref, rev_ref, slot_ref, edge_ref = next(it), next(it), next(it), next(it)
    recv_ref, own_ref, sum_ref = next(it), next(it), next(it)
    w_ref = next(it) if strips_in else None
    ring_ref = next(it) if nxt == "shrink" else None
    skip_ref, wn_ref = (next(it), next(it)) if nxt == "halo" else (None, None)
    rim_ref = next(it)
    next_ref, send_ref = (next(it), next(it)) if nxt != "none" else (None, None)
    lhs_ref, con_ref = (next(it), next(it))
    edge_buf, ring_buf, sum_buf, out_buf = next(it), next(it), next(it), next(it)
    lhsn_ref, conn_ref, big_buf = (next(it), next(it), next(it)) if nxt == "halo" else (None, None, None)

    rows, lp = recv_ref.shape[0], recv_ref.shape[1]
    tiles = own_ref.shape[0] // 4

    def incoming(i):
        pick = pick_ref[i]
        a = recv_ref[jnp.minimum(pick, rows - 1)]
        b = own_ref[jnp.maximum(pick - rows, 0)]
        return jnp.where(pick < rows, a.astype(F32), b.astype(F32))

    if strips_in:
        flip = flip_matrix(lp, n)

        def gather(t, carry):
            for e in range(4):
                i = t * 4 + e
                edge_buf[e] = incoming(i)

                @pl.when(rev_ref[i] == 1)
                def _():
                    edge_buf[e] = jnp.dot(flip, edge_buf[e].astype(BF), preferred_element_type=F32)

                put_shifts(lhs_ref, (e, t), 0, edge_buf[e], n)
            return carry

        lax.fori_loop(0, tiles, gather, 0)
        for e in range(4):
            lhs = lhs_ref[e].reshape(tiles * lp, 384).astype(BF)
            con_ref[e] = jnp.dot(lhs, w_ref[e], preferred_element_type=F32).reshape(tiles, lp, 128)
    else:

        def gather(t, carry):
            for e in range(4):
                con_ref[e, t] = incoming(t * 4 + e)
            return carry

        lax.fori_loop(0, tiles, gather, 0)

    end = n - 1
    corners = (
        (0, 0, 3, 0), (0, end, 1, 0), (2, 0, 3, end), (2, end, 1, end),
        (3, 0, 0, 0), (3, end, 2, 0), (1, 0, 0, end), (1, end, 2, end),
    )
    joints = (
        (0, 0, 3, 1), (0, end, 1, 1), (2, 0, 3, end - 1), (2, end, 1, end - 1),
        (3, 0, 0, 1), (3, end, 2, 1), (1, 0, 0, end - 1), (1, end, 2, end - 1),
    )
    if nxt == "shrink":
        out_buf[...] = jnp.zeros_like(out_buf)

    def finish(t, carry):
        for e in range(4):
            edge_buf[e] = sum_ref[t * 4 + e] + con_ref[e, t]
        for e, cell, other, at in corners:
            edge_buf[e, cell : cell + 1] = edge_buf[e, cell : cell + 1] + con_ref[other, t, at : at + 1]
        for e in range(4):
            y = silu(edge_buf[e]).astype(BF)
            rim_ref[t * 4 + e] = y
            edge_buf[e] = y.astype(F32)
        if nxt == "shrink":
            for e in range(4):
                ring_buf[e] = ring_ref[t * 4 + e].astype(F32)
            for e, cell, other, at in joints:
                ring_buf[e, cell : cell + 1] = edge_buf[other, at : at + 1]
            for e in range(4):
                i = t * 4 + e
                sum_buf[...] = edge_buf[e] + ring_buf[e]
                small = sum_buf[pl.ds(0, lp // 2, 2), :] + sum_buf[pl.ds(1, lp // 2, 2), :]
                out_buf[0 : lp // 2] = small * 0.25
                out = out_buf[...].astype(BF)
                next_ref[i] = out
                slot = slot_ref[i]

                @pl.when(slot >= 0)
                def _():
                    send_ref[slot] = out

        if nxt == "halo":
            k = big_buf.shape[0] // 2
            for e in range(4):
                put_shifts(lhsn_ref, (e, t), 0, skip_ref[t * 4 + e].astype(F32), 2 * n)
                big_buf[pl.ds(0, k, 2), :] = edge_buf[e, 0:k]
                big_buf[pl.ds(1, k, 2), :] = edge_buf[e, 0:k]
                put_shifts(lhsn_ref, (e, t), 384, big_buf[...], 2 * n)
        return carry

    lax.fori_loop(0, tiles, finish, 0)

    if nxt == "halo":
        lf = big_buf.shape[0]
        for f in range(4):
            lhs = lhsn_ref[f].reshape(tiles * lf, 768).astype(BF)
            out = jnp.dot(lhs, wn_ref[(f + 2) % 4], preferred_element_type=F32)
            conn_ref[f] = out.reshape(tiles, lf, 128)
        flip_n = flip_matrix(lf, 2 * n)

        def emit(t, carry):
            for f in range(4):
                i = t * 4 + f
                edge = edge_ref[i]

                @pl.when((edge != (f + 2) % 4) | (rev_ref[i] == 1))
                def _():
                    for lane in (0, 384):
                        big_buf[...] = lhsn_ref[f, t, :, lane + 128 : lane + 256].astype(F32)

                        @pl.when(rev_ref[i] == 1)
                        def _():
                            big_buf[...] = jnp.dot(flip_n, big_buf[...].astype(BF), preferred_element_type=F32)

                        put_shifts(lhsn_ref, (f, t), lane, big_buf[...], 2 * n)
                    conn_ref[f, t] = jnp.dot(
                        lhsn_ref[f, t].astype(BF), wn_ref[edge], preferred_element_type=F32
                    )

                out = conn_ref[f, t].astype(BF)
                next_ref[i] = out
                slot = slot_ref[i]

                @pl.when(slot >= 0)
                def _():
                    send_ref[slot] = out

            return carry

        lax.fori_loop(0, tiles, emit, 0)


def rim_step(n, plan, recv, own, sums, w=None, ring=None, skip=None, wn=None):
    pick, rev, slot, edge = plan
    rows, lp, c = recv.shape
    strips = own.shape[0]
    tiles = strips // 4
    nxt = "shrink" if ring is not None else ("halo" if skip is not None else "none")
    smem = pl.BlockSpec(memory_space=pltpu.SMEM)
    vmem = pl.BlockSpec(memory_space=pltpu.VMEM)
    args = [recv, own, sums] + [a for a in (w, ring, skip, wn) if a is not None]
    outs = [jax.ShapeDtypeStruct((strips, lp, c), BF)]
    lo = strip_rows(n // 2) if nxt == "shrink" else strip_rows(2 * n)
    if nxt != "none":
        outs += [jax.ShapeDtypeStruct((strips, lo, c), BF), jax.ShapeDtypeStruct((rows, lo, c), BF)]
    wide = lambda r: BF if r % 16 == 0 else F32
    scratch = [
        pltpu.VMEM((4, tiles, lp, 384), wide(lp)),
        pltpu.VMEM((4, tiles, lp, 128), F32),
        pltpu.VMEM((4, lp, 128), F32),
        pltpu.VMEM((4, lp, 128), F32),
        pltpu.VMEM((lp, 128), F32),
        pltpu.VMEM((lo, 128), F32),
    ]
    if nxt == "halo":
        scratch += [
            pltpu.VMEM((4, tiles, lo, 768), wide(lo)),
            pltpu.VMEM((4, tiles, lo, 128), F32),
            pltpu.VMEM((lo, 128), F32),
        ]

    def kernel(*refs):
        rim_kernel(n, nxt == "shrink", w is not None, nxt, refs)

    return pl.pallas_call(
        kernel,
        in_specs=[smem] * 4 + [vmem] * len(args),
        out_specs=[vmem] * len(outs),
        out_shape=outs,
        scratch_shapes=scratch,
        compiler_params=params(),
        name="rim_step",
    )(pick, rev, slot, edge, *args)


def spread_columns(strip, n, sublane, buf):
    buf[pl.ds(sublane, n, 8), :] = strip
    return buf[...].reshape(n, 8, 128)


def with_rims(x, rim, n, buf):
    sub = lax.broadcasted_iota(jnp.int32, (n, 8, 128), 1)
    head = jnp.where(sub == 0, spread_columns(rim[3], n, 0, buf), x[:, 0:8])
    tail = jnp.where(sub == 7, spread_columns(rim[1], n, 7, buf), x[:, n - 8 : n])
    x = jnp.concatenate([head, x[:, 8 : n - 8], tail], axis=1)
    return jnp.concatenate([rim[0][None], x[1 : n - 1], rim[2][None]], axis=0)


def column_shifts(x, n):
    col = lax.broadcasted_iota(jnp.int32, x.shape, 1)
    down = jnp.where(col == 0, 0.0, pltpu.roll(x, 1, 1))
    up = jnp.where(col == n - 1, 0.0, pltpu.roll(x, n - 1, 1))
    return down, x, up


def fill_pairs(y_ref, x, n):
    half, n_p = n // 2, y_ref.shape[1]
    zero = jnp.zeros((n_p, 384), BF)
    y_ref[0, :, 0:384] = zero
    y_ref[half, :, 384:768] = zero
    for s, body in enumerate(column_shifts(x, n)):
        b = body.astype(BF).reshape(half, 2, n, 128)
        y_ref[0:half, 0:n, 384 + s * 128 : 384 + s * 128 + 128] = b[:, 0]
        y_ref[1 : half + 1, 0:n, s * 128 : s * 128 + 128] = b[:, 1]


def fill_rows(u_ref, x, n):
    zero = jnp.zeros((u_ref.shape[1], 384), BF)
    u_ref[0] = zero
    u_ref[n + 1] = zero
    for s, body in enumerate(column_shifts(x, n)):
        u_ref[1 : n + 1, 0:n, s * 128 : s * 128 + 128] = body.astype(BF)


def pair_sums(y_ref, w_ref, q0, m, extra):
    n_p = y_ref.shape[1]
    a = y_ref[q0 : q0 + m].reshape(m * n_p, 768)
    b = y_ref[q0 + 1 : q0 + 1 + m].reshape(m * n_p, 768)
    acc = jnp.dot(a, w_ref[0:768, :], preferred_element_type=F32)
    acc = acc + jnp.dot(b, w_ref[768:1536, :], preferred_element_type=F32)
    acc = acc.reshape(m, n_p, 256)
    return acc if extra is None else acc + extra


def pair_chunks(n):
    half = n // 2
    m = 6 if half % 6 == 0 else half
    return [(q, m) for q in range(0, half, m)]


def column_of(acc, m, lo, sublane, colbuf):
    rows = jnp.stack([acc[:, lo : lo + 8, 0:128], acc[:, lo : lo + 8, 128:256]], axis=1)
    colbuf[0 : 16 * m] = rows.reshape(16 * m, 128)
    return colbuf[pl.ds(sublane, 2 * m, 8), :]


def put_sums(acc, sums_ref, g, q0, m, n, colbuf):
    cells = slice(2 * q0, 2 * q0 + 2 * m)
    if q0 == 0:
        sums_ref[g, 0] = acc[0, 0:n, 0:128]
    if q0 + m == n // 2:
        sums_ref[g, 2] = acc[m - 1, 0:n, 128:256]
    sums_ref[g, 3, cells] = column_of(acc, m, 0, 0, colbuf)
    sums_ref[g, 1, cells] = column_of(acc, m, n - 8, 7, colbuf)


def enc_kernel(*refs):
    it = iter(refs[:-4])
    x_ref, w_ref = next(it), next(it)
    rest = list(it)
    rim_ref = rest.pop(0) if len(rest) == 5 else None
    y_ref, sums_ref, ring_ref, s_ref = rest
    pairs, colbuf, sumbuf, ringbuf = refs[-4:]
    group, n = x_ref.shape[0], x_ref.shape[1]
    half = n // 2

    for g in range(group):
        x = x_ref[g].astype(F32)
        if rim_ref is not None:
            x = with_rims(x, [rim_ref[g, e].astype(F32) for e in range(4)], n, colbuf)
        fill_pairs(pairs, x, n)
        for q0, m in pair_chunks(n):
            acc = pair_sums(pairs, w_ref, q0, m, None)
            put_sums(acc, sums_ref, g, q0, m, n, colbuf)
            out = silu(acc).astype(BF)[:, 0:n]
            y_ref[g, q0 : q0 + m, 0] = out[:, :, 0:128]
            y_ref[g, q0 : q0 + m, 1] = out[:, :, 128:256]
            wide = out.astype(F32)
            if q0 == 0:
                ring_ref[g, 0] = out[0, :, 128:256]
            if q0 + m == half:
                ring_ref[g, 2] = out[m - 1, :, 0:128]
            ringbuf[1, 2 * q0 : 2 * q0 + 2 * m] = column_of(wide, m, n - 8, 6, colbuf)
            ringbuf[0, 2 * q0 : 2 * q0 + 2 * m] = column_of(wide, m, 0, 1, colbuf)
            both = wide[:, :, 0:128] + wide[:, :, 128:256]
            sumbuf[...] = both.reshape(m * n, 128)
            small = sumbuf[pl.ds(0, m * half, 2), :] + sumbuf[pl.ds(1, m * half, 2), :]
            s_ref[g, q0 : q0 + m] = (small * 0.25).reshape(m, half, 128).astype(BF)
        ring_ref[g, 1] = ringbuf[1].astype(BF)
        ring_ref[g, 3] = ringbuf[0].astype(BF)


def dec_kernel(x_ref, rim_ref, u_ref, *refs):
    refs = list(refs)
    urim_ref = refs.pop(0) if len(refs) == 9 else None
    w_ref, wu_ref, y_ref, sums_ref, pairs, rows, colbuf, acc_ref = refs
    group, n = x_ref.shape[0], x_ref.shape[1]
    half = n // 2
    hp = rows.shape[1]

    for g in range(group):
        u = u_ref[g].astype(F32)
        if urim_ref is not None:
            u = with_rims(u, [urim_ref[g, e].astype(F32) for e in range(4)], half, colbuf.at[0 : half * 8])
        fill_rows(rows, u, half)
        x = with_rims(x_ref[g].astype(F32), [rim_ref[g, e].astype(F32) for e in range(4)], n, colbuf)
        fill_pairs(pairs, x, n)
        for q0, m in pair_chunks(n):
            for b in range(2):
                acc = None
                for k in range(3):
                    lhs = rows[q0 + k : q0 + k + m, :, b * 128 : b * 128 + 256].reshape(m * hp, 256)
                    part = jnp.dot(lhs, wu_ref[b, k], preferred_element_type=F32)
                    acc = part if acc is None else acc + part
                acc = acc.reshape(m, hp, 256)
                for i in range(m):
                    for p in range(2):
                        acc_ref[p, i, pl.ds(b, half, 2), :] = acc[i, 0:half, p * 128 : p * 128 + 128]
            extra = jnp.concatenate([acc_ref[0], acc_ref[1]], axis=2)
            acc = pair_sums(pairs, w_ref, q0, m, extra)
            put_sums(acc, sums_ref, g, q0, m, n, colbuf)
            out = silu(acc).astype(BF)[:, 0:n]
            y_ref[g, q0 : q0 + m, 0] = out[:, :, 0:128]
            y_ref[g, q0 : q0 + m, 1] = out[:, :, 128:256]


def patch_kernel(x_ref, rim_ref, y_ref, colbuf):
    n = x_ref.shape[1]
    for g in range(x_ref.shape[0]):
        rim = [rim_ref[g, e].astype(F32) for e in range(4)]
        x = with_rims(x_ref[g].astype(F32), rim, n, colbuf)
        y_ref[g] = x.astype(BF)


def patch(x, rim, want):
    tiles, n, _, c = x.shape
    g = group_of(tiles, want)
    return pl.pallas_call(
        patch_kernel,
        grid=(tiles // g,),
        in_specs=[tile_spec(g, n, n, c), tile_spec(g, 4, n, c)],
        out_specs=tile_spec(g, n, n, c),
        out_shape=jax.ShapeDtypeStruct(x.shape, BF),
        scratch_shapes=[pltpu.VMEM((n * 8, 128), F32)],
        input_output_aliases={0: 0},
        compiler_params=params(),
        name="patch",
    )(x, rim.reshape(tiles, 4, n, c))


def group_of(tiles, want):
    return max(g for g in range(1, want + 1) if tiles % g == 0)


def pair_weights(w):
    zero = jnp.zeros((1,) + w.shape[1:], w.dtype)
    first = jnp.concatenate([w, zero], axis=0)
    second = jnp.concatenate([zero, w], axis=0)
    return jnp.concatenate([first.reshape(1536, 128), second.reshape(1536, 128)], axis=1)


def strip_weights(w):
    taps = jnp.stack([w[0], w[:, 2], w[2], w[:, 0]])
    return taps.reshape(4, -1, 128)


def decoder_strip_weights(w):
    c = w.shape[2] // 2
    return jnp.concatenate([strip_weights(w[:, :, c:]), strip_weights(w[:, :, :c])], axis=1)


def coarse_weights(w):
    w = w.astype(F32)
    zero = jnp.zeros_like(w[0])
    even = jnp.stack([w[0], w[1] + w[2], zero])
    odd = jnp.stack([zero, w[0] + w[1], w[2]])
    both = jnp.stack([even, odd], axis=3)
    left = jnp.stack([both[:, 0], both[:, 1] + both[:, 2]], axis=1)
    right = jnp.stack([both[:, 0] + both[:, 1], both[:, 2]], axis=1)
    return jnp.stack([left, right]).reshape(2, 3, 256, 256).astype(BF)


def tile_spec(group, *dims):
    return pl.BlockSpec((group,) + dims, lambda i: (i,) + (0,) * len(dims))


def whole_spec(shape):
    return pl.BlockSpec(shape, lambda i: (0,) * len(shape))


def enc_conv(x, rim, w, want):
    tiles, n, _, c = x.shape
    half, n_p = n // 2, up16(n)
    g = group_of(tiles, want)
    m = pair_chunks(n)[0][1]
    args, specs = [x, pair_weights(w)], [tile_spec(g, n, n, c), whole_spec((1536, 256))]
    if rim is not None:
        args.append(rim.reshape(tiles, 4, n, c))
        specs.append(tile_spec(g, 4, n, c))
    y, sums, ring, s = pl.pallas_call(
        enc_kernel,
        grid=(tiles // g,),
        in_specs=specs,
        out_specs=[
            tile_spec(g, half, 2, n, c), tile_spec(g, 4, n, c), tile_spec(g, 4, n, c), tile_spec(g, half, half, c)
        ],
        out_shape=[
            jax.ShapeDtypeStruct((tiles, half, 2, n, c), BF),
            jax.ShapeDtypeStruct((tiles, 4, n, c), F32),
            jax.ShapeDtypeStruct((tiles, 4, n, c), BF),
            jax.ShapeDtypeStruct((tiles, half, half, c), BF),
        ],
        scratch_shapes=[
            pltpu.VMEM((half + 1, n_p, 768), BF),
            pltpu.VMEM((n * 8, 128), F32),
            pltpu.VMEM((m * n, 128), F32),
            pltpu.VMEM((2, n, 128), F32),
        ],
        compiler_params=params(),
        cost_estimate=pl.CostEstimate(
            flops=tiles * n * n * 2 * 1536 * 128, bytes_accessed=tiles * n * n * 600, transcendentals=tiles * n * n * 128
        ),
        name="enc_conv",
    )(*args)
    strips = lambda a: a.reshape(tiles * 4, n, c)
    return y.reshape(tiles, n, n, c), strips(sums), strips(ring), s


def dec_conv(x, rim, u, urim, w, want):
    tiles, n, _, c = x.shape
    half, n_p, h_p = n // 2, up16(n), up16(n // 2)
    g = group_of(tiles, want)
    m = pair_chunks(n)[0][1]
    args = [x, rim.reshape(tiles, 4, n, c), u]
    specs = [tile_spec(g, n, n, c), tile_spec(g, 4, n, c), tile_spec(g, half, half, c)]
    if urim is not None:
        args.append(urim.reshape(tiles, 4, half, c))
        specs.append(tile_spec(g, 4, half, c))
    y, sums = pl.pallas_call(
        dec_kernel,
        grid=(tiles // g,),
        in_specs=specs + [whole_spec((1536, 256)), whole_spec((2, 3, 256, 256))],
        out_specs=[tile_spec(g, half, 2, n, c), tile_spec(g, 4, n, c)],
        out_shape=[
            jax.ShapeDtypeStruct((tiles, half, 2, n, c), BF),
            jax.ShapeDtypeStruct((tiles, 4, n, c), F32),
        ],
        scratch_shapes=[
            pltpu.VMEM((half + 1, n_p, 768), BF),
            pltpu.VMEM((half + 2, h_p, 384), BF),
            pltpu.VMEM((n * 8, 128), F32),
            pltpu.VMEM((2, m, n_p, 128), F32),
        ],
        compiler_params=params(),
        cost_estimate=pl.CostEstimate(
            flops=tiles * n * n * 2 * 2300 * 128, bytes_accessed=tiles * n * n * 600, transcendentals=tiles * n * n * 128
        ),
        name="dec_conv",
    )(*args, pair_weights(w[:, :, c:]), coarse_weights(w[:, :, :c]))
    return y.reshape(tiles, n, n, c), sums.reshape(tiles * 4, n, c)


def strips_of(field, ring=0):
    n = field.shape[1]
    far = n - 1 - ring
    out = jnp.stack([field[:, ring], field[:, :, far], field[:, far], field[:, :, ring]], axis=1)
    out = jnp.pad(out, ((0, 0), (0, 0), (0, strip_rows(n) - n), (0, 0)))
    return out.reshape(field.shape[0] * 4, strip_rows(n), field.shape[3])


def patched(field, rim):
    tiles, n, _, c = field.shape
    rim = rim.reshape(tiles, 4, -1, c)[:, :, :n]
    middle = jnp.concatenate(
        [rim[:, 3, 1 : n - 1, None], field[:, 1 : n - 1, 1 : n - 1], rim[:, 1, 1 : n - 1, None]], axis=2
    )
    return jnp.concatenate([rim[:, 0][:, None], middle, rim[:, 2][:, None]], axis=1)


def inner_sums(field, weight):
    return lax.conv_general_dilated(
        field,
        weight,
        (1, 1),
        ((1, 1), (1, 1)),
        dimension_numbers=("NHWC", "HWIO", "NHWC"),
        preferred_element_type=F32,
    )


def shrink(field):
    count, length, _, channels = field.shape
    blocks = field.astype(F32).reshape(count, length // 2, 2, length // 2, 2, channels)
    return (jnp.sum(blocks, axis=(2, 4)) * 0.25).astype(BF)


def enlarge(field):
    return jnp.repeat(jnp.repeat(field, 2, axis=1), 2, axis=2)


def per_device(features, edge_table, w_enc0, w_enc1, w_enc2, w_mid, w_dec2, w_dec1, w_dec0):
    tiles, n0 = features.shape[0], features.shape[1]
    devices = lax.axis_size("tile")
    position = lax.axis_index("tile")
    cap = pair_capacity(FACE_TILES, tiles)
    rows = devices * cap
    plan = routing_plan(edge_table, position, tiles, cap, devices)
    slot_row = plan[2]

    def trade(strips):
        length = strips.shape[1]
        out = lax.all_to_all(
            strips.reshape(devices, cap * length, 128), "tile", split_axis=0, concat_axis=0, tiled=True
        )
        return out.reshape(rows, length, 128)

    rim0 = tile_rims(features).reshape(tiles * 4, n0, 128)
    recv = trade(pack_strips(slot_row, rim0, rows))
    enc0, sums, ring, x1 = enc_conv(features, None, w_enc0, 1)
    enc0_rim, x1_rim, send = rim_step(n0, plan, recv, rim0, sums, w=strip_weights(w_enc0), ring=ring)

    recv = trade(send)
    enc1, sums, ring, x2 = enc_conv(x1, x1_rim, w_enc1, 4)
    enc1_rim, x2_rim, send = rim_step(n0 // 2, plan, recv, x1_rim, sums, w=strip_weights(w_enc1), ring=ring)

    recv = trade(send)
    sums = inner_sums(patched(x2, x2_rim), w_enc2)
    enc2 = jax.nn.silu(sums).astype(BF)
    enc2_rim, x3_rim, send = rim_step(
        n0 // 4, plan, recv, x2_rim, strips_of(sums), w=strip_weights(w_enc2), ring=strips_of(enc2, 1)
    )

    recv = trade(send)
    sums = inner_sums(patched(shrink(enc2), x3_rim), w_mid)
    middle = jax.nn.silu(sums).astype(BF)
    mid_rim, own, send = rim_step(
        n0 // 8, plan, recv, x3_rim, strips_of(sums), w=strip_weights(w_mid),
        skip=enc2_rim, wn=decoder_strip_weights(w_dec2),
    )

    recv = trade(send)
    joined = jnp.concatenate([enlarge(patched(middle, mid_rim)), patched(enc2, enc2_rim)], axis=3)
    sums = inner_sums(joined, w_dec2)
    dec2 = jax.nn.silu(sums).astype(BF)
    dec2_rim, own, send = rim_step(
        n0 // 4, plan, recv, own, strips_of(sums), skip=enc1_rim, wn=decoder_strip_weights(w_dec1)
    )

    recv = trade(send)
    dec1, sums = dec_conv(enc1, enc1_rim, patched(dec2, dec2_rim), None, w_dec1, 4)
    dec1_rim, own, send = rim_step(
        n0 // 2, plan, recv, own, sums, skip=enc0_rim, wn=decoder_strip_weights(w_dec0)
    )

    recv = trade(send)
    dec0, sums = dec_conv(enc0, enc0_rim, dec1, dec1_rim, w_dec0, 1)
    (dec0_rim,) = rim_step(n0, plan, recv, own, sums)
    return patch(dec0, dec0_rim, 2)


def solution(mesh):
    return jax.shard_map(
        per_device,
        mesh=mesh,
        in_specs=(P(("grp", "tile"), None, None, None), P(), P(), P(), P(), P(), P(), P(), P()),
        out_specs=P(("grp", "tile"), None, None, None),
        check_vma=False,
    )
```

```python
import jax
import jax.numpy as jnp
import numpy as np
from jax import lax
from jax.experimental import pallas as pl
from jax.experimental.pallas import tpu as pltpu
from jax.sharding import PartitionSpec as P

FACE_TILES = 8
VMEM_LIMIT = 50 * 2**20
BF = jnp.bfloat16
F32 = jnp.float32


def cube_links(tiles_side):
    basis = np.eye(3, dtype=np.int64)
    frames = []
    for axis_id in range(3):
        for orient in (1, -1):
            frames.append(
                (orient * basis[axis_id], basis[(axis_id + 1) % 3], basis[(axis_id + 2) % 3])
            )
    per_face = tiles_side * tiles_side
    tile_total = 6 * per_face
    centres = np.zeros((tile_total, 3), np.int64)
    lookup = {}
    for face_id in range(6):
        normal, row_axis, col_axis = frames[face_id]
        for row_id in range(tiles_side):
            for col_id in range(tiles_side):
                slot_id = face_id * per_face + row_id * tiles_side + col_id
                centre = (
                    tiles_side * normal
                    + (2 * row_id + 1 - tiles_side) * row_axis
                    + (2 * col_id + 1 - tiles_side) * col_axis
                )
                centres[slot_id] = centre
                lookup[tuple((int(entry) for entry in centre))] = slot_id
    partner = np.zeros((tile_total, 4), np.int64)
    for slot_id in range(tile_total):
        normal, row_axis, col_axis = frames[slot_id // per_face]
        outward = (-row_axis, col_axis, row_axis, -col_axis)
        for edge_id in range(4):
            beyond = tuple((int(entry) for entry in centres[slot_id] + 2 * outward[edge_id]))
            if beyond in lookup:
                partner[slot_id, edge_id] = lookup[beyond]
            else:
                partner[slot_id, edge_id] = lookup[
                    tuple((int(entry) for entry in centres[slot_id] + outward[edge_id] - normal))
                ]
    return partner


def pair_capacity(tiles_side, tiles_here):
    partner = cube_links(tiles_side)
    tile_total = partner.shape[0]
    blocks = tile_total // tiles_here
    source = np.repeat(np.arange(tile_total) // tiles_here, 4)
    target = partner.reshape(-1) // tiles_here
    identity = np.eye(blocks, dtype=np.int64)
    shared = identity[source].T @ identity[target]
    shared = shared * (1 - identity)
    return max(int(shared.max()), 1)


def own_strips(edge_table, position, tiles_here):
    rows = lax.dynamic_slice_in_dim(edge_table, position * tiles_here, tiles_here, 0)
    rows = rows.reshape(tiles_here * 4, 2)
    return rows[:, 0], rows[:, 1] // 2, rows[:, 1] % 2


def send_slots(edge_table, position, tiles_here, slot_count):
    partner, _, _ = own_strips(edge_table, position, tiles_here)
    target = partner // tiles_here
    order = jnp.arange(tiles_here * 4, dtype=jnp.int32)
    earlier = (order[None, :] < order[:, None]) & (target[None, :] == target[:, None])
    slot_rank = jnp.sum(earlier.astype(jnp.int32), axis=1)
    return jnp.where(target != position, target * slot_count + slot_rank, -1)


def listed(mask):
    order = jnp.arange(mask.shape[0], dtype=jnp.int32)
    rank = jnp.sum((mask[None, :] & (order[None, :] < order[:, None])).astype(jnp.int32), axis=1)
    hit = mask[None, :] & (rank[None, :] == order[:, None])
    found = jnp.sum(jnp.where(hit, order[None, :], 0), axis=1)
    return jnp.concatenate([found, jnp.sum(mask.astype(jnp.int32), keepdims=True)])


def receive_plan(edge_table, slot_row, position, tiles_here, slot_count, devices):
    strip_count = tiles_here * 4
    partner, matching, reversed_rows = own_strips(edge_table, position, tiles_here)
    target = partner // tiles_here
    order = jnp.arange(strip_count, dtype=jnp.int32)
    remote = target != position
    source_tiles = target[:, None] * tiles_here + jnp.arange(tiles_here, dtype=jnp.int32)[None, :]
    their_partners = jnp.take(edge_table[:, :, 0], source_tiles, axis=0).reshape(
        strip_count, strip_count
    )
    toward_me = their_partners // tiles_here == position
    wanted = partner % tiles_here * 4 + matching
    before_wanted = order[None, :] < wanted[:, None]
    recv_rank = jnp.sum((toward_me & before_wanted).astype(jnp.int32), axis=1)
    pick_row = jnp.where(remote, target * slot_count + recv_rank, devices * slot_count + wanted)
    odd = (matching != (order + 2) % 4) | (reversed_rows == 1)
    return (pick_row, reversed_rows, slot_row, matching, listed(remote), listed(odd))


def up16(n):
    return (n + 15) // 16 * 16


def strip_rows(n):
    return {6: 8, 12: 16}.get(n, n)


def params():
    return pltpu.CompilerParams(vmem_limit_bytes=VMEM_LIMIT)


def rims_kernel(slot_ref, lo_ref, hi_ref, top_ref, bottom_ref, out_ref, send_ref, colbuf):
    group, n = lo_ref.shape[0], lo_ref.shape[1]
    first = pl.program_id(0) * group * 4
    for g in range(group):
        colbuf[...] = lo_ref[g, :, 0:8, :].astype(F32).reshape(n * 8, 128)
        left = colbuf[pl.ds(0, n, 8), :]
        colbuf[...] = hi_ref[g, :, 8:16, :].astype(F32).reshape(n * 8, 128)
        right = colbuf[pl.ds(7, n, 8), :]
        out_ref[g, 0] = top_ref[g, 0]
        out_ref[g, 1] = right.astype(BF)
        out_ref[g, 2] = bottom_ref[g, 0]
        out_ref[g, 3] = left.astype(BF)
    for g in range(group):
        for e in range(4):
            slot = slot_ref[first + g * 4 + e]

            @pl.when(slot >= 0)
            def _():
                send_ref[slot] = out_ref[g, e]


def tile_rims(x, slot_row, rows):
    tiles, n, _, c = x.shape
    g = group_of(tiles, 4)
    last = n // 16 - 1
    return pl.pallas_call(
        rims_kernel,
        grid=(tiles // g,),
        in_specs=[
            pl.BlockSpec(memory_space=pltpu.SMEM),
            pl.BlockSpec((g, n, 16, c), lambda i: (i, 0, 0, 0)),
            pl.BlockSpec((g, n, 16, c), lambda i: (i, 0, last, 0)),
            pl.BlockSpec((g, 1, n, c), lambda i: (i, 0, 0, 0)),
            pl.BlockSpec((g, 1, n, c), lambda i: (i, n - 1, 0, 0)),
        ],
        out_specs=[tile_spec(g, 4, n, c), whole_spec((rows, n, c))],
        out_shape=[
            jax.ShapeDtypeStruct((tiles, 4, n, c), BF),
            jax.ShapeDtypeStruct((rows, n, c), BF),
        ],
        scratch_shapes=[pltpu.VMEM((n * 8, 128), F32)],
        compiler_params=params(),
        name="tile_rims",
    )(slot_row, x, x, x, x)


def silu(s):
    return s / (1.0 + jnp.exp(-s))


def strip_shifts(h, n):
    rows = h.shape[0]
    row = lax.broadcasted_iota(jnp.int32, h.shape, 0)
    half = h * 0.5
    down = jnp.where(row == 0, half, pltpu.roll(h, 1, 0))
    up = jnp.where(row == n - 1, half, pltpu.roll(h, rows - 1, 0))
    return down, up


def flip_matrix(rows, n):
    ri = lax.broadcasted_iota(jnp.int32, (rows, rows), 0)
    ci = lax.broadcasted_iota(jnp.int32, (rows, rows), 1)
    return (ri + ci == n - 1).astype(F32).astype(BF)


def put_shifts(ref, index, lane, h, n):
    down, up = strip_shifts(h, n)
    for s, part in enumerate((down, h, up)):
        ref[index + (slice(None), slice(lane + s * 128, lane + s * 128 + 128))] = part.astype(ref.dtype)


def each_tile(tiles, body):
    side = group_of(tiles, 3)

    def step(i, carry):
        for k in range(side):
            body(i * side + k, k)
        return carry

    lax.fori_loop(0, tiles // side, step, 0)


def each_listed(list_ref, body):
    def step(j, carry):
        body(list_ref[j])
        return carry

    lax.fori_loop(0, list_ref[list_ref.shape[0] - 1], step, 0)


def incoming(pick_ref, recv_ref, own_ref, i):
    rows = recv_ref.shape[0]
    pick = pick_ref[i]
    a = recv_ref[jnp.minimum(pick, rows - 1)].astype(F32)
    b = own_ref[jnp.maximum(pick - rows, 0)].astype(F32)
    return jnp.where(pick < rows, a, b)


def edge_taps(w_ref, e, lo):
    taps = ((0, 1, 2), (2, 5, 8), (6, 7, 8), (0, 3, 6))[e]
    return jnp.concatenate([w_ref[tap, lo : lo + 128, :] for tap in taps], axis=0)


def contributions(n, tiles, strip_of, w_ref, lo, rev_ref, edge_ref, odd_ref, lhs_ref, con_ref, taps_ref, buf):
    lp = lhs_ref.shape[2]
    for e in range(4):
        taps_ref[e] = edge_taps(w_ref, e, lo)

    def fill(t, k):
        for f in range(4):
            put_shifts(lhs_ref, (f, t), 0, strip_of(f, t, k), n)

    each_tile(tiles, fill)
    for f in range(4):
        lhs = lhs_ref[f].reshape(tiles * lp, 384).astype(BF)
        out = jnp.dot(lhs, taps_ref[(f + 2) % 4], preferred_element_type=F32)
        con_ref[f] = out.reshape(tiles, lp, 128)
    flip = flip_matrix(lp, n)

    def odd_one(i):
        f, t = i % 4, i // 4
        buf[...] = lhs_ref[f, t, :, 128:256].astype(F32)

        @pl.when(rev_ref[i] == 1)
        def _():
            buf[...] = jnp.dot(flip, buf[...].astype(BF), preferred_element_type=F32)

        put_shifts(lhs_ref, (f, t), 0, buf[...], n)
        con_ref[f, t] = jnp.dot(lhs_ref[f, t].astype(BF), taps_ref[edge_ref[i]], preferred_element_type=F32)

    each_listed(odd_ref, odd_one)


def skip_kernel(n, rev_ref, edge_ref, odd_ref, rim_ref, w_ref, out_ref, lhs_ref, con_ref, taps_ref, buf):
    tiles = rim_ref.shape[0] // 4
    contributions(
        n, tiles, lambda f, t, k: rim_ref[t * 4 + f].astype(F32), w_ref, 128,
        rev_ref, edge_ref, odd_ref, lhs_ref, con_ref, taps_ref, buf,
    )

    def put(t, k):
        for f in range(4):
            out_ref[t * 4 + f] = con_ref[f, t]

    each_tile(tiles, put)


def wide(rows):
    return BF if rows % 16 == 0 else F32


def skip_step(n, plan, rim, w):
    strips, lp, c = rim.shape
    smem = pl.BlockSpec(memory_space=pltpu.SMEM)
    vmem = pl.BlockSpec(memory_space=pltpu.VMEM)
    return pl.pallas_call(
        lambda *refs: skip_kernel(n, *refs),
        in_specs=[smem, smem, smem, vmem, vmem],
        out_specs=vmem,
        out_shape=jax.ShapeDtypeStruct((strips, lp, c), F32),
        scratch_shapes=[
            pltpu.VMEM((4, strips // 4, lp, 384), wide(lp)),
            pltpu.VMEM((4, strips // 4, lp, 128), F32),
            pltpu.VMEM((4, 384, 128), BF),
            pltpu.VMEM((lp, 128), F32),
        ],
        compiler_params=params(),
        cost_estimate=pl.CostEstimate(flops=strips * lp * 2 * 384 * 256, bytes_accessed=strips * lp * 768, transcendentals=0),
        name="skip_step",
    )(plan[1], plan[3], plan[5], rim, w.reshape(9, -1, c))


def corners(end):
    return (
        (0, 0, 3, 0), (0, end, 1, 0), (2, 0, 3, end), (2, end, 1, end),
        (3, 0, 0, 0), (3, end, 2, 0), (1, 0, 0, end), (1, end, 2, end),
    )


def rim_kernel(n, strips_in, nxt, refs):
    it = iter(refs)
    pick_ref, rev_ref, slot_ref, edge_ref, remote_ref, odd_ref = [next(it) for _ in range(6)]
    recv_ref, own_ref, sum_ref = next(it), next(it), next(it)
    w_ref = next(it) if strips_in else None
    ring_ref = next(it) if nxt == "shrink" else None
    skip_ref, wn_ref = (next(it), next(it)) if nxt == "halo" else (None, None)
    rim_ref, next_ref, send_ref = next(it), next(it), next(it)
    halo_ref, lhs_ref, con_ref = next(it), next(it), next(it)
    edge_buf, ring_buf, sum_buf, out_buf = next(it), next(it), next(it), next(it)
    lhsn_ref, conn_ref, taps_ref, big_buf = [next(it) for _ in range(4)] if nxt == "halo" else [None] * 4

    lp = recv_ref.shape[1]
    strips = own_ref.shape[0]
    tiles = strips // 4
    flip = flip_matrix(lp, n)

    if strips_in:

        def fetch(t, k):
            for e in range(4):
                i = t * 4 + e
                halo_ref[i] = incoming(pick_ref, recv_ref, own_ref, i).astype(BF)

        each_tile(tiles, fetch)

        def turn(i):
            @pl.when(rev_ref[i] == 1)
            def _():
                halo_ref[i] = jnp.dot(flip, halo_ref[i], preferred_element_type=F32).astype(BF)

        each_listed(odd_ref, turn)

        def fill(t, k):
            for e in range(4):
                put_shifts(lhs_ref, (e, t), 0, halo_ref[t * 4 + e].astype(F32), n)

        each_tile(tiles, fill)
        for e in range(4):
            lhs = lhs_ref[e].reshape(tiles * lp, 384).astype(BF)
            out = jnp.dot(lhs, edge_taps(w_ref, e, 0), preferred_element_type=F32)
            con_ref[e] = out.reshape(tiles, lp, 128)
    else:

        def fill(t, k):
            for e in range(4):
                con_ref[e, t] = incoming(pick_ref, recv_ref, own_ref, t * 4 + e)

        each_tile(tiles, fill)

    end = n - 1
    joints = (
        (0, 0, 3, 1), (0, end, 1, 1), (2, 0, 3, end - 1), (2, end, 1, end - 1),
        (3, 0, 0, 1), (3, end, 2, 1), (1, 0, 0, end - 1), (1, end, 2, end - 1),
    )
    if nxt == "shrink":
        out_buf[...] = jnp.zeros_like(out_buf)

    def finish(t, k):
        for e in range(4):
            edge_buf[k, e] = sum_ref[t * 4 + e] + con_ref[e, t]
        for e, cell, other, at in corners(end):
            cells = slice(cell, cell + 1)
            edge_buf[k, e, cells] = edge_buf[k, e, cells] + con_ref[other, t, at : at + 1]
        for e in range(4):
            y = silu(edge_buf[k, e]).astype(BF)
            rim_ref[t * 4 + e] = y
            edge_buf[k, e] = y.astype(F32)
        if nxt == "shrink":
            for e in range(4):
                ring_buf[k, e] = ring_ref[t * 4 + e].astype(F32)
            for e, cell, other, at in joints:
                ring_buf[k, e, cell : cell + 1] = edge_buf[k, other, at : at + 1]
            for e in range(4):
                sum_buf[k, e] = edge_buf[k, e] + ring_buf[k, e]
                small = sum_buf[k, e, pl.ds(0, lp // 2, 2), :] + sum_buf[k, e, pl.ds(1, lp // 2, 2), :]
                out_buf[k, e, 0 : lp // 2] = small * 0.25
                next_ref[t * 4 + e] = out_buf[k, e].astype(BF)

    each_tile(tiles, finish)

    if nxt == "halo":
        half = big_buf.shape[2] // 2

        def enlarged(f, t, k):
            rim = rim_ref[t * 4 + f].astype(F32)[0:half]
            big_buf[k, f, pl.ds(0, half, 2), :] = rim
            big_buf[k, f, pl.ds(1, half, 2), :] = rim
            return big_buf[k, f]

        contributions(
            2 * n, tiles, enlarged, wn_ref, 0,
            rev_ref, edge_ref, odd_ref, lhsn_ref, conn_ref, taps_ref, big_buf.at[0, 0],
        )

        def put(t, k):
            for f in range(4):
                next_ref[t * 4 + f] = (conn_ref[f, t] + skip_ref[t * 4 + f]).astype(BF)

        each_tile(tiles, put)

    def send(i):
        send_ref[slot_ref[i]] = next_ref[i]

    each_listed(remote_ref, send)


def rim_step(n, plan, recv, own, sums, w=None, ring=None, skip=None, wn=None):
    rows, lp, c = recv.shape
    strips = own.shape[0]
    tiles = strips // 4
    side = group_of(tiles, 3)
    nxt = "shrink" if ring is not None else "halo"
    smem = pl.BlockSpec(memory_space=pltpu.SMEM)
    vmem = pl.BlockSpec(memory_space=pltpu.VMEM)
    w = w if w is None else w.reshape(9, -1, c)
    wn = wn if wn is None else wn.reshape(9, -1, c)
    args = [recv, own, sums] + [a for a in (w, ring, skip, wn) if a is not None]
    lo = strip_rows(n // 2) if nxt == "shrink" else strip_rows(2 * n)
    outs = [
        jax.ShapeDtypeStruct((strips, lp, c), BF),
        jax.ShapeDtypeStruct((strips, lo, c), BF),
        jax.ShapeDtypeStruct((rows, lo, c), BF),
    ]
    scratch = [
        pltpu.VMEM((strips, lp, 128), BF),
        pltpu.VMEM((4, tiles, lp, 384), wide(lp)),
        pltpu.VMEM((4, tiles, lp, 128), F32),
        pltpu.VMEM((side, 4, lp, 128), F32),
        pltpu.VMEM((side, 4, lp, 128), F32),
        pltpu.VMEM((side, 4, lp, 128), F32),
        pltpu.VMEM((side, 4, lo, 128), F32),
    ]
    if nxt == "halo":
        scratch += [
            pltpu.VMEM((4, tiles, lo, 384), wide(lo)),
            pltpu.VMEM((4, tiles, lo, 128), F32),
            pltpu.VMEM((4, 384, 128), BF),
            pltpu.VMEM((side, 4, lo, 128), F32),
        ]

    def kernel(*refs):
        rim_kernel(n, w is not None, nxt, refs)

    return pl.pallas_call(
        kernel,
        in_specs=[smem] * 6 + [vmem] * len(args),
        out_specs=[vmem] * len(outs),
        out_shape=outs,
        scratch_shapes=scratch,
        compiler_params=params(),
        cost_estimate=pl.CostEstimate(flops=strips * lp * 2 * 384 * 512, bytes_accessed=strips * lp * 1500, transcendentals=0),
        name="rim_step",
    )(*plan, *args)


def spread_columns(strip, n, sublane, buf):
    buf[pl.ds(sublane, n, 8), :] = strip
    return buf[...].reshape(n, 8, 128)


def with_rims(x, rim, n, buf):
    sub = lax.broadcasted_iota(jnp.int32, (n, 8, 128), 1)
    head = jnp.where(sub == 0, spread_columns(rim[3], n, 0, buf), x[:, 0:8])
    tail = jnp.where(sub == 7, spread_columns(rim[1], n, 7, buf), x[:, n - 8 : n])
    x = jnp.concatenate([head, x[:, 8 : n - 8], tail], axis=1)
    return jnp.concatenate([rim[0][None], x[1 : n - 1], rim[2][None]], axis=0)


def column_shifts(x, n):
    col = lax.broadcasted_iota(jnp.int32, x.shape, 1)
    down = jnp.where(col == 0, 0.0, pltpu.roll(x, 1, 1))
    up = jnp.where(col == n - 1, 0.0, pltpu.roll(x, n - 1, 1))
    return down, x, up


def fill_pairs(y_ref, x, n):
    half, n_p = n // 2, y_ref.shape[1]
    zero = jnp.zeros((n_p, 384), BF)
    y_ref[0, :, 0:384] = zero
    y_ref[half, :, 384:768] = zero
    for s, body in enumerate(column_shifts(x, n)):
        b = body.astype(BF).reshape(half, 2, n, 128)
        y_ref[0:half, 0:n, 384 + s * 128 : 384 + s * 128 + 128] = b[:, 0]
        y_ref[1 : half + 1, 0:n, s * 128 : s * 128 + 128] = b[:, 1]


def fill_rows(u_ref, x, n):
    zero = jnp.zeros((u_ref.shape[1], 384), BF)
    u_ref[0] = zero
    u_ref[n + 1] = zero
    for s, body in enumerate(column_shifts(x, n)):
        u_ref[1 : n + 1, 0:n, s * 128 : s * 128 + 128] = body.astype(BF)


def pair_sums(y_ref, w_ref, q0, m, extra):
    n_p = y_ref.shape[1]
    a = y_ref[q0 : q0 + m].reshape(m * n_p, 768)
    b = y_ref[q0 + 1 : q0 + 1 + m].reshape(m * n_p, 768)
    acc = jnp.dot(a, w_ref[0:768, :], preferred_element_type=F32)
    acc = acc + jnp.dot(b, w_ref[768:1536, :], preferred_element_type=F32)
    acc = acc.reshape(m, n_p, 256)
    return acc if extra is None else acc + extra


def pair_chunks(n):
    half = n // 2
    m = 6 if half % 6 == 0 else half
    return [(q, m) for q in range(0, half, m)]


def column_of(acc, m, lo, sublane, colbuf):
    rows = jnp.stack([acc[:, lo : lo + 8, 0:128], acc[:, lo : lo + 8, 128:256]], axis=1)
    colbuf[0 : 16 * m] = rows.reshape(16 * m, 128)
    return colbuf[pl.ds(sublane, 2 * m, 8), :]


def put_sums(acc, sums_ref, g, q0, m, n, colbuf):
    cells = slice(2 * q0, 2 * q0 + 2 * m)
    if q0 == 0:
        sums_ref[g, 0] = acc[0, 0:n, 0:128]
    if q0 + m == n // 2:
        sums_ref[g, 2] = acc[m - 1, 0:n, 128:256]
    sums_ref[g, 3, cells] = column_of(acc, m, 0, 0, colbuf)
    sums_ref[g, 1, cells] = column_of(acc, m, n - 8, 7, colbuf)


def fill_pair_weights(raw_ref, lo, w_ref):
    for p in range(4):
        for col in range(3):
            at = slice((p * 3 + col) * 128, (p * 3 + col) * 128 + 128)
            for out in range(2):
                row = p - out
                tap = raw_ref[row * 3 + col, lo : lo + 128, :] if 0 <= row <= 2 else jnp.zeros((128, 128), BF)
                w_ref[at, out * 128 : out * 128 + 128] = tap


def fill_coarse_weights(raw_ref, w_ref):
    along = (((0,), (1, 2), ()), ((), (0, 1), (2,)))
    for b in range(2):
        for k in range(3):
            for slot in range(2):
                cols = along[b][slot + b]
                for out in range(2):
                    taps = [raw_ref[r * 3 + col, 0:128, :].astype(F32) for r in along[out][k] for col in cols]
                    total = sum(taps[1:], taps[0]) if taps else jnp.zeros((128, 128), F32)
                    w_ref[b, k, slot * 128 : slot * 128 + 128, out * 128 : out * 128 + 128] = total.astype(BF)


def enc_kernel(*refs):
    it = iter(refs[:-5])
    x_ref, raw_ref = next(it), next(it)
    rest = list(it)
    rim_ref = rest.pop(0) if len(rest) == 5 else None
    y_ref, sums_ref, ring_ref, s_ref = rest
    pairs, colbuf, sumbuf, ringbuf, w_ref = refs[-5:]

    @pl.when(pl.program_id(0) == 0)
    def _():
        fill_pair_weights(raw_ref, 0, w_ref)

    group, n = x_ref.shape[0], x_ref.shape[1]
    half = n // 2

    for g in range(group):
        x = x_ref[g].astype(F32)
        if rim_ref is not None:
            x = with_rims(x, [rim_ref[g, e].astype(F32) for e in range(4)], n, colbuf)
        fill_pairs(pairs, x, n)
        for q0, m in pair_chunks(n):
            acc = pair_sums(pairs, w_ref, q0, m, None)
            put_sums(acc, sums_ref, g, q0, m, n, colbuf)
            out = silu(acc).astype(BF)[:, 0:n]
            y_ref[g, q0 : q0 + m, 0] = out[:, :, 0:128]
            y_ref[g, q0 : q0 + m, 1] = out[:, :, 128:256]
            wide = out.astype(F32)
            if q0 == 0:
                ring_ref[g, 0] = out[0, :, 128:256]
            if q0 + m == half:
                ring_ref[g, 2] = out[m - 1, :, 0:128]
            ringbuf[1, 2 * q0 : 2 * q0 + 2 * m] = column_of(wide, m, n - 8, 6, colbuf)
            ringbuf[0, 2 * q0 : 2 * q0 + 2 * m] = column_of(wide, m, 0, 1, colbuf)
            both = wide[:, :, 0:128] + wide[:, :, 128:256]
            sumbuf[...] = both.reshape(m * n, 128)
            small = sumbuf[pl.ds(0, m * half, 2), :] + sumbuf[pl.ds(1, m * half, 2), :]
            s_ref[g, q0 : q0 + m] = (small * 0.25).reshape(m, half, 128).astype(BF)
        ring_ref[g, 1] = ringbuf[1].astype(BF)
        ring_ref[g, 3] = ringbuf[0].astype(BF)


def dec_kernel(x_ref, rim_ref, u_ref, *refs):
    refs = list(refs)
    urim_ref = refs.pop(0) if len(refs) == 10 else None
    raw_ref, y_ref, sums_ref, pairs, rows, colbuf, acc_ref, w_ref, wu_ref = refs

    @pl.when(pl.program_id(0) == 0)
    def _():
        fill_pair_weights(raw_ref, 128, w_ref)
        fill_coarse_weights(raw_ref, wu_ref)

    group, n = x_ref.shape[0], x_ref.shape[1]
    half = n // 2
    hp = rows.shape[1]

    for g in range(group):
        u = u_ref[g].astype(F32)
        if urim_ref is not None:
            u = with_rims(u, [urim_ref[g, e].astype(F32) for e in range(4)], half, colbuf.at[0 : half * 8])
        fill_rows(rows, u, half)
        x = with_rims(x_ref[g].astype(F32), [rim_ref[g, e].astype(F32) for e in range(4)], n, colbuf)
        fill_pairs(pairs, x, n)
        for q0, m in pair_chunks(n):
            for b in range(2):
                acc = None
                for k in range(3):
                    lhs = rows[q0 + k : q0 + k + m, :, b * 128 : b * 128 + 256].reshape(m * hp, 256)
                    part = jnp.dot(lhs, wu_ref[b, k], preferred_element_type=F32)
                    acc = part if acc is None else acc + part
                acc = acc.reshape(m, hp, 256)
                for i in range(m):
                    for p in range(2):
                        acc_ref[p, i, pl.ds(b, half, 2), :] = acc[i, 0:half, p * 128 : p * 128 + 128]
            extra = jnp.concatenate([acc_ref[0], acc_ref[1]], axis=2)
            acc = pair_sums(pairs, w_ref, q0, m, extra)
            put_sums(acc, sums_ref, g, q0, m, n, colbuf)
            out = silu(acc).astype(BF)[:, 0:n]
            y_ref[g, q0 : q0 + m, 0] = out[:, :, 0:128]
            y_ref[g, q0 : q0 + m, 1] = out[:, :, 128:256]


def last_kernel(pick_ref, recv_ref, own_ref, sum_ref, x_ref, y_ref, *scratch):
    rim_ref, edge_buf, slab_ref, colbuf, in_sem, out_sem, row_sem = scratch
    del x_ref
    strips, n = own_ref.shape[0], own_ref.shape[1]
    tiles = strips // 4
    parts = in_sem.shape[1]
    span = tiles // parts

    def slab(side, part):
        return y_ref.at[pl.ds(part * span, span), :, pl.ds(side * (n - 16), 16), :]

    def held(side, part):
        return slab_ref.at[side, pl.ds(part * span, span)]

    reads = [
        [pltpu.make_async_copy(slab(side, p), held(side, p), in_sem.at[side, p]) for p in range(parts)]
        for side in range(2)
    ]
    for p in range(parts):
        for side in range(2):
            reads[side][p].start()

    end = n - 1

    def finish(t, k):
        con = [incoming(pick_ref, recv_ref, own_ref, t * 4 + e) for e in range(4)]
        for e in range(4):
            edge_buf[k, e] = sum_ref[t * 4 + e] + con[e]
        for e, cell, other, at in corners(end):
            cells = slice(cell, cell + 1)
            edge_buf[k, e, cells] = edge_buf[k, e, cells] + con[other][at : at + 1]
        for e in range(4):
            rim_ref[t, e] = silu(edge_buf[k, e]).astype(BF)

    each_tile(tiles, finish)

    rows = [
        pltpu.make_async_copy(
            rim_ref.at[:, e, pl.ds(16, n - 32), :], y_ref.at[:, row, pl.ds(16, n - 32), :], row_sem.at[j]
        )
        for j, (e, row) in enumerate(((0, 0), (2, n - 1)))
    ]
    for copy in rows:
        copy.start()

    sub = lax.broadcasted_iota(jnp.int32, (n, 8, 128), 1)

    def patch(side, t):
        lo = 0 if side == 0 else n - 16
        near = slice(0, 8) if side == 0 else slice(8, 16)
        far = slice(8, 16) if side == 0 else slice(0, 8)
        x = slab_ref[side, t].astype(F32)
        cells = spread_columns(rim_ref[t, 3 if side == 0 else 1].astype(F32), n, 0 if side == 0 else 7, colbuf)
        new = jnp.where(sub == (0 if side == 0 else 7), cells, x[:, near])
        both = [new, x[:, far]] if side == 0 else [x[:, far], new]
        slab_ref[side, t] = jnp.concatenate(both, axis=1).astype(BF)
        slab_ref[side, t, 0] = rim_ref[t, 0, lo : lo + 16]
        slab_ref[side, t, n - 1] = rim_ref[t, 2, lo : lo + 16]

    writes = []
    for p in range(parts):
        for side in range(2):
            reads[side][p].wait()

            def step(t, carry, side=side):
                patch(side, t)
                return carry

            lax.fori_loop(p * span, p * span + span, step, 0)
            copy = pltpu.make_async_copy(held(side, p), slab(side, p), out_sem.at[side, p])
            copy.start()
            writes.append(copy)
    for copy in writes + rows:
        copy.wait()


def last_step(x, plan, recv, own, sums):
    tiles, n, _, c = x.shape
    strips = own.shape[0]
    parts = 4 if tiles % 4 == 0 else 1
    smem = pl.BlockSpec(memory_space=pltpu.SMEM)
    vmem = pl.BlockSpec(memory_space=pltpu.VMEM)
    anywhere = pl.BlockSpec(memory_space=pl.ANY)
    return pl.pallas_call(
        last_kernel,
        in_specs=[smem, vmem, vmem, vmem, anywhere],
        out_specs=anywhere,
        out_shape=jax.ShapeDtypeStruct(x.shape, BF),
        scratch_shapes=[
            pltpu.VMEM((tiles, 4, n, c), BF),
            pltpu.VMEM((group_of(tiles, 3), 4, n, c), F32),
            pltpu.VMEM((2, tiles, n, 16, c), BF),
            pltpu.VMEM((n * 8, c), F32),
            pltpu.SemaphoreType.DMA((2, parts)),
            pltpu.SemaphoreType.DMA((2, parts)),
            pltpu.SemaphoreType.DMA((2,)),
        ],
        input_output_aliases={4: 0},
        compiler_params=params(),
        name="last_step",
    )(plan[0], recv, own, sums, x)


def group_of(tiles, want):
    return max(g for g in range(1, want + 1) if tiles % g == 0)


def tile_spec(group, *dims):
    return pl.BlockSpec((group,) + dims, lambda i: (i,) + (0,) * len(dims))


def whole_spec(shape):
    return pl.BlockSpec(shape, lambda i: (0,) * len(shape))


def enc_conv(x, rim, w, want):
    tiles, n, _, c = x.shape
    half, n_p = n // 2, up16(n)
    g = group_of(tiles, want)
    m = pair_chunks(n)[0][1]
    args, specs = [x, w.reshape(9, c, c)], [tile_spec(g, n, n, c), whole_spec((9, c, c))]
    if rim is not None:
        args.append(rim.reshape(tiles, 4, n, c))
        specs.append(tile_spec(g, 4, n, c))
    y, sums, ring, s = pl.pallas_call(
        enc_kernel,
        grid=(tiles // g,),
        in_specs=specs,
        out_specs=[
            tile_spec(g, half, 2, n, c), tile_spec(g, 4, n, c), tile_spec(g, 4, n, c), tile_spec(g, half, half, c)
        ],
        out_shape=[
            jax.ShapeDtypeStruct((tiles, half, 2, n, c), BF),
            jax.ShapeDtypeStruct((tiles, 4, n, c), F32),
            jax.ShapeDtypeStruct((tiles, 4, n, c), BF),
            jax.ShapeDtypeStruct((tiles, half, half, c), BF),
        ],
        scratch_shapes=[
            pltpu.VMEM((half + 1, n_p, 768), BF),
            pltpu.VMEM((n * 8, 128), F32),
            pltpu.VMEM((m * n, 128), F32),
            pltpu.VMEM((2, n, 128), F32),
            pltpu.VMEM((1536, 256), BF),
        ],
        compiler_params=params(),
        cost_estimate=pl.CostEstimate(
            flops=tiles * n * n * 2 * 1536 * 128, bytes_accessed=tiles * n * n * 600, transcendentals=tiles * n * n * 128
        ),
        name="enc_conv",
    )(*args)
    strips = lambda a: a.reshape(tiles * 4, n, c)
    return y.reshape(tiles, n, n, c), strips(sums), strips(ring), s


def dec_conv(x, rim, u, urim, w, want):
    tiles, n, _, c = x.shape
    half, n_p, h_p = n // 2, up16(n), up16(n // 2)
    g = group_of(tiles, want)
    m = pair_chunks(n)[0][1]
    args = [x, rim.reshape(tiles, 4, n, c), u]
    specs = [tile_spec(g, n, n, c), tile_spec(g, 4, n, c), tile_spec(g, half, half, c)]
    if urim is not None:
        args.append(urim.reshape(tiles, 4, half, c))
        specs.append(tile_spec(g, 4, half, c))
    y, sums = pl.pallas_call(
        dec_kernel,
        grid=(tiles // g,),
        in_specs=specs + [whole_spec((9, 2 * c, c))],
        out_specs=[tile_spec(g, half, 2, n, c), tile_spec(g, 4, n, c)],
        out_shape=[
            jax.ShapeDtypeStruct((tiles, half, 2, n, c), BF),
            jax.ShapeDtypeStruct((tiles, 4, n, c), F32),
        ],
        scratch_shapes=[
            pltpu.VMEM((half + 1, n_p, 768), BF),
            pltpu.VMEM((half + 2, h_p, 384), BF),
            pltpu.VMEM((n * 8, 128), F32),
            pltpu.VMEM((2, m, n_p, 128), F32),
            pltpu.VMEM((1536, 256), BF),
            pltpu.VMEM((2, 3, 256, 256), BF),
        ],
        compiler_params=params(),
        cost_estimate=pl.CostEstimate(
            flops=tiles * n * n * 2 * 2300 * 128, bytes_accessed=tiles * n * n * 600, transcendentals=tiles * n * n * 128
        ),
        name="dec_conv",
    )(*args, w.reshape(9, 2 * c, c))
    return y.reshape(tiles, n, n, c), sums.reshape(tiles * 4, n, c)


def strips_of(field, ring=0):
    n = field.shape[1]
    far = n - 1 - ring
    out = jnp.stack([field[:, ring], field[:, :, far], field[:, far], field[:, :, ring]], axis=1)
    out = jnp.pad(out, ((0, 0), (0, 0), (0, strip_rows(n) - n), (0, 0)))
    return out.reshape(field.shape[0] * 4, strip_rows(n), field.shape[3])


def patched(field, rim):
    tiles, n, _, c = field.shape
    rim = rim.reshape(tiles, 4, -1, c)[:, :, :n]
    middle = jnp.concatenate(
        [rim[:, 3, 1 : n - 1, None], field[:, 1 : n - 1, 1 : n - 1], rim[:, 1, 1 : n - 1, None]], axis=2
    )
    return jnp.concatenate([rim[:, 0][:, None], middle, rim[:, 2][:, None]], axis=1)


def inner_sums(field, weight):
    return lax.conv_general_dilated(
        field,
        weight,
        (1, 1),
        ((1, 1), (1, 1)),
        dimension_numbers=("NHWC", "HWIO", "NHWC"),
        preferred_element_type=F32,
    )


def shrink(field):
    count, length, _, channels = field.shape
    blocks = field.astype(F32).reshape(count, length // 2, 2, length // 2, 2, channels)
    return (jnp.sum(blocks, axis=(2, 4)) * 0.25).astype(BF)


def enlarge(field):
    return jnp.repeat(jnp.repeat(field, 2, axis=1), 2, axis=2)


def per_device(features, edge_table, w_enc0, w_enc1, w_enc2, w_mid, w_dec2, w_dec1, w_dec0):
    tiles, n0 = features.shape[0], features.shape[1]
    devices = lax.axis_size("tile")
    position = lax.axis_index("tile")
    cap = pair_capacity(FACE_TILES, tiles)
    rows = devices * cap
    slot_row = send_slots(edge_table, position, tiles, cap)

    def trade(strips):
        length = strips.shape[1]
        out = lax.all_to_all(
            strips.reshape(devices, cap * length, 128), "tile", split_axis=0, concat_axis=0, tiled=True
        )
        return out.reshape(rows, length, 128)

    def after(value, token):
        return lax.optimization_barrier((value, token))[0]

    rim0, send = tile_rims(features, slot_row, rows)
    rim0 = rim0.reshape(tiles * 4, n0, 128)
    plan = receive_plan(after(edge_table, send), slot_row, position, tiles, cap, devices)
    recv = trade(send)
    enc0, sums, ring, x1 = enc_conv(features, None, w_enc0, 1)
    enc0_rim, x1_rim, send = rim_step(n0, plan, recv, rim0, sums, w=w_enc0, ring=ring)

    recv = trade(send)
    enc1, sums, ring, x2 = enc_conv(x1, x1_rim, w_enc1, 4)
    enc1_rim, x2_rim, send = rim_step(n0 // 2, plan, recv, x1_rim, sums, w=w_enc1, ring=ring)

    recv = trade(send)
    sums = inner_sums(patched(x2, x2_rim), w_enc2)
    enc2 = jax.nn.silu(sums).astype(BF)
    enc2_rim, x3_rim, send = rim_step(
        n0 // 4, plan, recv, x2_rim, strips_of(sums), w=w_enc2, ring=strips_of(enc2, 1)
    )

    recv = trade(send)
    sums = inner_sums(patched(shrink(enc2), x3_rim), w_mid)
    middle = jax.nn.silu(sums).astype(BF)
    skip2 = skip_step(n0 // 4, plan, enc2_rim, w_dec2)
    skip0 = skip_step(n0, plan, after(enc0_rim, x3_rim), w_dec0)
    mid_rim, own, send = rim_step(
        n0 // 8, plan, recv, x3_rim, strips_of(sums), w=w_mid,
        skip=skip2, wn=w_dec2,
    )

    recv = trade(send)
    joined = jnp.concatenate([enlarge(patched(middle, mid_rim)), patched(enc2, enc2_rim)], axis=3)
    sums = inner_sums(joined, w_dec2)
    dec2 = jax.nn.silu(sums).astype(BF)
    skip1 = skip_step(n0 // 2, plan, after(enc1_rim, mid_rim), w_dec1)
    dec2_rim, own, send = rim_step(
        n0 // 4, plan, recv, own, strips_of(sums), skip=skip1, wn=w_dec1
    )

    recv = trade(send)
    dec1, sums = dec_conv(enc1, enc1_rim, patched(dec2, dec2_rim), None, w_dec1, 4)
    dec1_rim, own, send = rim_step(
        n0 // 2, plan, recv, own, sums, skip=skip0, wn=w_dec0
    )

    recv = trade(send)
    dec0, sums = dec_conv(enc0, enc0_rim, dec1, dec1_rim, w_dec0, 1)
    return last_step(dec0, plan, recv, own, sums)


def solution(mesh):
    return jax.shard_map(
        per_device,
        mesh=mesh,
        in_specs=(P(("grp", "tile"), None, None, None), P(), P(), P(), P(), P(), P(), P(), P()),
        out_specs=P(("grp", "tile"), None, None, None),
        check_vma=False,
    )
```

```python
import jax
import jax.numpy as jnp
import numpy as np
from jax import lax
from jax.experimental import pallas as pl
from jax.experimental.pallas import tpu as pltpu
from jax.sharding import PartitionSpec as P

FACE_TILES = 8
EARLY_TILES = (0, 0, 0)
VMEM_LIMIT = 50 * 2**20
BF = jnp.bfloat16
F32 = jnp.float32


def cube_links(tiles_side):
    basis = np.eye(3, dtype=np.int64)
    frames = []
    for axis_id in range(3):
        for orient in (1, -1):
            frames.append(
                (orient * basis[axis_id], basis[(axis_id + 1) % 3], basis[(axis_id + 2) % 3])
            )
    per_face = tiles_side * tiles_side
    tile_total = 6 * per_face
    centres = np.zeros((tile_total, 3), np.int64)
    lookup = {}
    for face_id in range(6):
        normal, row_axis, col_axis = frames[face_id]
        for row_id in range(tiles_side):
            for col_id in range(tiles_side):
                slot_id = face_id * per_face + row_id * tiles_side + col_id
                centre = (
                    tiles_side * normal
                    + (2 * row_id + 1 - tiles_side) * row_axis
                    + (2 * col_id + 1 - tiles_side) * col_axis
                )
                centres[slot_id] = centre
                lookup[tuple((int(entry) for entry in centre))] = slot_id
    partner = np.zeros((tile_total, 4), np.int64)
    for slot_id in range(tile_total):
        normal, row_axis, col_axis = frames[slot_id // per_face]
        outward = (-row_axis, col_axis, row_axis, -col_axis)
        for edge_id in range(4):
            beyond = tuple((int(entry) for entry in centres[slot_id] + 2 * outward[edge_id]))
            if beyond in lookup:
                partner[slot_id, edge_id] = lookup[beyond]
            else:
                partner[slot_id, edge_id] = lookup[
                    tuple((int(entry) for entry in centres[slot_id] + outward[edge_id] - normal))
                ]
    return partner


def pair_capacity(tiles_side, tiles_here):
    partner = cube_links(tiles_side)
    tile_total = partner.shape[0]
    blocks = tile_total // tiles_here
    source = np.repeat(np.arange(tile_total) // tiles_here, 4)
    target = partner.reshape(-1) // tiles_here
    identity = np.eye(blocks, dtype=np.int64)
    shared = identity[source].T @ identity[target]
    shared = shared * (1 - identity)
    return max(int(shared.max()), 1)


def own_strips(edge_table, position, tiles_here):
    rows = lax.dynamic_slice_in_dim(edge_table, position * tiles_here, tiles_here, 0)
    rows = rows.reshape(tiles_here * 4, 2)
    return rows[:, 0], rows[:, 1] // 2, rows[:, 1] % 2


def send_slots(edge_table, position, tiles_here, slot_count):
    partner, _, _ = own_strips(edge_table, position, tiles_here)
    target = partner // tiles_here
    order = jnp.arange(tiles_here * 4, dtype=jnp.int32)
    earlier = (order[None, :] < order[:, None]) & (target[None, :] == target[:, None])
    slot_rank = jnp.sum(earlier.astype(jnp.int32), axis=1)
    return jnp.where(target != position, target * slot_count + slot_rank, -1)


def listed(mask):
    order = jnp.arange(mask.shape[0], dtype=jnp.int32)
    rank = jnp.sum((mask[None, :] & (order[None, :] < order[:, None])).astype(jnp.int32), axis=1)
    hit = mask[None, :] & (rank[None, :] == order[:, None])
    found = jnp.sum(jnp.where(hit, order[None, :], 0), axis=1)
    return jnp.concatenate([found, jnp.sum(mask.astype(jnp.int32), keepdims=True)])


def receive_plan(edge_table, slot_row, position, tiles_here, slot_count, devices):
    strip_count = tiles_here * 4
    partner, matching, reversed_rows = own_strips(edge_table, position, tiles_here)
    target = partner // tiles_here
    order = jnp.arange(strip_count, dtype=jnp.int32)
    remote = target != position
    wanted = partner % tiles_here * 4 + matching
    toward_me = edge_table[:, :, 0].reshape(devices, strip_count) // tiles_here == position
    before = (order[:, None] < order[None, :]).astype(BF)
    ranks = jnp.dot(toward_me.astype(BF), before, preferred_element_type=F32).astype(BF)
    blocks = jnp.arange(devices, dtype=jnp.int32)
    from_target = (target[:, None] == blocks[None, :]).astype(BF)
    their_ranks = jnp.dot(from_target, ranks, preferred_element_type=F32)
    recv_rank = jnp.sum(jnp.where(wanted[:, None] == order[None, :], their_ranks, 0.0), axis=1).astype(jnp.int32)
    pick_row = jnp.where(remote, target * slot_count + recv_rank, devices * slot_count + wanted)
    odd = (matching != (order + 2) % 4) | (reversed_rows == 1)
    return (pick_row, reversed_rows, slot_row, matching, listed(remote), listed(odd))


def up16(n):
    return (n + 15) // 16 * 16


def strip_rows(n):
    return {6: 8, 12: 16}.get(n, n)


def params():
    return pltpu.CompilerParams(vmem_limit_bytes=VMEM_LIMIT)


def rims_kernel(slot_ref, lo_ref, hi_ref, top_ref, bottom_ref, out_ref, send_ref, colbuf):
    group, n = lo_ref.shape[0], lo_ref.shape[1]
    first = pl.program_id(0) * group * 4
    for g in range(group):
        colbuf[...] = lo_ref[g, :, 0:8, :].astype(F32).reshape(n * 8, 128)
        left = colbuf[pl.ds(0, n, 8), :]
        colbuf[...] = hi_ref[g, :, 8:16, :].astype(F32).reshape(n * 8, 128)
        right = colbuf[pl.ds(7, n, 8), :]
        out_ref[g, 0] = top_ref[g, 0]
        out_ref[g, 1] = right.astype(BF)
        out_ref[g, 2] = bottom_ref[g, 0]
        out_ref[g, 3] = left.astype(BF)
    for g in range(group):
        for e in range(4):
            slot = slot_ref[first + g * 4 + e]

            @pl.when(slot >= 0)
            def _():
                send_ref[slot] = out_ref[g, e]


def tile_rims(x, slot_row, rows):
    tiles, n, _, c = x.shape
    g = group_of(tiles, 4)
    last = n // 16 - 1
    return pl.pallas_call(
        rims_kernel,
        grid=(tiles // g,),
        in_specs=[
            pl.BlockSpec(memory_space=pltpu.SMEM),
            pl.BlockSpec((g, n, 16, c), lambda i: (i, 0, 0, 0)),
            pl.BlockSpec((g, n, 16, c), lambda i: (i, 0, last, 0)),
            pl.BlockSpec((g, 1, n, c), lambda i: (i, 0, 0, 0)),
            pl.BlockSpec((g, 1, n, c), lambda i: (i, n - 1, 0, 0)),
        ],
        out_specs=[tile_spec(g, 4, n, c), whole_spec((rows, n, c))],
        out_shape=[
            jax.ShapeDtypeStruct((tiles, 4, n, c), BF),
            jax.ShapeDtypeStruct((rows, n, c), BF),
        ],
        scratch_shapes=[pltpu.VMEM((n * 8, 128), F32)],
        compiler_params=params(),
        name="tile_rims",
    )(slot_row, x, x, x, x)


def silu(s):
    half = s * 0.5
    return half + half * jnp.tanh(half)


def strip_shifts(h, n):
    rows = h.shape[0]
    row = lax.broadcasted_iota(jnp.int32, h.shape, 0)
    half = h * 0.5
    down = jnp.where(row == 0, half, pltpu.roll(h, 1, 0))
    up = jnp.where(row == n - 1, half, pltpu.roll(h, rows - 1, 0))
    return down, up


def flip_matrix(rows, n):
    ri = lax.broadcasted_iota(jnp.int32, (rows, rows), 0)
    ci = lax.broadcasted_iota(jnp.int32, (rows, rows), 1)
    return (ri + ci == n - 1).astype(F32).astype(BF)


def put_shifts(ref, index, lane, h, n):
    down, up = strip_shifts(h, n)
    for s, part in enumerate((down, h, up)):
        ref[index + (slice(None), slice(lane + s * 128, lane + s * 128 + 128))] = part.astype(ref.dtype)


def each_tile(tiles, body):
    side = group_of(tiles, 3)

    def step(i, carry):
        for k in range(side):
            body(i * side + k, k)
        return carry

    lax.fori_loop(0, tiles // side, step, 0)


def each_listed(list_ref, body):
    def step(j, carry):
        body(list_ref[j])
        return carry

    lax.fori_loop(0, list_ref[list_ref.shape[0] - 1], step, 0)


def incoming(pick_ref, recv_ref, own_ref, i):
    rows = recv_ref.shape[0]
    pick = pick_ref[i]
    a = recv_ref[jnp.minimum(pick, rows - 1)].astype(F32)
    b = own_ref[jnp.maximum(pick - rows, 0)].astype(F32)
    return jnp.where(pick < rows, a, b)


def edge_taps(w_ref, e, lo):
    taps = ((0, 1, 2), (2, 5, 8), (6, 7, 8), (0, 3, 6))[e]
    return jnp.concatenate([w_ref[tap, lo : lo + 128, :] for tap in taps], axis=0)


def contributions(n, tiles, strip_of, w_ref, lo, rev_ref, edge_ref, odd_ref, lhs_ref, con_ref, taps_ref, buf):
    lp = lhs_ref.shape[2]
    for e in range(4):
        taps_ref[e] = edge_taps(w_ref, e, lo)

    def fill(t, k):
        for f in range(4):
            put_shifts(lhs_ref, (f, t), 0, strip_of(f, t, k), n)

    each_tile(tiles, fill)
    for f in range(4):
        lhs = lhs_ref[f].reshape(tiles * lp, 384).astype(BF)
        out = jnp.dot(lhs, taps_ref[(f + 2) % 4], preferred_element_type=F32)
        con_ref[f] = out.reshape(tiles, lp, 128)
    flip = flip_matrix(lp, n)

    def odd_one(i):
        f, t = i % 4, i // 4
        buf[...] = lhs_ref[f, t, :, 128:256].astype(F32)

        @pl.when(rev_ref[i] == 1)
        def _():
            buf[...] = jnp.dot(flip, buf[...].astype(BF), preferred_element_type=F32)

        put_shifts(lhs_ref, (f, t), 0, buf[...], n)
        con_ref[f, t] = jnp.dot(lhs_ref[f, t].astype(BF), taps_ref[edge_ref[i]], preferred_element_type=F32)

    each_listed(odd_ref, odd_one)


def skip_kernel(n, rev_ref, edge_ref, odd_ref, rim_ref, w_ref, out_ref, lhs_ref, con_ref, taps_ref, buf):
    tiles = rim_ref.shape[0] // 4
    contributions(
        n, tiles, lambda f, t, k: rim_ref[t * 4 + f].astype(F32), w_ref, 128,
        rev_ref, edge_ref, odd_ref, lhs_ref, con_ref, taps_ref, buf,
    )

    def put(t, k):
        for f in range(4):
            out_ref[t * 4 + f] = con_ref[f, t]

    each_tile(tiles, put)


def wide(rows):
    return BF if rows % 16 == 0 else F32


def skip_step(n, plan, rim, w):
    strips, lp, c = rim.shape
    smem = pl.BlockSpec(memory_space=pltpu.SMEM)
    vmem = pl.BlockSpec(memory_space=pltpu.VMEM)
    return pl.pallas_call(
        lambda *refs: skip_kernel(n, *refs),
        in_specs=[smem, smem, smem, vmem, vmem],
        out_specs=vmem,
        out_shape=jax.ShapeDtypeStruct((strips, lp, c), F32),
        scratch_shapes=[
            pltpu.VMEM((4, strips // 4, lp, 384), wide(lp)),
            pltpu.VMEM((4, strips // 4, lp, 128), F32),
            pltpu.VMEM((4, 384, 128), BF),
            pltpu.VMEM((lp, 128), F32),
        ],
        compiler_params=params(),
        cost_estimate=pl.CostEstimate(flops=strips * lp * 2 * 384 * 256, bytes_accessed=strips * lp * 768, transcendentals=0),
        name="skip_step",
    )(plan[1], plan[3], plan[5], rim, w.reshape(9, -1, c))


def corners(end):
    return (
        (0, 0, 3, 0), (0, end, 1, 0), (2, 0, 3, end), (2, end, 1, end),
        (3, 0, 0, 0), (3, end, 2, 0), (1, 0, 0, end), (1, end, 2, end),
    )


def rim_kernel(n, strips_in, nxt, refs):
    it = iter(refs)
    pick_ref, rev_ref, slot_ref, edge_ref, remote_ref, odd_ref = [next(it) for _ in range(6)]
    recv_ref, own_ref, sum_ref = next(it), next(it), next(it)
    w_ref = next(it) if strips_in else None
    ring_ref = next(it) if nxt == "shrink" else None
    skip_ref, wn_ref = (next(it), next(it)) if nxt == "halo" else (None, None)
    rim_ref, next_ref, send_ref = next(it), next(it), next(it)
    halo_ref, lhs_ref, con_ref = next(it), next(it), next(it)
    edge_buf, ring_buf, sum_buf, out_buf = next(it), next(it), next(it), next(it)
    lhsn_ref, conn_ref, taps_ref, big_buf = [next(it) for _ in range(4)] if nxt == "halo" else [None] * 4

    lp = recv_ref.shape[1]
    strips = own_ref.shape[0]
    tiles = strips // 4
    flip = flip_matrix(lp, n)

    if strips_in:

        def fetch(t, k):
            for e in range(4):
                i = t * 4 + e
                halo_ref[i] = incoming(pick_ref, recv_ref, own_ref, i).astype(BF)

        each_tile(tiles, fetch)

        def turn(i):
            @pl.when(rev_ref[i] == 1)
            def _():
                halo_ref[i] = jnp.dot(flip, halo_ref[i], preferred_element_type=F32).astype(BF)

        each_listed(odd_ref, turn)

        def fill(t, k):
            for e in range(4):
                put_shifts(lhs_ref, (e, t), 0, halo_ref[t * 4 + e].astype(F32), n)

        each_tile(tiles, fill)
        for e in range(4):
            lhs = lhs_ref[e].reshape(tiles * lp, 384).astype(BF)
            out = jnp.dot(lhs, edge_taps(w_ref, e, 0), preferred_element_type=F32)
            con_ref[e] = out.reshape(tiles, lp, 128)
    else:

        def fill(t, k):
            for e in range(4):
                con_ref[e, t] = incoming(pick_ref, recv_ref, own_ref, t * 4 + e)

        each_tile(tiles, fill)

    end = n - 1
    joints = (
        (0, 0, 3, 1), (0, end, 1, 1), (2, 0, 3, end - 1), (2, end, 1, end - 1),
        (3, 0, 0, 1), (3, end, 2, 1), (1, 0, 0, end - 1), (1, end, 2, end - 1),
    )
    if nxt == "shrink":
        out_buf[...] = jnp.zeros_like(out_buf)

    def finish(t, k):
        for e in range(4):
            edge_buf[k, e] = sum_ref[t * 4 + e] + con_ref[e, t]
        for e, cell, other, at in corners(end):
            cells = slice(cell, cell + 1)
            edge_buf[k, e, cells] = edge_buf[k, e, cells] + con_ref[other, t, at : at + 1]
        for e in range(4):
            y = silu(edge_buf[k, e]).astype(BF)
            rim_ref[t * 4 + e] = y
            edge_buf[k, e] = y.astype(F32)
        if nxt == "shrink":
            for e in range(4):
                ring_buf[k, e] = ring_ref[t * 4 + e].astype(F32)
            for e, cell, other, at in joints:
                ring_buf[k, e, cell : cell + 1] = edge_buf[k, other, at : at + 1]
            for e in range(4):
                sum_buf[k, e] = edge_buf[k, e] + ring_buf[k, e]
                small = sum_buf[k, e, pl.ds(0, lp // 2, 2), :] + sum_buf[k, e, pl.ds(1, lp // 2, 2), :]
                out_buf[k, e, 0 : lp // 2] = small * 0.25
                next_ref[t * 4 + e] = out_buf[k, e].astype(BF)

    each_tile(tiles, finish)

    if nxt == "halo":
        half = big_buf.shape[2] // 2

        def enlarged(f, t, k):
            rim = rim_ref[t * 4 + f].astype(F32)[0:half]
            big_buf[k, f, pl.ds(0, half, 2), :] = rim
            big_buf[k, f, pl.ds(1, half, 2), :] = rim
            return big_buf[k, f]

        contributions(
            2 * n, tiles, enlarged, wn_ref, 0,
            rev_ref, edge_ref, odd_ref, lhsn_ref, conn_ref, taps_ref, big_buf.at[0, 0],
        )

        def put(t, k):
            for f in range(4):
                next_ref[t * 4 + f] = (conn_ref[f, t] + skip_ref[t * 4 + f]).astype(BF)

        each_tile(tiles, put)

    def send(i):
        send_ref[slot_ref[i]] = next_ref[i]

    each_listed(remote_ref, send)


def rim_step(n, plan, recv, own, sums, w=None, ring=None, skip=None, wn=None):
    rows, lp, c = recv.shape
    strips = own.shape[0]
    tiles = strips // 4
    side = group_of(tiles, 3)
    nxt = "shrink" if ring is not None else "halo"
    smem = pl.BlockSpec(memory_space=pltpu.SMEM)
    vmem = pl.BlockSpec(memory_space=pltpu.VMEM)
    w = w if w is None else w.reshape(9, -1, c)
    wn = wn if wn is None else wn.reshape(9, -1, c)
    args = [recv, own, sums] + [a for a in (w, ring, skip, wn) if a is not None]
    lo = strip_rows(n // 2) if nxt == "shrink" else strip_rows(2 * n)
    outs = [
        jax.ShapeDtypeStruct((strips, lp, c), BF),
        jax.ShapeDtypeStruct((strips, lo, c), BF),
        jax.ShapeDtypeStruct((rows, lo, c), BF),
    ]
    scratch = [
        pltpu.VMEM((strips, lp, 128), BF),
        pltpu.VMEM((4, tiles, lp, 384), wide(lp)),
        pltpu.VMEM((4, tiles, lp, 128), F32),
        pltpu.VMEM((side, 4, lp, 128), F32),
        pltpu.VMEM((side, 4, lp, 128), F32),
        pltpu.VMEM((side, 4, lp, 128), F32),
        pltpu.VMEM((side, 4, lo, 128), F32),
    ]
    if nxt == "halo":
        scratch += [
            pltpu.VMEM((4, tiles, lo, 384), wide(lo)),
            pltpu.VMEM((4, tiles, lo, 128), F32),
            pltpu.VMEM((4, 384, 128), BF),
            pltpu.VMEM((side, 4, lo, 128), F32),
        ]

    def kernel(*refs):
        rim_kernel(n, w is not None, nxt, refs)

    return pl.pallas_call(
        kernel,
        in_specs=[smem] * 6 + [vmem] * len(args),
        out_specs=[vmem] * len(outs),
        out_shape=outs,
        scratch_shapes=scratch,
        compiler_params=params(),
        cost_estimate=pl.CostEstimate(flops=strips * lp * 2 * 384 * 512, bytes_accessed=strips * lp * 1500, transcendentals=0),
        name="rim_step",
    )(*plan, *args)


def spread_columns(strip, n, sublane, buf):
    buf[pl.ds(sublane, n, 8), :] = strip
    return buf[...].reshape(n, 8, 128)


def with_rims(x, rim, n, buf):
    sub = lax.broadcasted_iota(jnp.int32, (n, 8, 128), 1)
    head = jnp.where(sub == 0, spread_columns(rim[3], n, 0, buf), x[:, 0:8])
    tail = jnp.where(sub == 7, spread_columns(rim[1], n, 7, buf), x[:, n - 8 : n])
    x = jnp.concatenate([head, x[:, 8 : n - 8], tail], axis=1)
    return jnp.concatenate([rim[0][None], x[1 : n - 1], rim[2][None]], axis=0)


def column_shifts(x, n):
    sub = lax.broadcasted_iota(jnp.int32, (x.shape[0], 8, 128), 1)
    down = pltpu.roll(x, 1, 1)
    up = pltpu.roll(x, n - 1, 1)
    down = jnp.concatenate([jnp.where(sub == 0, 0.0, down[:, 0:8]), down[:, 8:n]], axis=1)
    up = jnp.concatenate([up[:, 0 : n - 8], jnp.where(sub == 7, 0.0, up[:, n - 8 : n])], axis=1)
    return down, x, up


def fill_pairs(y_ref, x, n):
    half, n_p = n // 2, y_ref.shape[1]
    zero = jnp.zeros((n_p, 384), BF)
    y_ref[0, :, 0:384] = zero
    y_ref[half, :, 384:768] = zero
    for s, body in enumerate(column_shifts(x, n)):
        b = body.astype(BF).reshape(half, 2, n, 128)
        y_ref[0:half, 0:n, 384 + s * 128 : 384 + s * 128 + 128] = b[:, 0]
        y_ref[1 : half + 1, 0:n, s * 128 : s * 128 + 128] = b[:, 1]


def fill_rows(u_ref, x, n):
    zero = jnp.zeros((u_ref.shape[1], 384), BF)
    u_ref[0] = zero
    u_ref[n + 1] = zero
    for s, body in enumerate(column_shifts(x, n)):
        u_ref[1 : n + 1, 0:n, s * 128 : s * 128 + 128] = body.astype(BF)


def pair_sums(y_ref, w_ref, q0, m, extra):
    n_p = y_ref.shape[1]
    a = y_ref[q0 : q0 + m].reshape(m * n_p, 768)
    b = y_ref[q0 + 1 : q0 + 1 + m].reshape(m * n_p, 768)
    acc = jnp.dot(a, w_ref[0:768, :], preferred_element_type=F32)
    acc = acc + jnp.dot(b, w_ref[768:1536, :], preferred_element_type=F32)
    acc = acc.reshape(m, n_p, 256)
    return acc if extra is None else acc + extra


def pair_chunks(n, most):
    half = n // 2
    m = max(m for m in range(1, most + 1) if half % m == 0)
    return [(q, m) for q in range(0, half, m)]


ENC_PAIRS = {48: 24}
DEC_PAIRS = {48: 12}


def column_of(acc, m, lo, sublane, colbuf):
    rows = jnp.stack([acc[:, lo : lo + 8, 0:128], acc[:, lo : lo + 8, 128:256]], axis=1)
    colbuf[0 : 16 * m] = rows.reshape(16 * m, 128)
    return colbuf[pl.ds(sublane, 2 * m, 8), :]


def put_sums(acc, sums_ref, g, q0, m, n, colbuf):
    cells = slice(2 * q0, 2 * q0 + 2 * m)
    if q0 == 0:
        sums_ref[g, 0] = acc[0, 0:n, 0:128]
    if q0 + m == n // 2:
        sums_ref[g, 2] = acc[m - 1, 0:n, 128:256]
    sums_ref[g, 3, cells] = column_of(acc, m, 0, 0, colbuf)
    sums_ref[g, 1, cells] = column_of(acc, m, n - 8, 7, colbuf)


def fill_pair_weights(raw_ref, lo, w_ref):
    for p in range(4):
        for col in range(3):
            at = slice((p * 3 + col) * 128, (p * 3 + col) * 128 + 128)
            for out in range(2):
                row = p - out
                tap = raw_ref[row * 3 + col, lo : lo + 128, :] if 0 <= row <= 2 else jnp.zeros((128, 128), BF)
                w_ref[at, out * 128 : out * 128 + 128] = tap


def fill_coarse_weights(raw_ref, w_ref):
    along = (((0,), (1, 2), ()), ((), (0, 1), (2,)))
    for b in range(2):
        for k in range(3):
            for slot in range(2):
                cols = along[b][slot + b]
                for out in range(2):
                    taps = [raw_ref[r * 3 + col, 0:128, :].astype(F32) for r in along[out][k] for col in cols]
                    total = sum(taps[1:], taps[0]) if taps else jnp.zeros((128, 128), F32)
                    w_ref[b, k, slot * 128 : slot * 128 + 128, out * 128 : out * 128 + 128] = total.astype(BF)


def enc_kernel(*refs):
    it = iter(refs[:-5])
    x_ref, raw_ref = next(it), next(it)
    rest = list(it)
    rim_ref = rest.pop(0) if len(rest) == 5 else None
    y_ref, sums_ref, ring_ref, s_ref = rest
    pairs, colbuf, sumbuf, ringbuf, w_ref = refs[-5:]

    @pl.when(pl.program_id(0) == 0)
    def _():
        fill_pair_weights(raw_ref, 0, w_ref)

    group, n = x_ref.shape[0], x_ref.shape[1]
    half = n // 2

    for g in range(group):
        x = x_ref[g].astype(F32)
        if rim_ref is not None:
            x = with_rims(x, [rim_ref[g, e].astype(F32) for e in range(4)], n, colbuf)
        fill_pairs(pairs, x, n)
        for q0, m in pair_chunks(n, ENC_PAIRS.get(n, 6)):
            acc = pair_sums(pairs, w_ref, q0, m, None)
            put_sums(acc, sums_ref, g, q0, m, n, colbuf)
            out = silu(acc).astype(BF)[:, 0:n]
            y_ref[g, q0 : q0 + m, 0] = out[:, :, 0:128]
            y_ref[g, q0 : q0 + m, 1] = out[:, :, 128:256]
            wide = out.astype(F32)
            if q0 == 0:
                ring_ref[g, 0] = out[0, :, 128:256]
            if q0 + m == half:
                ring_ref[g, 2] = out[m - 1, :, 0:128]
            ringbuf[1, 2 * q0 : 2 * q0 + 2 * m] = column_of(wide, m, n - 8, 6, colbuf)
            ringbuf[0, 2 * q0 : 2 * q0 + 2 * m] = column_of(wide, m, 0, 1, colbuf)
            both = wide[:, :, 0:128] + wide[:, :, 128:256]
            sumbuf[...] = both.reshape(m * n, 128)
            small = sumbuf[pl.ds(0, m * half, 2), :] + sumbuf[pl.ds(1, m * half, 2), :]
            s_ref[g, q0 : q0 + m] = (small * 0.25).reshape(m, half, 128).astype(BF)
        ring_ref[g, 1] = ringbuf[1].astype(BF)
        ring_ref[g, 3] = ringbuf[0].astype(BF)


def skip_sums_kernel(x_ref, rim_ref, raw_ref, out_ref, pairs, colbuf, w_ref):
    n = x_ref.shape[1]

    @pl.when(pl.program_id(0) == 0)
    def _():
        fill_pair_weights(raw_ref, 128, w_ref)

    x = with_rims(x_ref[0].astype(F32), [rim_ref[0, e].astype(F32) for e in range(4)], n, colbuf)
    fill_pairs(pairs, x, n)
    for q0, m in pair_chunks(n, DEC_PAIRS.get(n, 6)):
        out_ref[0, q0 : q0 + m] = pair_sums(pairs, w_ref, q0, m, None)


def skip_sums(x, rim, w, first, count):
    tiles, n, _, c = x.shape
    half, n_p = n // 2, up16(n)
    return pl.pallas_call(
        skip_sums_kernel,
        grid=(count,),
        in_specs=[
            pl.BlockSpec((1, n, n, c), lambda i: (first + i, 0, 0, 0)),
            pl.BlockSpec((1, 4, n, c), lambda i: (first + i, 0, 0, 0)),
            whole_spec((9, 2 * c, c)),
        ],
        out_specs=tile_spec(1, half, n_p, 2 * c),
        out_shape=jax.ShapeDtypeStruct((count, half, n_p, 2 * c), F32),
        scratch_shapes=[
            pltpu.VMEM((half + 1, n_p, 768), BF),
            pltpu.VMEM((n * 8, 128), F32),
            pltpu.VMEM((1536, 256), BF),
        ],
        compiler_params=params(),
        cost_estimate=pl.CostEstimate(
            flops=count * n * n * 2 * 1536 * 128, bytes_accessed=count * n * n * 1300, transcendentals=0
        ),
        name="skip_sums",
    )(x, rim.reshape(tiles, 4, n, c), w.reshape(9, 2 * c, c))


def dec_kernel(ready, coarse_rims, aliased, *refs):
    refs = list(refs)
    if ready:
        pre_ref = refs.pop(0)
    else:
        x_ref, rim_ref = refs.pop(0), refs.pop(0)
    u_ref = refs.pop(0)
    urim_ref = refs.pop(0) if coarse_rims else None
    raw_ref = refs.pop(0)
    if aliased:
        refs = refs[2:]
    y_ref, sums_ref, pairs, rows, colbuf, acc_ref, w_ref, wu_ref = refs
    group, n = y_ref.shape[0], y_ref.shape[3]
    half = n // 2
    hp = rows.shape[1]

    @pl.when(pl.program_id(0) == 0)
    def _():
        if not ready:
            fill_pair_weights(raw_ref, 128, w_ref)
        fill_coarse_weights(raw_ref, wu_ref)

    for g in range(group):
        u = u_ref[g].astype(F32)
        if urim_ref is not None:
            u = with_rims(u, [urim_ref[g, e].astype(F32) for e in range(4)], half, colbuf.at[0 : half * 8])
        fill_rows(rows, u, half)
        if not ready:
            x = with_rims(x_ref[g].astype(F32), [rim_ref[g, e].astype(F32) for e in range(4)], n, colbuf)
            fill_pairs(pairs, x, n)
        for q0, m in pair_chunks(n, DEC_PAIRS.get(n, 6)):
            for b in range(2):
                acc = None
                for k in range(3):
                    lhs = rows[q0 + k : q0 + k + m, :, b * 128 : b * 128 + 256].reshape(m * hp, 256)
                    part = jnp.dot(lhs, wu_ref[b, k], preferred_element_type=F32)
                    acc = part if acc is None else acc + part
                acc = acc.reshape(m, hp, 256)
                for i in range(m):
                    for p in range(2):
                        acc_ref[p, i, pl.ds(b, half, 2), :] = acc[i, 0:half, p * 128 : p * 128 + 128]
            extra = jnp.concatenate([acc_ref[0], acc_ref[1]], axis=2)
            if ready:
                acc = pre_ref[g, q0 : q0 + m] + extra
            else:
                acc = pair_sums(pairs, w_ref, q0, m, extra)
            put_sums(acc, sums_ref, g, q0, m, n, colbuf)
            out = silu(acc).astype(BF)[:, 0:n]
            y_ref[g, q0 : q0 + m, 0] = out[:, :, 0:128]
            y_ref[g, q0 : q0 + m, 1] = out[:, :, 128:256]


def last_kernel(pick_ref, recv_ref, own_ref, sum_ref, x_ref, y_ref, *scratch):
    rim_ref, edge_buf, slab_ref, colbuf, in_sem, out_sem, row_sem = scratch
    del x_ref
    strips, n = own_ref.shape[0], own_ref.shape[1]
    tiles = strips // 4
    parts = in_sem.shape[1]
    span = tiles // parts

    def slab(side, part):
        return y_ref.at[pl.ds(part * span, span), :, pl.ds(side * (n - 16), 16), :]

    def held(side, part):
        return slab_ref.at[side, pl.ds(part * span, span)]

    reads = [
        [pltpu.make_async_copy(slab(side, p), held(side, p), in_sem.at[side, p]) for p in range(parts)]
        for side in range(2)
    ]
    for p in range(parts):
        for side in range(2):
            reads[side][p].start()

    end = n - 1

    def finish(t, k):
        con = [incoming(pick_ref, recv_ref, own_ref, t * 4 + e) for e in range(4)]
        for e in range(4):
            edge_buf[k, e] = sum_ref[t * 4 + e] + con[e]
        for e, cell, other, at in corners(end):
            cells = slice(cell, cell + 1)
            edge_buf[k, e, cells] = edge_buf[k, e, cells] + con[other][at : at + 1]
        for e in range(4):
            rim_ref[t, e] = silu(edge_buf[k, e]).astype(BF)

    each_tile(tiles, finish)

    rows = [
        pltpu.make_async_copy(
            rim_ref.at[:, e, pl.ds(16, n - 32), :], y_ref.at[:, row, pl.ds(16, n - 32), :], row_sem.at[j]
        )
        for j, (e, row) in enumerate(((0, 0), (2, n - 1)))
    ]
    for copy in rows:
        copy.start()

    sub = lax.broadcasted_iota(jnp.int32, (n, 8, 128), 1)

    def patch(side, t):
        lo = 0 if side == 0 else n - 16
        near = slice(0, 8) if side == 0 else slice(8, 16)
        far = slice(8, 16) if side == 0 else slice(0, 8)
        x = slab_ref[side, t].astype(F32)
        cells = spread_columns(rim_ref[t, 3 if side == 0 else 1].astype(F32), n, 0 if side == 0 else 7, colbuf)
        new = jnp.where(sub == (0 if side == 0 else 7), cells, x[:, near])
        both = [new, x[:, far]] if side == 0 else [x[:, far], new]
        slab_ref[side, t] = jnp.concatenate(both, axis=1).astype(BF)
        slab_ref[side, t, 0] = rim_ref[t, 0, lo : lo + 16]
        slab_ref[side, t, n - 1] = rim_ref[t, 2, lo : lo + 16]

    writes = []
    for p in range(parts):
        for side in range(2):
            reads[side][p].wait()

            def step(t, carry, side=side):
                patch(side, t)
                return carry

            lax.fori_loop(p * span, p * span + span, step, 0)
            copy = pltpu.make_async_copy(held(side, p), slab(side, p), out_sem.at[side, p])
            copy.start()
            writes.append(copy)
    for copy in writes + rows:
        copy.wait()


def last_step(x, plan, recv, own, sums):
    tiles, n, _, c = x.shape
    strips = own.shape[0]
    parts = 4 if tiles % 4 == 0 else 1
    smem = pl.BlockSpec(memory_space=pltpu.SMEM)
    vmem = pl.BlockSpec(memory_space=pltpu.VMEM)
    anywhere = pl.BlockSpec(memory_space=pl.ANY)
    return pl.pallas_call(
        last_kernel,
        in_specs=[smem, vmem, vmem, vmem, anywhere],
        out_specs=anywhere,
        out_shape=jax.ShapeDtypeStruct(x.shape, BF),
        scratch_shapes=[
            pltpu.VMEM((tiles, 4, n, c), BF),
            pltpu.VMEM((group_of(tiles, 3), 4, n, c), F32),
            pltpu.VMEM((2, tiles, n, 16, c), BF),
            pltpu.VMEM((n * 8, c), F32),
            pltpu.SemaphoreType.DMA((2, parts)),
            pltpu.SemaphoreType.DMA((2, parts)),
            pltpu.SemaphoreType.DMA((2,)),
        ],
        input_output_aliases={4: 0},
        compiler_params=params(),
        name="last_step",
    )(plan[0], recv, own, sums, x)


def group_of(tiles, want):
    return max(g for g in range(1, want + 1) if tiles % g == 0)


def tile_spec(group, *dims):
    return pl.BlockSpec((group,) + dims, lambda i: (i,) + (0,) * len(dims))


def whole_spec(shape):
    return pl.BlockSpec(shape, lambda i: (0,) * len(shape))


def enc_conv(x, rim, w, want):
    tiles, n, _, c = x.shape
    half, n_p = n // 2, up16(n)
    g = group_of(tiles, want)
    m = pair_chunks(n, ENC_PAIRS.get(n, 6))[0][1]
    args, specs = [x, w.reshape(9, c, c)], [tile_spec(g, n, n, c), whole_spec((9, c, c))]
    if rim is not None:
        args.append(rim.reshape(tiles, 4, n, c))
        specs.append(tile_spec(g, 4, n, c))
    y, sums, ring, s = pl.pallas_call(
        enc_kernel,
        grid=(tiles // g,),
        in_specs=specs,
        out_specs=[
            tile_spec(g, half, 2, n, c), tile_spec(g, 4, n, c), tile_spec(g, 4, n, c), tile_spec(g, half, half, c)
        ],
        out_shape=[
            jax.ShapeDtypeStruct((tiles, half, 2, n, c), BF),
            jax.ShapeDtypeStruct((tiles, 4, n, c), F32),
            jax.ShapeDtypeStruct((tiles, 4, n, c), BF),
            jax.ShapeDtypeStruct((tiles, half, half, c), BF),
        ],
        scratch_shapes=[
            pltpu.VMEM((half + 1, n_p, 768), BF),
            pltpu.VMEM((n * 8, 128), F32),
            pltpu.VMEM((m * n, 128), F32),
            pltpu.VMEM((2, n, 128), F32),
            pltpu.VMEM((1536, 256), BF),
        ],
        compiler_params=params(),
        cost_estimate=pl.CostEstimate(
            flops=tiles * n * n * 2 * 1536 * 128, bytes_accessed=tiles * n * n * 600, transcendentals=tiles * n * n * 128
        ),
        name="enc_conv",
    )(*args)
    strips = lambda a: a.reshape(tiles * 4, n, c)
    return y.reshape(tiles, n, n, c), strips(sums), strips(ring), s


def dec_conv(x, rim, u, urim, w, want, pre=None, first=0, last=None, base=None):
    tiles, n, _, c = x.shape
    last = tiles if last is None else last
    half, n_p, h_p = n // 2, up16(n), up16(n // 2)
    g = group_of(last - first, want)
    m = pair_chunks(n, DEC_PAIRS.get(n, 6))[0][1]
    at = first // g
    spec = lambda *dims: pl.BlockSpec((g,) + dims, lambda i: (at + i,) + (0,) * len(dims))
    if pre is None:
        args, specs = [x, rim.reshape(tiles, 4, n, c)], [spec(n, n, c), spec(4, n, c)]
    else:
        args, specs = [pre], [tile_spec(g, half, n_p, 2 * c)]
    args, specs = args + [u], specs + [spec(half, half, c)]
    if urim is not None:
        args.append(urim.reshape(tiles, 4, half, c))
        specs.append(spec(4, half, c))
    args.append(w.reshape(9, 2 * c, c))
    specs.append(whole_spec((9, 2 * c, c)))
    aliases = {}
    if base is not None:
        aliases = {len(args): 0, len(args) + 1: 1}
        args += list(base)
        specs += [pl.BlockSpec(memory_space=pl.ANY)] * 2

    def kernel(*refs):
        dec_kernel(pre is not None, urim is not None, base is not None, *refs)

    count = last - first
    y, sums = pl.pallas_call(
        kernel,
        grid=(count // g,),
        in_specs=specs,
        out_specs=[spec(half, 2, n, c), spec(4, n, c)],
        out_shape=[
            jax.ShapeDtypeStruct((tiles, half, 2, n, c), BF),
            jax.ShapeDtypeStruct((tiles, 4, n, c), F32),
        ],
        scratch_shapes=[
            pltpu.VMEM((half + 1, n_p, 768), BF),
            pltpu.VMEM((half + 2, h_p, 384), BF),
            pltpu.VMEM((n * 8, 128), F32),
            pltpu.VMEM((2, m, n_p, 128), F32),
            pltpu.VMEM((1536, 256), BF),
            pltpu.VMEM((2, 3, 256, 256), BF),
        ],
        input_output_aliases=aliases,
        compiler_params=params(),
        cost_estimate=pl.CostEstimate(
            flops=count * n * n * 2 * 2300 * 128, bytes_accessed=count * n * n * 600, transcendentals=count * n * n * 128
        ),
        name="dec_conv",
    )(*args)
    return y, sums


def strips_of(field, ring=0):
    n = field.shape[1]
    far = n - 1 - ring
    out = jnp.stack([field[:, ring], field[:, :, far], field[:, far], field[:, :, ring]], axis=1)
    out = jnp.pad(out, ((0, 0), (0, 0), (0, strip_rows(n) - n), (0, 0)))
    return out.reshape(field.shape[0] * 4, strip_rows(n), field.shape[3])


def patched(field, rim):
    tiles, n, _, c = field.shape
    rim = rim.reshape(tiles, 4, -1, c)[:, :, :n]
    middle = jnp.concatenate(
        [rim[:, 3, 1 : n - 1, None], field[:, 1 : n - 1, 1 : n - 1], rim[:, 1, 1 : n - 1, None]], axis=2
    )
    return jnp.concatenate([rim[:, 0][:, None], middle, rim[:, 2][:, None]], axis=1)


def inner_sums(field, weight):
    return lax.conv_general_dilated(
        field,
        weight,
        (1, 1),
        ((1, 1), (1, 1)),
        dimension_numbers=("NHWC", "HWIO", "NHWC"),
        preferred_element_type=F32,
    )


def shrink(field):
    count, length, _, channels = field.shape
    blocks = field.astype(F32).reshape(count, length // 2, 2, length // 2, 2, channels)
    return (jnp.sum(blocks, axis=(2, 4)) * 0.25).astype(BF)


def enlarge(field):
    return jnp.repeat(jnp.repeat(field, 2, axis=1), 2, axis=2)


def per_device(features, edge_table, w_enc0, w_enc1, w_enc2, w_mid, w_dec2, w_dec1, w_dec0):
    tiles, n0 = features.shape[0], features.shape[1]
    devices = lax.axis_size("tile")
    position = lax.axis_index("tile")
    cap = pair_capacity(FACE_TILES, tiles)
    rows = devices * cap
    slot_row = send_slots(edge_table, position, tiles, cap)

    def trade(strips):
        length = strips.shape[1]
        out = lax.all_to_all(
            strips.reshape(devices, cap * length, 128), "tile", split_axis=0, concat_axis=0, tiled=True
        )
        return out.reshape(rows, length, 128)

    def after(value, token):
        return lax.optimization_barrier((value, token))[0]

    cuts = [0] + [tiles * share // 24 for share in EARLY_TILES] + [tiles]
    early_tiles = list(zip(cuts[:-1], cuts[1:]))

    def ahead(value, token, part):
        first, last = early_tiles[part]
        if last == first:
            return value, None
        return lax.optimization_barrier((value, skip_sums(enc0, after(enc0_rim, token), w_dec0, first, last - first)))

    rim0, send = tile_rims(features, slot_row, rows)
    rim0 = rim0.reshape(tiles * 4, n0, 128)
    plan = receive_plan(after(edge_table, send), slot_row, position, tiles, cap, devices)
    recv = trade(send)
    enc0, sums, ring, x1 = enc_conv(features, None, w_enc0, 1)
    enc0_rim, x1_rim, send = rim_step(n0, plan, recv, rim0, sums, w=w_enc0, ring=ring)

    recv = trade(send)
    enc1, sums, ring, x2 = enc_conv(x1, x1_rim, w_enc1, 4)
    enc1_rim, x2_rim, send = rim_step(n0 // 2, plan, recv, x1_rim, sums, w=w_enc1, ring=ring)

    recv = trade(send)
    sums = inner_sums(patched(x2, x2_rim), w_enc2)
    sums, early3 = ahead(sums, x2_rim, 0)
    enc2 = jax.nn.silu(sums).astype(BF)
    enc2_rim, x3_rim, send = rim_step(
        n0 // 4, plan, recv, x2_rim, strips_of(sums), w=w_enc2, ring=strips_of(enc2, 1)
    )

    recv = trade(send)
    sums = inner_sums(patched(shrink(enc2), x3_rim), w_mid)
    middle = jax.nn.silu(sums).astype(BF)
    sums, early4 = ahead(sums, x3_rim, 1)
    skip2 = skip_step(n0 // 4, plan, enc2_rim, w_dec2)
    skip0 = skip_step(n0, plan, after(enc0_rim, x3_rim), w_dec0)
    mid_rim, own, send = rim_step(
        n0 // 8, plan, recv, x3_rim, strips_of(sums), w=w_mid,
        skip=skip2, wn=w_dec2,
    )

    recv = trade(send)
    joined = jnp.concatenate([enlarge(patched(middle, mid_rim)), patched(enc2, enc2_rim)], axis=3)
    sums = inner_sums(joined, w_dec2)
    dec2 = jax.nn.silu(sums).astype(BF)
    sums, early5 = ahead(sums, mid_rim, 2)
    skip1 = skip_step(n0 // 2, plan, after(enc1_rim, mid_rim), w_dec1)
    dec2_rim, own, send = rim_step(
        n0 // 4, plan, recv, own, strips_of(sums), skip=skip1, wn=w_dec1
    )

    recv = trade(send)
    dec1, sums = dec_conv(enc1, enc1_rim, patched(dec2, dec2_rim), None, w_dec1, 4)
    dec1, sums = dec1.reshape(enc1.shape), sums.reshape(x1_rim.shape)
    dec1_rim, own, send = rim_step(
        n0 // 2, plan, recv, own, sums, skip=skip0, wn=w_dec0
    )

    recv = trade(send)
    base = None
    for (first, last), pre in zip(early_tiles, (early3, early4, early5, None)):
        if last > first:
            base = dec_conv(enc0, enc0_rim, dec1, dec1_rim, w_dec0, 1, pre, first, last, base)
    dec0, sums = base
    return last_step(dec0.reshape(enc0.shape), plan, recv, own, sums.reshape(rim0.shape))


def solution(mesh):
    return jax.shard_map(
        per_device,
        mesh=mesh,
        in_specs=(P(("grp", "tile"), None, None, None), P(), P(), P(), P(), P(), P(), P(), P()),
        out_specs=P(("grp", "tile"), None, None, None),
        check_vma=False,
    )
```

```python
import jax
import jax.numpy as jnp
import numpy as np
from jax import lax
from jax.experimental import pallas as pl
from jax.experimental.pallas import tpu as pltpu
from jax.sharding import PartitionSpec as P

FACE_TILES = 8
VMEM_LIMIT = 50 * 2**20
BF = jnp.bfloat16
F32 = jnp.float32


def cube_links(tiles_side):
    basis = np.eye(3, dtype=np.int64)
    frames = []
    for axis_id in range(3):
        for orient in (1, -1):
            frames.append(
                (orient * basis[axis_id], basis[(axis_id + 1) % 3], basis[(axis_id + 2) % 3])
            )
    per_face = tiles_side * tiles_side
    tile_total = 6 * per_face
    centres = np.zeros((tile_total, 3), np.int64)
    lookup = {}
    for face_id in range(6):
        normal, row_axis, col_axis = frames[face_id]
        for row_id in range(tiles_side):
            for col_id in range(tiles_side):
                slot_id = face_id * per_face + row_id * tiles_side + col_id
                centre = (
                    tiles_side * normal
                    + (2 * row_id + 1 - tiles_side) * row_axis
                    + (2 * col_id + 1 - tiles_side) * col_axis
                )
                centres[slot_id] = centre
                lookup[tuple((int(entry) for entry in centre))] = slot_id
    partner = np.zeros((tile_total, 4), np.int64)
    for slot_id in range(tile_total):
        normal, row_axis, col_axis = frames[slot_id // per_face]
        outward = (-row_axis, col_axis, row_axis, -col_axis)
        for edge_id in range(4):
            beyond = tuple((int(entry) for entry in centres[slot_id] + 2 * outward[edge_id]))
            if beyond in lookup:
                partner[slot_id, edge_id] = lookup[beyond]
            else:
                partner[slot_id, edge_id] = lookup[
                    tuple((int(entry) for entry in centres[slot_id] + outward[edge_id] - normal))
                ]
    return partner


def pair_capacity(tiles_side, tiles_here):
    partner = cube_links(tiles_side)
    tile_total = partner.shape[0]
    blocks = tile_total // tiles_here
    source = np.repeat(np.arange(tile_total) // tiles_here, 4)
    target = partner.reshape(-1) // tiles_here
    identity = np.eye(blocks, dtype=np.int64)
    shared = identity[source].T @ identity[target]
    shared = shared * (1 - identity)
    return max(int(shared.max()), 1)


def own_strips(edge_table, position, tiles_here):
    rows = lax.dynamic_slice_in_dim(edge_table, position * tiles_here, tiles_here, 0)
    rows = rows.reshape(tiles_here * 4, 2)
    return rows[:, 0], rows[:, 1] // 2, rows[:, 1] % 2


def send_slots(edge_table, position, tiles_here, slot_count):
    partner, _, _ = own_strips(edge_table, position, tiles_here)
    target = partner // tiles_here
    order = jnp.arange(tiles_here * 4, dtype=jnp.int32)
    earlier = (order[None, :] < order[:, None]) & (target[None, :] == target[:, None])
    slot_rank = jnp.sum(earlier.astype(jnp.int32), axis=1)
    return jnp.where(target != position, target * slot_count + slot_rank, -1)


def listed(mask):
    order = jnp.arange(mask.shape[0], dtype=jnp.int32)
    rank = jnp.sum((mask[None, :] & (order[None, :] < order[:, None])).astype(jnp.int32), axis=1)
    hit = mask[None, :] & (rank[None, :] == order[:, None])
    found = jnp.sum(jnp.where(hit, order[None, :], 0), axis=1)
    total = jnp.sum(mask.astype(jnp.int32), keepdims=True)
    found = jnp.where(order < total, found, mask.shape[0])
    return jnp.concatenate([found, jnp.full((3,), mask.shape[0], jnp.int32), total])


def receive_plan(edge_table, slot_row, position, tiles_here, slot_count, devices):
    strip_count = tiles_here * 4
    partner, matching, reversed_rows = own_strips(edge_table, position, tiles_here)
    target = partner // tiles_here
    order = jnp.arange(strip_count, dtype=jnp.int32)
    remote = target != position
    wanted = partner % tiles_here * 4 + matching
    toward_me = edge_table[:, :, 0].reshape(devices, strip_count) // tiles_here == position
    before = (order[:, None] < order[None, :]).astype(BF)
    ranks = jnp.dot(toward_me.astype(BF), before, preferred_element_type=F32).astype(BF)
    blocks = jnp.arange(devices, dtype=jnp.int32)
    from_target = (target[:, None] == blocks[None, :]).astype(BF)
    their_ranks = jnp.dot(from_target, ranks, preferred_element_type=F32)
    recv_rank = jnp.sum(jnp.where(wanted[:, None] == order[None, :], their_ranks, 0.0), axis=1).astype(jnp.int32)
    pick_row = jnp.where(remote, target * slot_count + recv_rank, devices * slot_count + wanted)
    odd = (matching != (order + 2) % 4) | (reversed_rows == 1)
    one_more = lambda a: jnp.concatenate([a, jnp.zeros((1,), jnp.int32)])
    return (pick_row, one_more(reversed_rows), slot_row, one_more(matching), listed(remote), listed(odd))


def up16(n):
    return (n + 15) // 16 * 16


def strip_rows(n):
    return {6: 8, 12: 16}.get(n, n)


def params():
    return pltpu.CompilerParams(vmem_limit_bytes=VMEM_LIMIT)


def rims_kernel(slot_ref, lo_ref, hi_ref, top_ref, bottom_ref, out_ref, send_ref, colbuf):
    group, n = lo_ref.shape[0], lo_ref.shape[1]
    first = pl.program_id(0) * group * 4
    for g in range(group):
        colbuf[...] = lo_ref[g, :, 0:8, :].astype(F32).reshape(n * 8, 128)
        left = colbuf[pl.ds(0, n, 8), :]
        colbuf[...] = hi_ref[g, :, 8:16, :].astype(F32).reshape(n * 8, 128)
        right = colbuf[pl.ds(7, n, 8), :]
        out_ref[g, 0] = top_ref[g, 0]
        out_ref[g, 1] = right.astype(BF)
        out_ref[g, 2] = bottom_ref[g, 0]
        out_ref[g, 3] = left.astype(BF)
    for g in range(group):
        for e in range(4):
            slot = slot_ref[first + g * 4 + e]

            @pl.when(slot >= 0)
            def _():
                send_ref[slot] = out_ref[g, e]


def tile_rims(x, slot_row, rows):
    tiles, n, _, c = x.shape
    g = group_of(tiles, 4)
    last = n // 16 - 1
    return pl.pallas_call(
        rims_kernel,
        grid=(tiles // g,),
        in_specs=[
            pl.BlockSpec(memory_space=pltpu.SMEM),
            pl.BlockSpec((g, n, 16, c), lambda i: (i, 0, 0, 0)),
            pl.BlockSpec((g, n, 16, c), lambda i: (i, 0, last, 0)),
            pl.BlockSpec((g, 1, n, c), lambda i: (i, 0, 0, 0)),
            pl.BlockSpec((g, 1, n, c), lambda i: (i, n - 1, 0, 0)),
        ],
        out_specs=[tile_spec(g, 4, n, c), whole_spec((rows, n, c))],
        out_shape=[
            jax.ShapeDtypeStruct((tiles, 4, n, c), BF),
            jax.ShapeDtypeStruct((rows, n, c), BF),
        ],
        scratch_shapes=[pltpu.VMEM((n * 8, 128), F32)],
        compiler_params=params(),
        name="tile_rims",
    )(slot_row, x, x, x, x)


def silu(s):
    half = s * 0.5
    return half + half * jnp.tanh(half)


def strip_shifts(h, n):
    rows = h.shape[0]
    row = lax.broadcasted_iota(jnp.int32, h.shape, 0)
    half = h * 0.5
    down = jnp.where(row == 0, half, pltpu.roll(h, 1, 0))
    up = jnp.where(row == n - 1, half, pltpu.roll(h, rows - 1, 0))
    return down, up


def flip_matrices(rows, n):
    ri = lax.broadcasted_iota(jnp.int32, (rows, rows), 0)
    ci = lax.broadcasted_iota(jnp.int32, (rows, rows), 1)
    return (ri + ci == n - 1).astype(F32), (ri == ci).astype(F32)


def put_shifts(ref, index, lane, h, n):
    down, up = strip_shifts(h, n)
    for s, part in enumerate((down, h, up)):
        ref[index + (slice(None), slice(lane + s * 128, lane + s * 128 + 128))] = part.astype(ref.dtype)


def each_tile(tiles, body):
    side = group_of(tiles, 3)

    def step(i, carry):
        for k in range(side):
            body(i * side + k, k)
        return carry

    lax.fori_loop(0, tiles // side, step, 0)


def each_listed(list_ref, body):
    def step(j, carry):
        body(list_ref[j])
        return carry

    lax.fori_loop(0, list_ref[list_ref.shape[0] - 1], step, 0)


def each_four(list_ref, body):
    def step(j, carry):
        body([list_ref[j * 4 + k] for k in range(4)])
        return carry

    lax.fori_loop(0, (list_ref[list_ref.shape[0] - 1] + 3) // 4, step, 0)


def turned(rev_ref, i, h, flip, keep):
    order = jnp.where(rev_ref[i] == 1, flip, keep).astype(BF)
    return jnp.dot(order, h.astype(BF), preferred_element_type=F32)


def incoming(pick_ref, recv_ref, own_ref, i):
    rows = recv_ref.shape[0]
    pick = pick_ref[i]
    a = recv_ref[jnp.minimum(pick, rows - 1)].astype(F32)
    b = own_ref[jnp.maximum(pick - rows, 0)].astype(F32)
    return jnp.where(pick < rows, a, b)


def edge_taps(w_ref, e, lo):
    taps = ((0, 1, 2), (2, 5, 8), (6, 7, 8), (0, 3, 6))[e]
    return jnp.concatenate([w_ref[tap, lo : lo + 128, :] for tap in taps], axis=0)


def contributions(n, tiles, strip_of, w_ref, lo, rev_ref, edge_ref, odd_ref, lhs_ref, con_ref, taps_ref):
    lp = lhs_ref.shape[2]
    for e in range(4):
        taps_ref[e] = edge_taps(w_ref, e, lo)

    def fill(t, k):
        for f in range(4):
            put_shifts(lhs_ref, (f, t), 0, strip_of(f, t, k), n)

    each_tile(tiles, fill)
    for f in range(4):
        lhs = lhs_ref[f, 0:tiles].reshape(tiles * lp, 384).astype(BF)
        out = jnp.dot(lhs, taps_ref[(f + 2) % 4], preferred_element_type=F32)
        con_ref[f, 0:tiles] = out.reshape(tiles, lp, 128)
    flip, keep = flip_matrices(lp, n)

    def odd_ones(four):
        halos = [lhs_ref[i % 4, i // 4, :, 128:256] for i in four]
        halos = [turned(rev_ref, i, h, flip, keep) for i, h in zip(four, halos)]
        taps = [taps_ref[edge_ref[i]] for i in four]
        sums = []
        for h, tap in zip(halos, taps):
            down, up = strip_shifts(h, n)
            lhs = jnp.concatenate([down.astype(BF), h.astype(BF), up.astype(BF)], axis=1)
            sums.append(jnp.dot(lhs, tap, preferred_element_type=F32))
        for i, total in zip(four, sums):
            con_ref[i % 4, i // 4] = total

    each_four(odd_ref, odd_ones)


def skip_kernel(n, rev_ref, edge_ref, odd_ref, rim_ref, w_ref, out_ref, lhs_ref, con_ref, taps_ref):
    tiles = rim_ref.shape[0] // 4
    contributions(
        n, tiles, lambda f, t, k: rim_ref[t * 4 + f].astype(F32), w_ref, 128,
        rev_ref, edge_ref, odd_ref, lhs_ref, con_ref, taps_ref,
    )

    def put(t, k):
        for f in range(4):
            out_ref[t * 4 + f] = con_ref[f, t]

    each_tile(tiles, put)


def wide(rows):
    return BF if rows % 16 == 0 else F32


def skip_step(n, plan, rim, w):
    strips, lp, c = rim.shape
    smem = pl.BlockSpec(memory_space=pltpu.SMEM)
    vmem = pl.BlockSpec(memory_space=pltpu.VMEM)
    return pl.pallas_call(
        lambda *refs: skip_kernel(n, *refs),
        in_specs=[smem, smem, smem, vmem, vmem],
        out_specs=vmem,
        out_shape=jax.ShapeDtypeStruct((strips, lp, c), F32),
        scratch_shapes=[
            pltpu.VMEM((4, strips // 4 + 1, lp, 384), wide(lp)),
            pltpu.VMEM((4, strips // 4 + 1, lp, 128), F32),
            pltpu.VMEM((4, 384, 128), BF),
        ],
        compiler_params=params(),
        cost_estimate=pl.CostEstimate(flops=strips * lp * 2 * 384 * 256, bytes_accessed=strips * lp * 768, transcendentals=0),
        name="skip_step",
    )(plan[1], plan[3], plan[5], rim, w.reshape(9, -1, c))


def corners(end):
    return (
        (0, 0, 3, 0), (0, end, 1, 0), (2, 0, 3, end), (2, end, 1, end),
        (3, 0, 0, 0), (3, end, 2, 0), (1, 0, 0, end), (1, end, 2, end),
    )


def rim_kernel(n, strips_in, nxt, refs):
    it = iter(refs)
    pick_ref, rev_ref, slot_ref, edge_ref, remote_ref, odd_ref = [next(it) for _ in range(6)]
    recv_ref, own_ref, sum_ref = next(it), next(it), next(it)
    w_ref = next(it) if strips_in else None
    ring_ref = next(it) if nxt == "shrink" else None
    skip_ref, wn_ref = (next(it), next(it)) if nxt == "halo" else (None, None)
    rim_ref, next_ref, send_ref = next(it), next(it), next(it)
    halo_ref, lhs_ref, con_ref = next(it), next(it), next(it)
    edge_buf, ring_buf, sum_buf, out_buf = next(it), next(it), next(it), next(it)
    lhsn_ref, conn_ref, taps_ref, big_buf = [next(it) for _ in range(4)] if nxt == "halo" else [None] * 4

    lp = recv_ref.shape[1]
    strips = own_ref.shape[0]
    tiles = strips // 4
    flip, keep = flip_matrices(lp, n)

    if strips_in:

        def fetch(t, k):
            for e in range(4):
                i = t * 4 + e
                halo_ref[i] = incoming(pick_ref, recv_ref, own_ref, i).astype(BF)

        each_tile(tiles, fetch)

        def turn(four):
            halos = [turned(rev_ref, i, halo_ref[i], flip, keep).astype(BF) for i in four]
            for i, h in zip(four, halos):
                halo_ref[i] = h

        each_four(odd_ref, turn)

        def fill(t, k):
            for e in range(4):
                put_shifts(lhs_ref, (e, t), 0, halo_ref[t * 4 + e].astype(F32), n)

        each_tile(tiles, fill)
        for e in range(4):
            lhs = lhs_ref[e].reshape(tiles * lp, 384).astype(BF)
            out = jnp.dot(lhs, edge_taps(w_ref, e, 0), preferred_element_type=F32)
            con_ref[e] = out.reshape(tiles, lp, 128)
    else:

        def fill(t, k):
            for e in range(4):
                con_ref[e, t] = incoming(pick_ref, recv_ref, own_ref, t * 4 + e)

        each_tile(tiles, fill)

    end = n - 1
    joints = (
        (0, 0, 3, 1), (0, end, 1, 1), (2, 0, 3, end - 1), (2, end, 1, end - 1),
        (3, 0, 0, 1), (3, end, 2, 1), (1, 0, 0, end - 1), (1, end, 2, end - 1),
    )
    if nxt == "shrink":
        out_buf[...] = jnp.zeros_like(out_buf)

    def finish(t, k):
        for e in range(4):
            edge_buf[k, e] = sum_ref[t * 4 + e] + con_ref[e, t]
        for e, cell, other, at in corners(end):
            cells = slice(cell, cell + 1)
            edge_buf[k, e, cells] = edge_buf[k, e, cells] + con_ref[other, t, at : at + 1]
        for e in range(4):
            y = silu(edge_buf[k, e]).astype(BF)
            rim_ref[t * 4 + e] = y
            edge_buf[k, e] = y.astype(F32)
        if nxt == "shrink":
            for e in range(4):
                ring_buf[k, e] = ring_ref[t * 4 + e].astype(F32)
            for e, cell, other, at in joints:
                ring_buf[k, e, cell : cell + 1] = edge_buf[k, other, at : at + 1]
            for e in range(4):
                sum_buf[k, e] = edge_buf[k, e] + ring_buf[k, e]
                small = sum_buf[k, e, pl.ds(0, lp // 2, 2), :] + sum_buf[k, e, pl.ds(1, lp // 2, 2), :]
                out_buf[k, e, 0 : lp // 2] = small * 0.25
                next_ref[t * 4 + e] = out_buf[k, e].astype(BF)

    each_tile(tiles, finish)

    if nxt == "halo":
        half = big_buf.shape[2] // 2

        def enlarged(f, t, k):
            rim = rim_ref[t * 4 + f].astype(F32)[0:half]
            big_buf[k, f, pl.ds(0, half, 2), :] = rim
            big_buf[k, f, pl.ds(1, half, 2), :] = rim
            return big_buf[k, f]

        contributions(
            2 * n, tiles, enlarged, wn_ref, 0,
            rev_ref, edge_ref, odd_ref, lhsn_ref, conn_ref, taps_ref,
        )

        def put(t, k):
            for f in range(4):
                next_ref[t * 4 + f] = (conn_ref[f, t] + skip_ref[t * 4 + f]).astype(BF)

        each_tile(tiles, put)

    def send(i):
        send_ref[slot_ref[i]] = next_ref[i]

    each_listed(remote_ref, send)


def rim_step(n, plan, recv, own, sums, w=None, ring=None, skip=None, wn=None):
    rows, lp, c = recv.shape
    strips = own.shape[0]
    tiles = strips // 4
    side = group_of(tiles, 3)
    nxt = "shrink" if ring is not None else "halo"
    smem = pl.BlockSpec(memory_space=pltpu.SMEM)
    vmem = pl.BlockSpec(memory_space=pltpu.VMEM)
    w = w if w is None else w.reshape(9, -1, c)
    wn = wn if wn is None else wn.reshape(9, -1, c)
    args = [recv, own, sums] + [a for a in (w, ring, skip, wn) if a is not None]
    lo = strip_rows(n // 2) if nxt == "shrink" else strip_rows(2 * n)
    outs = [
        jax.ShapeDtypeStruct((strips, lp, c), BF),
        jax.ShapeDtypeStruct((strips, lo, c), BF),
        jax.ShapeDtypeStruct((rows, lo, c), BF),
    ]
    scratch = [
        pltpu.VMEM((strips + 1, lp, 128), BF),
        pltpu.VMEM((4, tiles, lp, 384), wide(lp)),
        pltpu.VMEM((4, tiles, lp, 128), F32),
        pltpu.VMEM((side, 4, lp, 128), F32),
        pltpu.VMEM((side, 4, lp, 128), F32),
        pltpu.VMEM((side, 4, lp, 128), F32),
        pltpu.VMEM((side, 4, lo, 128), F32),
    ]
    if nxt == "halo":
        scratch += [
            pltpu.VMEM((4, tiles + 1, lo, 384), wide(lo)),
            pltpu.VMEM((4, tiles + 1, lo, 128), F32),
            pltpu.VMEM((4, 384, 128), BF),
            pltpu.VMEM((side, 4, lo, 128), F32),
        ]

    def kernel(*refs):
        rim_kernel(n, w is not None, nxt, refs)

    return pl.pallas_call(
        kernel,
        in_specs=[smem] * 6 + [vmem] * len(args),
        out_specs=[vmem] * len(outs),
        out_shape=outs,
        scratch_shapes=scratch,
        compiler_params=params(),
        cost_estimate=pl.CostEstimate(flops=strips * lp * 2 * 384 * 512, bytes_accessed=strips * lp * 1500, transcendentals=0),
        name="rim_step",
    )(*plan, *args)


def spread_columns(strip, n, sublane, buf):
    buf[pl.ds(sublane, n, 8), :] = strip
    return buf[...].reshape(n, 8, 128)


def with_rims(x, rim, n, buf):
    sub = lax.broadcasted_iota(jnp.int32, (n, 8, 128), 1)
    head = jnp.where(sub == 0, spread_columns(rim[3], n, 0, buf), x[:, 0:8])
    tail = jnp.where(sub == 7, spread_columns(rim[1], n, 7, buf), x[:, n - 8 : n])
    x = jnp.concatenate([head, x[:, 8 : n - 8], tail], axis=1)
    return jnp.concatenate([rim[0][None], x[1 : n - 1], rim[2][None]], axis=0)


def column_shifts(x, n):
    sub = lax.broadcasted_iota(jnp.int32, (x.shape[0], 8, 128), 1)
    down = pltpu.roll(x, 1, 1)
    up = pltpu.roll(x, n - 1, 1)
    down = jnp.concatenate([jnp.where(sub == 0, 0.0, down[:, 0:8]), down[:, 8:n]], axis=1)
    up = jnp.concatenate([up[:, 0 : n - 8], jnp.where(sub == 7, 0.0, up[:, n - 8 : n])], axis=1)
    return down, x, up


def fill_pairs(y_ref, x, n):
    half, n_p = n // 2, y_ref.shape[1]
    zero = jnp.zeros((n_p, 384), BF)
    y_ref[0, :, 0:384] = zero
    y_ref[half, :, 384:768] = zero
    for s, body in enumerate(column_shifts(x, n)):
        b = body.astype(BF).reshape(half, 2, n, 128)
        y_ref[0:half, 0:n, 384 + s * 128 : 384 + s * 128 + 128] = b[:, 0]
        y_ref[1 : half + 1, 0:n, s * 128 : s * 128 + 128] = b[:, 1]


def in_pairs(n):
    return n % 16 == 8 and n % 2 == 0


def fill_row_pairs(u_ref, x, n):
    half = n // 2
    zero = jnp.zeros((n, 384), BF)
    u_ref[0, 0:n] = zero
    u_ref[half, n : 2 * n] = zero
    for s, body in enumerate(column_shifts(x, n)):
        b = body.astype(BF).reshape(half, 2, n, 128)
        lanes = slice(s * 128, s * 128 + 128)
        u_ref[0:half, n : 2 * n, lanes] = b[:, 0]
        u_ref[1 : half + 1, 0:n, lanes] = b[:, 1]
        u_ref[half + 1 : n + 1, 0:n, lanes] = b[:, 0]
        u_ref[half + 1 : n + 1, n : 2 * n, lanes] = b[:, 1]


def coarse_lhs(u_ref, n, start, m, lanes):
    if in_pairs(n):
        at = start // 2 if start % 2 == 0 else n // 2 + 1 + start // 2
        return u_ref[at : at + m // 2, :, lanes].reshape(m * n, 256), n
    return u_ref[start : start + m, :, lanes].reshape(m * u_ref.shape[1], 256), u_ref.shape[1]


def fill_rows(u_ref, x, n):
    zero = jnp.zeros((u_ref.shape[1], 384), BF)
    u_ref[0] = zero
    u_ref[n + 1] = zero
    for s, body in enumerate(column_shifts(x, n)):
        u_ref[1 : n + 1, 0:n, s * 128 : s * 128 + 128] = body.astype(BF)


def pair_sums(y_ref, w_ref, q0, m, extra):
    n_p = y_ref.shape[1]
    a = y_ref[q0 : q0 + m].reshape(m * n_p, 768)
    b = y_ref[q0 + 1 : q0 + 1 + m].reshape(m * n_p, 768)
    acc = jnp.dot(a, w_ref[0:768, :], preferred_element_type=F32)
    acc = acc + jnp.dot(b, w_ref[768:1536, :], preferred_element_type=F32)
    acc = acc.reshape(m, n_p, 256)
    return acc if extra is None else acc + extra


def pair_chunks(n, most):
    half = n // 2
    m = max(m for m in range(1, most + 1) if half % m == 0)
    return [(q, m) for q in range(0, half, m)]


ENC_PAIRS = {48: 24}
DEC_PAIRS = {48: 12}


def column_of(acc, m, lo, sublane, colbuf):
    rows = jnp.stack([acc[:, lo : lo + 8, 0:128], acc[:, lo : lo + 8, 128:256]], axis=1)
    colbuf[0 : 16 * m] = rows.reshape(16 * m, 128)
    return colbuf[pl.ds(sublane, 2 * m, 8), :]


def put_sums(acc, sums_ref, g, q0, m, n, colbuf):
    cells = slice(2 * q0, 2 * q0 + 2 * m)
    if q0 == 0:
        sums_ref[g, 0] = acc[0, 0:n, 0:128]
    if q0 + m == n // 2:
        sums_ref[g, 2] = acc[m - 1, 0:n, 128:256]
    sums_ref[g, 3, cells] = column_of(acc, m, 0, 0, colbuf)
    sums_ref[g, 1, cells] = column_of(acc, m, n - 8, 7, colbuf)


def fill_pair_weights(raw_ref, lo, w_ref):
    for p in range(4):
        for col in range(3):
            at = slice((p * 3 + col) * 128, (p * 3 + col) * 128 + 128)
            for out in range(2):
                row = p - out
                tap = raw_ref[row * 3 + col, lo : lo + 128, :] if 0 <= row <= 2 else jnp.zeros((128, 128), BF)
                w_ref[at, out * 128 : out * 128 + 128] = tap


def fill_coarse_weights(raw_ref, w_ref):
    along = (((0,), (1, 2), ()), ((), (0, 1), (2,)))
    for b in range(2):
        for k in range(3):
            for slot in range(2):
                cols = along[b][slot + b]
                for out in range(2):
                    taps = [raw_ref[r * 3 + col, 0:128, :].astype(F32) for r in along[out][k] for col in cols]
                    total = sum(taps[1:], taps[0]) if taps else jnp.zeros((128, 128), F32)
                    w_ref[b, k, slot * 128 : slot * 128 + 128, out * 128 : out * 128 + 128] = total.astype(BF)


def enc_kernel(*refs):
    it = iter(refs[:-5])
    x_ref, raw_ref = next(it), next(it)
    rest = list(it)
    rim_ref = rest.pop(0) if len(rest) == 5 else None
    y_ref, sums_ref, ring_ref, s_ref = rest
    pairs, colbuf, sumbuf, ringbuf, w_ref = refs[-5:]

    @pl.when(pl.program_id(0) == 0)
    def _():
        fill_pair_weights(raw_ref, 0, w_ref)

    group, n = x_ref.shape[0], x_ref.shape[1]
    half = n // 2

    for g in range(group):
        x = x_ref[g].astype(F32)
        if rim_ref is not None:
            x = with_rims(x, [rim_ref[g, e].astype(F32) for e in range(4)], n, colbuf)
        fill_pairs(pairs, x, n)
        for q0, m in pair_chunks(n, ENC_PAIRS.get(n, 6)):
            acc = pair_sums(pairs, w_ref, q0, m, None)
            put_sums(acc, sums_ref, g, q0, m, n, colbuf)
            out = silu(acc).astype(BF)[:, 0:n]
            y_ref[g, q0 : q0 + m, 0] = out[:, :, 0:128]
            y_ref[g, q0 : q0 + m, 1] = out[:, :, 128:256]
            wide = out.astype(F32)
            if q0 == 0:
                ring_ref[g, 0] = out[0, :, 128:256]
            if q0 + m == half:
                ring_ref[g, 2] = out[m - 1, :, 0:128]
            ringbuf[1, 2 * q0 : 2 * q0 + 2 * m] = column_of(wide, m, n - 8, 6, colbuf)
            ringbuf[0, 2 * q0 : 2 * q0 + 2 * m] = column_of(wide, m, 0, 1, colbuf)
            both = wide[:, :, 0:128] + wide[:, :, 128:256]
            sumbuf[...] = both.reshape(m * n, 128)
            small = sumbuf[pl.ds(0, m * half, 2), :] + sumbuf[pl.ds(1, m * half, 2), :]
            s_ref[g, q0 : q0 + m] = (small * 0.25).reshape(m, half, 128).astype(BF)
        ring_ref[g, 1] = ringbuf[1].astype(BF)
        ring_ref[g, 3] = ringbuf[0].astype(BF)


def dec_kernel(coarse_rims, *refs):
    refs = list(refs)
    x_ref, rim_ref, u_ref = refs.pop(0), refs.pop(0), refs.pop(0)
    urim_ref = refs.pop(0) if coarse_rims else None
    raw_ref = refs.pop(0)
    y_ref, sums_ref, pairs, rows, colbuf, acc_ref, w_ref, wu_ref = refs
    group, n = y_ref.shape[0], y_ref.shape[3]
    half = n // 2

    @pl.when(pl.program_id(0) == 0)
    def _():
        fill_pair_weights(raw_ref, 128, w_ref)
        fill_coarse_weights(raw_ref, wu_ref)

    for g in range(group):
        u = u_ref[g].astype(F32)
        if urim_ref is not None:
            u = with_rims(u, [urim_ref[g, e].astype(F32) for e in range(4)], half, colbuf.at[0 : half * 8])
        (fill_row_pairs if in_pairs(half) else fill_rows)(rows, u, half)
        x = with_rims(x_ref[g].astype(F32), [rim_ref[g, e].astype(F32) for e in range(4)], n, colbuf)
        fill_pairs(pairs, x, n)
        for q0, m in pair_chunks(n, DEC_PAIRS.get(n, 6)):
            for b in range(2):
                acc = None
                for k in range(3):
                    lhs, hp = coarse_lhs(rows, half, q0 + k, m, slice(b * 128, b * 128 + 256))
                    part = jnp.dot(lhs, wu_ref[b, k], preferred_element_type=F32)
                    acc = part if acc is None else acc + part
                acc = acc.reshape(m, hp, 256)
                for i in range(m):
                    for p in range(2):
                        acc_ref[p, i, pl.ds(b, half, 2), :] = acc[i, 0:half, p * 128 : p * 128 + 128]
            extra = jnp.concatenate([acc_ref[0], acc_ref[1]], axis=2)
            acc = pair_sums(pairs, w_ref, q0, m, extra)
            put_sums(acc, sums_ref, g, q0, m, n, colbuf)
            out = silu(acc).astype(BF)[:, 0:n]
            y_ref[g, q0 : q0 + m, 0] = out[:, :, 0:128]
            y_ref[g, q0 : q0 + m, 1] = out[:, :, 128:256]


def last_kernel(pick_ref, recv_ref, own_ref, sum_ref, x_ref, y_ref, *scratch):
    rim_ref, edge_buf, slab_ref, colbuf, in_sem, out_sem, row_sem = scratch
    del x_ref
    strips, n = own_ref.shape[0], own_ref.shape[1]
    tiles = strips // 4
    parts = in_sem.shape[1]
    span = tiles // parts

    def slab(side, part):
        return y_ref.at[pl.ds(part * span, span), :, pl.ds(side * (n - 16), 16), :]

    def held(side, part):
        return slab_ref.at[side, pl.ds(part * span, span)]

    reads = [
        [pltpu.make_async_copy(slab(side, p), held(side, p), in_sem.at[side, p]) for p in range(parts)]
        for side in range(2)
    ]
    for p in range(parts):
        for side in range(2):
            reads[side][p].start()

    end = n - 1

    def finish(t, k):
        con = [incoming(pick_ref, recv_ref, own_ref, t * 4 + e) for e in range(4)]
        for e in range(4):
            edge_buf[k, e] = sum_ref[t * 4 + e] + con[e]
        for e, cell, other, at in corners(end):
            cells = slice(cell, cell + 1)
            edge_buf[k, e, cells] = edge_buf[k, e, cells] + con[other][at : at + 1]
        for e in range(4):
            rim_ref[t, e] = silu(edge_buf[k, e]).astype(BF)

    each_tile(tiles, finish)

    rows = [
        pltpu.make_async_copy(
            rim_ref.at[:, e, pl.ds(16, n - 32), :], y_ref.at[:, row, pl.ds(16, n - 32), :], row_sem.at[j]
        )
        for j, (e, row) in enumerate(((0, 0), (2, n - 1)))
    ]
    for copy in rows:
        copy.start()

    sub = lax.broadcasted_iota(jnp.int32, (n, 8, 128), 1)

    def patch(side, t):
        lo = 0 if side == 0 else n - 16
        near = slice(0, 8) if side == 0 else slice(8, 16)
        far = slice(8, 16) if side == 0 else slice(0, 8)
        x = slab_ref[side, t].astype(F32)
        cells = spread_columns(rim_ref[t, 3 if side == 0 else 1].astype(F32), n, 0 if side == 0 else 7, colbuf)
        new = jnp.where(sub == (0 if side == 0 else 7), cells, x[:, near])
        both = [new, x[:, far]] if side == 0 else [x[:, far], new]
        slab_ref[side, t] = jnp.concatenate(both, axis=1).astype(BF)
        slab_ref[side, t, 0] = rim_ref[t, 0, lo : lo + 16]
        slab_ref[side, t, n - 1] = rim_ref[t, 2, lo : lo + 16]

    writes = []
    for p in range(parts):
        for side in range(2):
            reads[side][p].wait()

            def step(t, carry, side=side):
                patch(side, t)
                return carry

            lax.fori_loop(p * span, p * span + span, step, 0)
            copy = pltpu.make_async_copy(held(side, p), slab(side, p), out_sem.at[side, p])
            copy.start()
            writes.append(copy)
    for copy in writes + rows:
        copy.wait()


def last_step(x, plan, recv, own, sums):
    tiles, n, _, c = x.shape
    strips = own.shape[0]
    parts = 4 if tiles % 4 == 0 else 1
    smem = pl.BlockSpec(memory_space=pltpu.SMEM)
    vmem = pl.BlockSpec(memory_space=pltpu.VMEM)
    anywhere = pl.BlockSpec(memory_space=pl.ANY)
    return pl.pallas_call(
        last_kernel,
        in_specs=[smem, vmem, vmem, vmem, anywhere],
        out_specs=anywhere,
        out_shape=jax.ShapeDtypeStruct(x.shape, BF),
        scratch_shapes=[
            pltpu.VMEM((tiles, 4, n, c), BF),
            pltpu.VMEM((group_of(tiles, 3), 4, n, c), F32),
            pltpu.VMEM((2, tiles, n, 16, c), BF),
            pltpu.VMEM((n * 8, c), F32),
            pltpu.SemaphoreType.DMA((2, parts)),
            pltpu.SemaphoreType.DMA((2, parts)),
            pltpu.SemaphoreType.DMA((2,)),
        ],
        input_output_aliases={4: 0},
        compiler_params=params(),
        name="last_step",
    )(plan[0], recv, own, sums, x)


def group_of(tiles, want):
    return max(g for g in range(1, want + 1) if tiles % g == 0)


def tile_spec(group, *dims):
    return pl.BlockSpec((group,) + dims, lambda i: (i,) + (0,) * len(dims))


def whole_spec(shape):
    return pl.BlockSpec(shape, lambda i: (0,) * len(shape))


def enc_conv(x, rim, w, want):
    tiles, n, _, c = x.shape
    half, n_p = n // 2, up16(n)
    g = group_of(tiles, want)
    m = pair_chunks(n, ENC_PAIRS.get(n, 6))[0][1]
    args, specs = [x, w.reshape(9, c, c)], [tile_spec(g, n, n, c), whole_spec((9, c, c))]
    if rim is not None:
        args.append(rim.reshape(tiles, 4, n, c))
        specs.append(tile_spec(g, 4, n, c))
    y, sums, ring, s = pl.pallas_call(
        enc_kernel,
        grid=(tiles // g,),
        in_specs=specs,
        out_specs=[
            tile_spec(g, half, 2, n, c), tile_spec(g, 4, n, c), tile_spec(g, 4, n, c), tile_spec(g, half, half, c)
        ],
        out_shape=[
            jax.ShapeDtypeStruct((tiles, half, 2, n, c), BF),
            jax.ShapeDtypeStruct((tiles, 4, n, c), F32),
            jax.ShapeDtypeStruct((tiles, 4, n, c), BF),
            jax.ShapeDtypeStruct((tiles, half, half, c), BF),
        ],
        scratch_shapes=[
            pltpu.VMEM((half + 1, n_p, 768), BF),
            pltpu.VMEM((n * 8, 128), F32),
            pltpu.VMEM((m * n, 128), F32),
            pltpu.VMEM((2, n, 128), F32),
            pltpu.VMEM((1536, 256), BF),
        ],
        compiler_params=params(),
        cost_estimate=pl.CostEstimate(
            flops=tiles * n * n * 2 * 1536 * 128, bytes_accessed=tiles * n * n * 600, transcendentals=tiles * n * n * 128
        ),
        name="enc_conv",
    )(*args)
    strips = lambda a: a.reshape(tiles * 4, n, c)
    return y.reshape(tiles, n, n, c), strips(sums), strips(ring), s


def dec_conv(x, rim, u, urim, w, want):
    tiles, n, _, c = x.shape
    half, n_p = n // 2, up16(n)
    g = group_of(tiles, want)
    m = pair_chunks(n, DEC_PAIRS.get(n, 6))[0][1]
    args = [x, rim.reshape(tiles, 4, n, c), u]
    specs = [tile_spec(g, n, n, c), tile_spec(g, 4, n, c), tile_spec(g, half, half, c)]
    if urim is not None:
        args.append(urim.reshape(tiles, 4, half, c))
        specs.append(tile_spec(g, 4, half, c))
    args.append(w.reshape(9, 2 * c, c))
    specs.append(whole_spec((9, 2 * c, c)))
    rows = (half + 1, 2 * half, 384) if in_pairs(half) else (half + 2, up16(half), 384)

    def kernel(*refs):
        dec_kernel(urim is not None, *refs)

    y, sums = pl.pallas_call(
        kernel,
        grid=(tiles // g,),
        in_specs=specs,
        out_specs=[tile_spec(g, half, 2, n, c), tile_spec(g, 4, n, c)],
        out_shape=[
            jax.ShapeDtypeStruct((tiles, half, 2, n, c), BF),
            jax.ShapeDtypeStruct((tiles, 4, n, c), F32),
        ],
        scratch_shapes=[
            pltpu.VMEM((half + 1, n_p, 768), BF),
            pltpu.VMEM(rows, BF),
            pltpu.VMEM((n * 8, 128), F32),
            pltpu.VMEM((2, m, n_p, 128), F32),
            pltpu.VMEM((1536, 256), BF),
            pltpu.VMEM((2, 3, 256, 256), BF),
        ],
        compiler_params=params(),
        cost_estimate=pl.CostEstimate(
            flops=tiles * n * n * 2 * 2300 * 128, bytes_accessed=tiles * n * n * 600, transcendentals=tiles * n * n * 128
        ),
        name="dec_conv",
    )(*args)
    return y.reshape(x.shape), sums.reshape(tiles * 4, n, c)


def strips_of(field, ring=0):
    n = field.shape[1]
    far = n - 1 - ring
    out = jnp.stack([field[:, ring], field[:, :, far], field[:, far], field[:, :, ring]], axis=1)
    out = jnp.pad(out, ((0, 0), (0, 0), (0, strip_rows(n) - n), (0, 0)))
    return out.reshape(field.shape[0] * 4, strip_rows(n), field.shape[3])


def patched(field, rim):
    tiles, n, _, c = field.shape
    rim = rim.reshape(tiles, 4, -1, c)[:, :, :n]
    middle = jnp.concatenate(
        [rim[:, 3, 1 : n - 1, None], field[:, 1 : n - 1, 1 : n - 1], rim[:, 1, 1 : n - 1, None]], axis=2
    )
    return jnp.concatenate([rim[:, 0][:, None], middle, rim[:, 2][:, None]], axis=1)


def inner_sums(field, weight):
    return lax.conv_general_dilated(
        field,
        weight,
        (1, 1),
        ((1, 1), (1, 1)),
        dimension_numbers=("NHWC", "HWIO", "NHWC"),
        preferred_element_type=F32,
    )


def shrink(field):
    count, length, _, channels = field.shape
    blocks = field.astype(F32).reshape(count, length // 2, 2, length // 2, 2, channels)
    return (jnp.sum(blocks, axis=(2, 4)) * 0.25).astype(BF)


def enlarge(field):
    return jnp.repeat(jnp.repeat(field, 2, axis=1), 2, axis=2)


def per_device(features, edge_table, w_enc0, w_enc1, w_enc2, w_mid, w_dec2, w_dec1, w_dec0):
    tiles, n0 = features.shape[0], features.shape[1]
    devices = lax.axis_size("tile")
    position = lax.axis_index("tile")
    cap = pair_capacity(FACE_TILES, tiles)
    rows = devices * cap
    slot_row = send_slots(edge_table, position, tiles, cap)

    def trade(strips):
        length = strips.shape[1]
        out = lax.all_to_all(
            strips.reshape(devices, cap * length, 128), "tile", split_axis=0, concat_axis=0, tiled=True
        )
        return out.reshape(rows, length, 128)

    def after(value, token):
        return lax.optimization_barrier((value, token))[0]

    rim0, send = tile_rims(features, slot_row, rows)
    rim0 = rim0.reshape(tiles * 4, n0, 128)
    plan = receive_plan(after(edge_table, send), slot_row, position, tiles, cap, devices)
    recv = trade(send)
    enc0, sums, ring, x1 = enc_conv(features, None, w_enc0, 1)
    enc0_rim, x1_rim, send = rim_step(n0, plan, recv, rim0, sums, w=w_enc0, ring=ring)

    recv = trade(send)
    enc1, sums, ring, x2 = enc_conv(x1, x1_rim, w_enc1, 4)
    enc1_rim, x2_rim, send = rim_step(n0 // 2, plan, recv, x1_rim, sums, w=w_enc1, ring=ring)

    recv = trade(send)
    sums = inner_sums(patched(x2, x2_rim), w_enc2)
    enc2 = jax.nn.silu(sums).astype(BF)
    enc2_rim, x3_rim, send = rim_step(
        n0 // 4, plan, recv, x2_rim, strips_of(sums), w=w_enc2, ring=strips_of(enc2, 1)
    )

    recv = trade(send)
    sums = inner_sums(patched(shrink(enc2), x3_rim), w_mid)
    middle = jax.nn.silu(sums).astype(BF)
    skip2 = skip_step(n0 // 4, plan, enc2_rim, w_dec2)
    skip0 = skip_step(n0, plan, after(enc0_rim, x3_rim), w_dec0)
    sums, skip0 = lax.optimization_barrier((sums, skip0))
    mid_rim, own, send = rim_step(
        n0 // 8, plan, recv, x3_rim, strips_of(sums), w=w_mid,
        skip=skip2, wn=w_dec2,
    )

    recv = trade(send)
    joined = jnp.concatenate([enlarge(patched(middle, mid_rim)), patched(enc2, enc2_rim)], axis=3)
    sums = inner_sums(joined, w_dec2)
    dec2 = jax.nn.silu(sums).astype(BF)
    skip1 = skip_step(n0 // 2, plan, after(enc1_rim, mid_rim), w_dec1)
    dec2_rim, own, send = rim_step(
        n0 // 4, plan, recv, own, strips_of(sums), skip=skip1, wn=w_dec1
    )

    recv = trade(send)
    dec1, sums = dec_conv(enc1, enc1_rim, patched(dec2, dec2_rim), None, w_dec1, 4)
    dec1_rim, own, send = rim_step(
        n0 // 2, plan, recv, own, sums, skip=skip0, wn=w_dec0
    )

    recv = trade(send)
    dec0, sums = dec_conv(enc0, enc0_rim, dec1, dec1_rim, w_dec0, 1)
    return last_step(dec0, plan, recv, own, sums)


def solution(mesh):
    return jax.shard_map(
        per_device,
        mesh=mesh,
        in_specs=(P(("grp", "tile"), None, None, None), P(), P(), P(), P(), P(), P(), P(), P()),
        out_specs=P(("grp", "tile"), None, None, None),
        check_vma=False,
    )
```

```python
import jax
import jax.numpy as jnp
import numpy as np
from jax import lax
from jax.experimental import pallas as pl
from jax.experimental.pallas import tpu as pltpu
from jax.sharding import PartitionSpec as P

FACE_TILES = 8
RIM_TILES = 12
VMEM_LIMIT = 50 * 2**20
BF = jnp.bfloat16
F32 = jnp.float32


def cube_links(tiles_side):
    basis = np.eye(3, dtype=np.int64)
    frames = []
    for axis_id in range(3):
        for orient in (1, -1):
            frames.append(
                (orient * basis[axis_id], basis[(axis_id + 1) % 3], basis[(axis_id + 2) % 3])
            )
    per_face = tiles_side * tiles_side
    tile_total = 6 * per_face
    centres = np.zeros((tile_total, 3), np.int64)
    lookup = {}
    for face_id in range(6):
        normal, row_axis, col_axis = frames[face_id]
        for row_id in range(tiles_side):
            for col_id in range(tiles_side):
                slot_id = face_id * per_face + row_id * tiles_side + col_id
                centre = (
                    tiles_side * normal
                    + (2 * row_id + 1 - tiles_side) * row_axis
                    + (2 * col_id + 1 - tiles_side) * col_axis
                )
                centres[slot_id] = centre
                lookup[tuple((int(entry) for entry in centre))] = slot_id
    partner = np.zeros((tile_total, 4), np.int64)
    for slot_id in range(tile_total):
        normal, row_axis, col_axis = frames[slot_id // per_face]
        outward = (-row_axis, col_axis, row_axis, -col_axis)
        for edge_id in range(4):
            beyond = tuple((int(entry) for entry in centres[slot_id] + 2 * outward[edge_id]))
            if beyond in lookup:
                partner[slot_id, edge_id] = lookup[beyond]
            else:
                partner[slot_id, edge_id] = lookup[
                    tuple((int(entry) for entry in centres[slot_id] + outward[edge_id] - normal))
                ]
    return partner


def pair_capacity(tiles_side, tiles_here):
    partner = cube_links(tiles_side)
    tile_total = partner.shape[0]
    blocks = tile_total // tiles_here
    source = np.repeat(np.arange(tile_total) // tiles_here, 4)
    target = partner.reshape(-1) // tiles_here
    identity = np.eye(blocks, dtype=np.int64)
    shared = identity[source].T @ identity[target]
    shared = shared * (1 - identity)
    return max(int(shared.max()), 1)


def own_strips(edge_table, position, tiles_here):
    rows = lax.dynamic_slice_in_dim(edge_table, position * tiles_here, tiles_here, 0)
    rows = rows.reshape(tiles_here * 4, 2)
    return rows[:, 0], rows[:, 1] // 2, rows[:, 1] % 2


def send_slots(edge_table, position, tiles_here, slot_count):
    partner, _, _ = own_strips(edge_table, position, tiles_here)
    target = partner // tiles_here
    order = jnp.arange(tiles_here * 4, dtype=jnp.int32)
    earlier = (order[None, :] < order[:, None]) & (target[None, :] == target[:, None])
    slot_rank = jnp.sum(earlier.astype(jnp.int32), axis=1)
    return jnp.where(target != position, target * slot_count + slot_rank, -1)


def listed(mask):
    order = jnp.arange(mask.shape[0], dtype=jnp.int32)
    rank = jnp.sum((mask[None, :] & (order[None, :] < order[:, None])).astype(jnp.int32), axis=1)
    hit = mask[None, :] & (rank[None, :] == order[:, None])
    found = jnp.sum(jnp.where(hit, order[None, :], 0), axis=1)
    total = jnp.sum(mask.astype(jnp.int32), keepdims=True)
    found = jnp.where(order < total, found, mask.shape[0])
    return jnp.concatenate([found, jnp.full((3,), mask.shape[0], jnp.int32), total])


def receive_plan(edge_table, slot_row, position, tiles_here, slot_count, devices):
    strip_count = tiles_here * 4
    partner, matching, reversed_rows = own_strips(edge_table, position, tiles_here)
    target = partner // tiles_here
    order = jnp.arange(strip_count, dtype=jnp.int32)
    remote = target != position
    wanted = partner % tiles_here * 4 + matching
    toward_me = edge_table[:, :, 0].reshape(devices, strip_count) // tiles_here == position
    before = (order[:, None] < order[None, :]).astype(BF)
    ranks = jnp.dot(toward_me.astype(BF), before, preferred_element_type=F32).astype(BF)
    blocks = jnp.arange(devices, dtype=jnp.int32)
    from_target = (target[:, None] == blocks[None, :]).astype(BF)
    their_ranks = jnp.dot(from_target, ranks, preferred_element_type=F32)
    recv_rank = jnp.sum(jnp.where(wanted[:, None] == order[None, :], their_ranks, 0.0), axis=1).astype(jnp.int32)
    pick_row = lambda count: jnp.where(remote, target * count + recv_rank, devices * count + wanted)
    odd = (matching != (order + 2) % 4) | (reversed_rows == 1)
    one_more = lambda a: jnp.concatenate([a, jnp.zeros((1,), jnp.int32)])
    even = (slot_count + 1) // 2 * 2
    paired_slot = slot_row + target * (even - slot_count)
    shared = (one_more(reversed_rows), one_more(matching), listed(remote), listed(odd))
    return (pick_row(slot_count), pick_row(even)), (slot_row, paired_slot), shared


def up16(n):
    return (n + 15) // 16 * 16


def strip_rows(n):
    return {6: 8, 12: 16}.get(n, n)


def two_up(rows):
    return rows == 16


def send_shape(devices, cap, rows):
    return (devices * ((cap + 1) // 2), 24) if two_up(rows) else (devices * cap, rows)


def params():
    return pltpu.CompilerParams(vmem_limit_bytes=VMEM_LIMIT)


def rims_kernel(slot_ref, lo_ref, hi_ref, top_ref, bottom_ref, out_ref, send_ref, colbuf):
    group, n = lo_ref.shape[0], lo_ref.shape[1]
    first = pl.program_id(0) * group * 4
    for g in range(group):
        colbuf[...] = lo_ref[g, :, 0:8, :].astype(F32).reshape(n * 8, 128)
        left = colbuf[pl.ds(0, n, 8), :]
        colbuf[...] = hi_ref[g, :, 8:16, :].astype(F32).reshape(n * 8, 128)
        right = colbuf[pl.ds(7, n, 8), :]
        out_ref[g, 0] = top_ref[g, 0]
        out_ref[g, 1] = right.astype(BF)
        out_ref[g, 2] = bottom_ref[g, 0]
        out_ref[g, 3] = left.astype(BF)
    for g in range(group):
        for e in range(4):
            slot = slot_ref[first + g * 4 + e]

            @pl.when(slot >= 0)
            def _():
                send_ref[slot] = out_ref[g, e]


def tile_rims(x, slot_row, rows):
    tiles, n, _, c = x.shape
    g = group_of(tiles, RIM_TILES)
    last = n // 16 - 1
    return pl.pallas_call(
        rims_kernel,
        grid=(tiles // g,),
        in_specs=[
            pl.BlockSpec(memory_space=pltpu.SMEM),
            pl.BlockSpec((g, n, 16, c), lambda i: (i, 0, 0, 0)),
            pl.BlockSpec((g, n, 16, c), lambda i: (i, 0, last, 0)),
            pl.BlockSpec((g, 1, n, c), lambda i: (i, 0, 0, 0)),
            pl.BlockSpec((g, 1, n, c), lambda i: (i, n - 1, 0, 0)),
        ],
        out_specs=[tile_spec(g, 4, n, c), whole_spec((rows, n, c))],
        out_shape=[
            jax.ShapeDtypeStruct((tiles, 4, n, c), BF),
            jax.ShapeDtypeStruct((rows, n, c), BF),
        ],
        scratch_shapes=[pltpu.VMEM((n * 8, 128), F32)],
        compiler_params=params(),
        name="tile_rims",
    )(slot_row, x, x, x, x)


def silu(s):
    half = s * 0.5
    return half + half * jnp.tanh(half)


def strip_shifts(h, n):
    rows = h.shape[0]
    row = lax.broadcasted_iota(jnp.int32, h.shape, 0)
    half = h * 0.5
    down = jnp.where(row == 0, half, pltpu.roll(h, 1, 0))
    up = jnp.where(row == n - 1, half, pltpu.roll(h, rows - 1, 0))
    return down, up


def flip_matrices(rows, n):
    ri = lax.broadcasted_iota(jnp.int32, (rows, rows), 0)
    ci = lax.broadcasted_iota(jnp.int32, (rows, rows), 1)
    return (ri + ci == n - 1).astype(F32), (ri == ci).astype(F32)


def put_shifts(ref, index, lane, h, n):
    down, up = strip_shifts(h, n)
    for s, part in enumerate((down, h, up)):
        ref[index + (slice(None), slice(lane + s * 128, lane + s * 128 + 128))] = part.astype(ref.dtype)


def each_tile(tiles, body):
    side = group_of(tiles, 3)

    def step(i, carry):
        for k in range(side):
            body(i * side + k, k)
        return carry

    lax.fori_loop(0, tiles // side, step, 0)


def each_listed(list_ref, body):
    def step(j, carry):
        body(list_ref[j])
        return carry

    lax.fori_loop(0, list_ref[list_ref.shape[0] - 1], step, 0)


def each_four(list_ref, body):
    def step(j, carry):
        body([list_ref[j * 4 + k] for k in range(4)])
        return carry

    lax.fori_loop(0, (list_ref[list_ref.shape[0] - 1] + 3) // 4, step, 0)


def turned(rev_ref, i, h, flip, keep):
    order = jnp.where(rev_ref[i] == 1, flip, keep).astype(BF)
    return jnp.dot(order, h.astype(BF), preferred_element_type=F32)


def incoming(pick_ref, recv_ref, own_ref, i):
    paired = own_ref.shape[1] != recv_ref.shape[1]
    slots = recv_ref.shape[0] * (2 if paired else 1)
    pick = pick_ref[i]
    away = pick < slots
    slot = jnp.minimum(pick, slots - 1)
    b = own_ref[jnp.maximum(pick - slots, 0)].astype(F32)
    if not paired:
        return jnp.where(away, recv_ref[slot].astype(F32), b)
    a = recv_ref[slot >> 1].astype(F32)
    row = lax.broadcasted_iota(jnp.int32, (16, 128), 0)
    a = jnp.where(row < 12, jnp.where((slot & 1) == 1, pltpu.roll(a, 12, 0), a)[0:16], 0.0)
    return jnp.where(away, a, b)


def edge_taps(w_ref, e, lo):
    taps = ((0, 1, 2), (2, 5, 8), (6, 7, 8), (0, 3, 6))[e]
    return jnp.concatenate([w_ref[tap, lo : lo + 128, :] for tap in taps], axis=0)


def contributions(n, tiles, strip_of, w_ref, lo, rev_ref, edge_ref, odd_ref, lhs_ref, con_ref, taps_ref):
    lp = lhs_ref.shape[2]
    for e in range(4):
        taps_ref[e] = edge_taps(w_ref, e, lo)

    def fill(t, k):
        for f in range(4):
            put_shifts(lhs_ref, (f, t), 0, strip_of(f, t, k), n)

    each_tile(tiles, fill)
    for f in range(4):
        lhs = lhs_ref[f, 0:tiles].reshape(tiles * lp, 384).astype(BF)
        out = jnp.dot(lhs, taps_ref[(f + 2) % 4], preferred_element_type=F32)
        con_ref[f, 0:tiles] = out.reshape(tiles, lp, 128)
    flip, keep = flip_matrices(lp, n)

    def odd_ones(four):
        halos = [lhs_ref[i % 4, i // 4, :, 128:256] for i in four]
        halos = [turned(rev_ref, i, h, flip, keep) for i, h in zip(four, halos)]
        taps = [taps_ref[edge_ref[i]] for i in four]
        sums = []
        for h, tap in zip(halos, taps):
            down, up = strip_shifts(h, n)
            lhs = jnp.concatenate([down.astype(BF), h.astype(BF), up.astype(BF)], axis=1)
            sums.append(jnp.dot(lhs, tap, preferred_element_type=F32))
        for i, total in zip(four, sums):
            con_ref[i % 4, i // 4] = total

    each_four(odd_ref, odd_ones)


def skip_kernel(n, rev_ref, edge_ref, odd_ref, rim_ref, w_ref, out_ref, lhs_ref, con_ref, taps_ref):
    tiles = rim_ref.shape[0] // 4
    contributions(
        n, tiles, lambda f, t, k: rim_ref[t * 4 + f].astype(F32), w_ref, 128,
        rev_ref, edge_ref, odd_ref, lhs_ref, con_ref, taps_ref,
    )

    def put(t, k):
        for f in range(4):
            out_ref[t * 4 + f] = con_ref[f, t]

    each_tile(tiles, put)


def wide(rows):
    return BF if rows % 16 == 0 else F32


def skip_step(n, plan, rim, w):
    strips, lp, c = rim.shape
    smem = pl.BlockSpec(memory_space=pltpu.SMEM)
    vmem = pl.BlockSpec(memory_space=pltpu.VMEM)
    return pl.pallas_call(
        lambda *refs: skip_kernel(n, *refs),
        in_specs=[smem, smem, smem, vmem, vmem],
        out_specs=vmem,
        out_shape=jax.ShapeDtypeStruct((strips, lp, c), F32),
        scratch_shapes=[
            pltpu.VMEM((4, strips // 4 + 1, lp, 384), wide(lp)),
            pltpu.VMEM((4, strips // 4 + 1, lp, 128), F32),
            pltpu.VMEM((4, 384, 128), BF),
        ],
        compiler_params=params(),
        cost_estimate=pl.CostEstimate(flops=strips * lp * 2 * 384 * 256, bytes_accessed=strips * lp * 768, transcendentals=0),
        name="skip_step",
    )(plan[2][0], plan[2][1], plan[2][3], rim, w.reshape(9, -1, c))


def corners(end):
    return (
        (0, 0, 3, 0), (0, end, 1, 0), (2, 0, 3, end), (2, end, 1, end),
        (3, 0, 0, 0), (3, end, 2, 0), (1, 0, 0, end), (1, end, 2, end),
    )


def rim_kernel(n, strips_in, nxt, refs):
    it = iter(refs)
    pick_ref, rev_ref, slot_ref, edge_ref, remote_ref, odd_ref = [next(it) for _ in range(6)]
    recv_ref, own_ref, sum_ref = next(it), next(it), next(it)
    w_ref = next(it) if strips_in else None
    ring_ref = next(it) if nxt == "shrink" else None
    skip_ref, wn_ref = (next(it), next(it)) if nxt == "halo" else (None, None)
    rim_ref, next_ref, send_ref = next(it), next(it), next(it)
    halo_ref, lhs_ref, con_ref = next(it), next(it), next(it)
    edge_buf, ring_buf, sum_buf, out_buf = next(it), next(it), next(it), next(it)
    lhsn_ref, conn_ref, taps_ref, big_buf = [next(it) for _ in range(4)] if nxt == "halo" else [None] * 4

    strips, lp = own_ref.shape[0], own_ref.shape[1]
    tiles = strips // 4
    flip, keep = flip_matrices(lp, n)

    if strips_in:

        def fetch(t, k):
            for e in range(4):
                i = t * 4 + e
                halo_ref[i] = incoming(pick_ref, recv_ref, own_ref, i).astype(BF)

        each_tile(tiles, fetch)

        def turn(four):
            halos = [turned(rev_ref, i, halo_ref[i], flip, keep).astype(BF) for i in four]
            for i, h in zip(four, halos):
                halo_ref[i] = h

        each_four(odd_ref, turn)

        def fill(t, k):
            for e in range(4):
                put_shifts(lhs_ref, (e, t), 0, halo_ref[t * 4 + e].astype(F32), n)

        each_tile(tiles, fill)
        for e in range(4):
            lhs = lhs_ref[e].reshape(tiles * lp, 384).astype(BF)
            out = jnp.dot(lhs, edge_taps(w_ref, e, 0), preferred_element_type=F32)
            con_ref[e] = out.reshape(tiles, lp, 128)
    else:

        def fill(t, k):
            for e in range(4):
                con_ref[e, t] = incoming(pick_ref, recv_ref, own_ref, t * 4 + e)

        each_tile(tiles, fill)

    end = n - 1
    joints = (
        (0, 0, 3, 1), (0, end, 1, 1), (2, 0, 3, end - 1), (2, end, 1, end - 1),
        (3, 0, 0, 1), (3, end, 2, 1), (1, 0, 0, end - 1), (1, end, 2, end - 1),
    )
    if nxt == "shrink":
        out_buf[...] = jnp.zeros_like(out_buf)

    def finish(t, k):
        for e in range(4):
            edge_buf[k, e] = sum_ref[t * 4 + e] + con_ref[e, t]
        for e, cell, other, at in corners(end):
            cells = slice(cell, cell + 1)
            edge_buf[k, e, cells] = edge_buf[k, e, cells] + con_ref[other, t, at : at + 1]
        for e in range(4):
            y = silu(edge_buf[k, e]).astype(BF)
            rim_ref[t * 4 + e] = y
            edge_buf[k, e] = y.astype(F32)
        if nxt == "shrink":
            for e in range(4):
                ring_buf[k, e] = ring_ref[t * 4 + e].astype(F32)
            for e, cell, other, at in joints:
                ring_buf[k, e, cell : cell + 1] = edge_buf[k, other, at : at + 1]
            for e in range(4):
                sum_buf[k, e] = edge_buf[k, e] + ring_buf[k, e]
                small = sum_buf[k, e, pl.ds(0, lp // 2, 2), :] + sum_buf[k, e, pl.ds(1, lp // 2, 2), :]
                out_buf[k, e, 0 : lp // 2] = small * 0.25
                next_ref[t * 4 + e] = out_buf[k, e].astype(BF)

    each_tile(tiles, finish)

    if nxt == "halo":
        half = big_buf.shape[2] // 2

        def enlarged(f, t, k):
            rim = rim_ref[t * 4 + f].astype(F32)[0:half]
            big_buf[k, f, pl.ds(0, half, 2), :] = rim
            big_buf[k, f, pl.ds(1, half, 2), :] = rim
            return big_buf[k, f]

        contributions(
            2 * n, tiles, enlarged, wn_ref, 0,
            rev_ref, edge_ref, odd_ref, lhsn_ref, conn_ref, taps_ref,
        )

        def put(t, k):
            for f in range(4):
                next_ref[t * 4 + f] = (conn_ref[f, t] + skip_ref[t * 4 + f]).astype(BF)

        each_tile(tiles, put)

    def send(i):
        slot = slot_ref[i]
        if next_ref.shape[1] == send_ref.shape[1]:
            send_ref[slot] = next_ref[i]
        else:
            block, second = slot >> 1, (slot & 1) == 1
            strip = jnp.concatenate([next_ref[i].astype(F32), jnp.zeros((8, 128), F32)], axis=0)
            row = lax.broadcasted_iota(jnp.int32, (24, 128), 0)
            held = send_ref[block].astype(F32)
            both = jnp.where(second, jnp.where(row < 12, held, pltpu.roll(strip, 12, 0)), jnp.where(row < 12, strip, held))
            send_ref[block] = both.astype(BF)

    each_listed(remote_ref, send)


def rim_step(n, devices, cap, plan, recv, own, sums, w=None, ring=None, skip=None, wn=None):
    strips, lp, c = own.shape
    tiles = strips // 4
    side = group_of(tiles, 3)
    nxt = "shrink" if ring is not None else "halo"
    smem = pl.BlockSpec(memory_space=pltpu.SMEM)
    vmem = pl.BlockSpec(memory_space=pltpu.VMEM)
    w = w if w is None else w.reshape(9, -1, c)
    wn = wn if wn is None else wn.reshape(9, -1, c)
    args = [recv, own, sums] + [a for a in (w, ring, skip, wn) if a is not None]
    lo = strip_rows(n // 2) if nxt == "shrink" else strip_rows(2 * n)
    outs = [
        jax.ShapeDtypeStruct((strips, lp, c), BF),
        jax.ShapeDtypeStruct((strips, lo, c), BF),
        jax.ShapeDtypeStruct(send_shape(devices, cap, lo) + (c,), BF),
    ]
    scratch = [
        pltpu.VMEM((strips + 1, lp, 128), BF),
        pltpu.VMEM((4, tiles, lp, 384), wide(lp)),
        pltpu.VMEM((4, tiles, lp, 128), F32),
        pltpu.VMEM((side, 4, lp, 128), F32),
        pltpu.VMEM((side, 4, lp, 128), F32),
        pltpu.VMEM((side, 4, lp, 128), F32),
        pltpu.VMEM((side, 4, lo, 128), F32),
    ]
    if nxt == "halo":
        scratch += [
            pltpu.VMEM((4, tiles + 1, lo, 384), wide(lo)),
            pltpu.VMEM((4, tiles + 1, lo, 128), F32),
            pltpu.VMEM((4, 384, 128), BF),
            pltpu.VMEM((side, 4, lo, 128), F32),
        ]

    def kernel(*refs):
        rim_kernel(n, w is not None, nxt, refs)

    return pl.pallas_call(
        kernel,
        in_specs=[smem] * 6 + [vmem] * len(args),
        out_specs=[vmem] * len(outs),
        out_shape=outs,
        scratch_shapes=scratch,
        compiler_params=params(),
        cost_estimate=pl.CostEstimate(flops=strips * lp * 2 * 384 * 512, bytes_accessed=strips * lp * 1500, transcendentals=0),
        name="rim_step",
    )(plan[0][int(two_up(lp))], plan[2][0], plan[1][int(two_up(lo))], *plan[2][1:], *args)


def spread_columns(strip, n, sublane, buf):
    buf[pl.ds(sublane, n, 8), :] = strip
    return buf[...].reshape(n, 8, 128)


def with_rims(x, rim, n, buf):
    sub = lax.broadcasted_iota(jnp.int32, (n, 8, 128), 1)
    head = jnp.where(sub == 0, spread_columns(rim[3], n, 0, buf), x[:, 0:8])
    tail = jnp.where(sub == 7, spread_columns(rim[1], n, 7, buf), x[:, n - 8 : n])
    x = jnp.concatenate([head, x[:, 8 : n - 8], tail], axis=1)
    return jnp.concatenate([rim[0][None], x[1 : n - 1], rim[2][None]], axis=0)


def column_shifts(x, n):
    sub = lax.broadcasted_iota(jnp.int32, (x.shape[0], 8, 128), 1)
    down = pltpu.roll(x, 1, 1)
    up = pltpu.roll(x, n - 1, 1)
    down = jnp.concatenate([jnp.where(sub == 0, 0.0, down[:, 0:8]), down[:, 8:n]], axis=1)
    up = jnp.concatenate([up[:, 0 : n - 8], jnp.where(sub == 7, 0.0, up[:, n - 8 : n])], axis=1)
    return down, x, up


def fill_pairs(y_ref, x, n):
    half, n_p = n // 2, y_ref.shape[1]
    zero = jnp.zeros((n_p, 384), BF)
    y_ref[0, :, 0:384] = zero
    y_ref[half, :, 384:768] = zero
    for s, body in enumerate(column_shifts(x, n)):
        b = body.astype(BF).reshape(half, 2, n, 128)
        y_ref[0:half, 0:n, 384 + s * 128 : 384 + s * 128 + 128] = b[:, 0]
        y_ref[1 : half + 1, 0:n, s * 128 : s * 128 + 128] = b[:, 1]


def in_pairs(n):
    return n % 16 == 8 and n % 2 == 0


def fill_row_pairs(u_ref, x, n):
    half = n // 2
    zero = jnp.zeros((n, 384), BF)
    u_ref[0, 0:n] = zero
    u_ref[half, n : 2 * n] = zero
    for s, body in enumerate(column_shifts(x, n)):
        b = body.astype(BF).reshape(half, 2, n, 128)
        lanes = slice(s * 128, s * 128 + 128)
        u_ref[0:half, n : 2 * n, lanes] = b[:, 0]
        u_ref[1 : half + 1, 0:n, lanes] = b[:, 1]
        u_ref[half + 1 : n + 1, 0:n, lanes] = b[:, 0]
        u_ref[half + 1 : n + 1, n : 2 * n, lanes] = b[:, 1]


def coarse_lhs(u_ref, n, start, m, lanes):
    if in_pairs(n):
        at = start // 2 if start % 2 == 0 else n // 2 + 1 + start // 2
        return u_ref[at : at + m // 2, :, lanes].reshape(m * n, 256), n
    return u_ref[start : start + m, :, lanes].reshape(m * u_ref.shape[1], 256), u_ref.shape[1]


def fill_rows(u_ref, x, n):
    zero = jnp.zeros((u_ref.shape[1], 384), BF)
    u_ref[0] = zero
    u_ref[n + 1] = zero
    for s, body in enumerate(column_shifts(x, n)):
        u_ref[1 : n + 1, 0:n, s * 128 : s * 128 + 128] = body.astype(BF)


def pair_sums(y_ref, w_ref, q0, m, extra):
    n_p = y_ref.shape[1]
    a = y_ref[q0 : q0 + m].reshape(m * n_p, 768)
    b = y_ref[q0 + 1 : q0 + 1 + m].reshape(m * n_p, 768)
    acc = jnp.dot(a, w_ref[0:768, :], preferred_element_type=F32)
    acc = acc + jnp.dot(b, w_ref[768:1536, :], preferred_element_type=F32)
    acc = acc.reshape(m, n_p, 256)
    return acc if extra is None else acc + extra


def pair_chunks(n, most):
    half = n // 2
    m = max(m for m in range(1, most + 1) if half % m == 0)
    return [(q, m) for q in range(0, half, m)]


ENC_PAIRS = {48: 24}
DEC_PAIRS = {48: 12}


def column_of(acc, m, lo, sublane, colbuf):
    rows = jnp.stack([acc[:, lo : lo + 8, 0:128], acc[:, lo : lo + 8, 128:256]], axis=1)
    colbuf[0 : 16 * m] = rows.reshape(16 * m, 128)
    return colbuf[pl.ds(sublane, 2 * m, 8), :]


def put_sums(acc, sums_ref, g, q0, m, n, colbuf):
    cells = slice(2 * q0, 2 * q0 + 2 * m)
    if q0 == 0:
        sums_ref[g, 0] = acc[0, 0:n, 0:128]
    if q0 + m == n // 2:
        sums_ref[g, 2] = acc[m - 1, 0:n, 128:256]
    sums_ref[g, 3, cells] = column_of(acc, m, 0, 0, colbuf)
    sums_ref[g, 1, cells] = column_of(acc, m, n - 8, 7, colbuf)


def fill_pair_weights(raw_ref, lo, w_ref):
    for p in range(4):
        for col in range(3):
            at = slice((p * 3 + col) * 128, (p * 3 + col) * 128 + 128)
            for out in range(2):
                row = p - out
                tap = raw_ref[row * 3 + col, lo : lo + 128, :] if 0 <= row <= 2 else jnp.zeros((128, 128), BF)
                w_ref[at, out * 128 : out * 128 + 128] = tap


def fill_coarse_weights(raw_ref, w_ref):
    along = (((0,), (1, 2), ()), ((), (0, 1), (2,)))
    for b in range(2):
        for k in range(3):
            for slot in range(2):
                cols = along[b][slot + b]
                for out in range(2):
                    taps = [raw_ref[r * 3 + col, 0:128, :].astype(F32) for r in along[out][k] for col in cols]
                    total = sum(taps[1:], taps[0]) if taps else jnp.zeros((128, 128), F32)
                    w_ref[b, k, slot * 128 : slot * 128 + 128, out * 128 : out * 128 + 128] = total.astype(BF)


def enc_kernel(*refs):
    it = iter(refs[:-5])
    x_ref, raw_ref = next(it), next(it)
    rest = list(it)
    rim_ref = rest.pop(0) if len(rest) == 5 else None
    y_ref, sums_ref, ring_ref, s_ref = rest
    pairs, colbuf, sumbuf, ringbuf, w_ref = refs[-5:]

    @pl.when(pl.program_id(0) == 0)
    def _():
        fill_pair_weights(raw_ref, 0, w_ref)

    group, n = x_ref.shape[0], x_ref.shape[1]
    half = n // 2

    for g in range(group):
        x = x_ref[g].astype(F32)
        if rim_ref is not None:
            x = with_rims(x, [rim_ref[g, e].astype(F32) for e in range(4)], n, colbuf)
        fill_pairs(pairs, x, n)
        for q0, m in pair_chunks(n, ENC_PAIRS.get(n, 6)):
            acc = pair_sums(pairs, w_ref, q0, m, None)
            put_sums(acc, sums_ref, g, q0, m, n, colbuf)
            out = silu(acc).astype(BF)[:, 0:n]
            y_ref[g, q0 : q0 + m, 0] = out[:, :, 0:128]
            y_ref[g, q0 : q0 + m, 1] = out[:, :, 128:256]
            wide = out.astype(F32)
            if q0 == 0:
                ring_ref[g, 0] = out[0, :, 128:256]
            if q0 + m == half:
                ring_ref[g, 2] = out[m - 1, :, 0:128]
            ringbuf[1, 2 * q0 : 2 * q0 + 2 * m] = column_of(wide, m, n - 8, 6, colbuf)
            ringbuf[0, 2 * q0 : 2 * q0 + 2 * m] = column_of(wide, m, 0, 1, colbuf)
            both = wide[:, :, 0:128] + wide[:, :, 128:256]
            sumbuf[...] = both.reshape(m * n, 128)
            small = sumbuf[pl.ds(0, m * half, 2), :] + sumbuf[pl.ds(1, m * half, 2), :]
            s_ref[g, q0 : q0 + m] = (small * 0.25).reshape(m, half, 128).astype(BF)
        ring_ref[g, 1] = ringbuf[1].astype(BF)
        ring_ref[g, 3] = ringbuf[0].astype(BF)


def dec_kernel(coarse_rims, *refs):
    refs = list(refs)
    x_ref, rim_ref, u_ref = refs.pop(0), refs.pop(0), refs.pop(0)
    urim_ref = refs.pop(0) if coarse_rims else None
    raw_ref = refs.pop(0)
    y_ref, sums_ref, pairs, rows, colbuf, acc_ref, w_ref, wu_ref = refs
    group, n = y_ref.shape[0], y_ref.shape[3]
    half = n // 2

    @pl.when(pl.program_id(0) == 0)
    def _():
        fill_pair_weights(raw_ref, 128, w_ref)
        fill_coarse_weights(raw_ref, wu_ref)

    for g in range(group):
        u = u_ref[g].astype(F32)
        if urim_ref is not None:
            u = with_rims(u, [urim_ref[g, e].astype(F32) for e in range(4)], half, colbuf.at[0 : half * 8])
        (fill_row_pairs if in_pairs(half) else fill_rows)(rows, u, half)
        x = with_rims(x_ref[g].astype(F32), [rim_ref[g, e].astype(F32) for e in range(4)], n, colbuf)
        fill_pairs(pairs, x, n)
        for q0, m in pair_chunks(n, DEC_PAIRS.get(n, 6)):
            for b in range(2):
                acc = None
                for k in range(3):
                    lhs, hp = coarse_lhs(rows, half, q0 + k, m, slice(b * 128, b * 128 + 256))
                    part = jnp.dot(lhs, wu_ref[b, k], preferred_element_type=F32)
                    acc = part if acc is None else acc + part
                acc = acc.reshape(m, hp, 256)
                for i in range(m):
                    for p in range(2):
                        acc_ref[p, i, pl.ds(b, half, 2), :] = acc[i, 0:half, p * 128 : p * 128 + 128]
            extra = jnp.concatenate([acc_ref[0], acc_ref[1]], axis=2)
            acc = pair_sums(pairs, w_ref, q0, m, extra)
            put_sums(acc, sums_ref, g, q0, m, n, colbuf)
            out = silu(acc).astype(BF)[:, 0:n]
            y_ref[g, q0 : q0 + m, 0] = out[:, :, 0:128]
            y_ref[g, q0 : q0 + m, 1] = out[:, :, 128:256]


def last_kernel(pick_ref, recv_ref, own_ref, sum_ref, x_ref, y_ref, *scratch):
    rim_ref, edge_buf, slab_ref, colbuf, in_sem, out_sem, row_sem = scratch
    del x_ref
    strips, n = own_ref.shape[0], own_ref.shape[1]
    tiles = strips // 4
    parts = in_sem.shape[1]
    span = tiles // parts

    def slab(side, part):
        return y_ref.at[pl.ds(part * span, span), :, pl.ds(side * (n - 16), 16), :]

    def held(side, part):
        return slab_ref.at[side, pl.ds(part * span, span)]

    reads = [
        [pltpu.make_async_copy(slab(side, p), held(side, p), in_sem.at[side, p]) for p in range(parts)]
        for side in range(2)
    ]
    for p in range(parts):
        for side in range(2):
            reads[side][p].start()

    end = n - 1

    def finish(t, k):
        con = [incoming(pick_ref, recv_ref, own_ref, t * 4 + e) for e in range(4)]
        for e in range(4):
            edge_buf[k, e] = sum_ref[t * 4 + e] + con[e]
        for e, cell, other, at in corners(end):
            cells = slice(cell, cell + 1)
            edge_buf[k, e, cells] = edge_buf[k, e, cells] + con[other][at : at + 1]
        for e in range(4):
            rim_ref[t, e] = silu(edge_buf[k, e]).astype(BF)

    each_tile(tiles, finish)

    rows = [
        pltpu.make_async_copy(
            rim_ref.at[:, e, pl.ds(16, n - 32), :], y_ref.at[:, row, pl.ds(16, n - 32), :], row_sem.at[j]
        )
        for j, (e, row) in enumerate(((0, 0), (2, n - 1)))
    ]
    for copy in rows:
        copy.start()

    sub = lax.broadcasted_iota(jnp.int32, (n, 8, 128), 1)

    def patch(side, t):
        lo = 0 if side == 0 else n - 16
        near = slice(0, 8) if side == 0 else slice(8, 16)
        far = slice(8, 16) if side == 0 else slice(0, 8)
        x = slab_ref[side, t].astype(F32)
        cells = spread_columns(rim_ref[t, 3 if side == 0 else 1].astype(F32), n, 0 if side == 0 else 7, colbuf)
        new = jnp.where(sub == (0 if side == 0 else 7), cells, x[:, near])
        both = [new, x[:, far]] if side == 0 else [x[:, far], new]
        slab_ref[side, t] = jnp.concatenate(both, axis=1).astype(BF)
        slab_ref[side, t, 0] = rim_ref[t, 0, lo : lo + 16]
        slab_ref[side, t, n - 1] = rim_ref[t, 2, lo : lo + 16]

    writes = []
    for p in range(parts):
        for side in range(2):
            reads[side][p].wait()

            def step(t, carry, side=side):
                patch(side, t)
                return carry

            lax.fori_loop(p * span, p * span + span, step, 0)
            copy = pltpu.make_async_copy(held(side, p), slab(side, p), out_sem.at[side, p])
            copy.start()
            writes.append(copy)
    for copy in writes + rows:
        copy.wait()


def last_step(x, plan, recv, own, sums):
    tiles, n, _, c = x.shape
    strips = own.shape[0]
    parts = 4 if tiles % 4 == 0 else 1
    smem = pl.BlockSpec(memory_space=pltpu.SMEM)
    vmem = pl.BlockSpec(memory_space=pltpu.VMEM)
    anywhere = pl.BlockSpec(memory_space=pl.ANY)
    return pl.pallas_call(
        last_kernel,
        in_specs=[smem, vmem, vmem, vmem, anywhere],
        out_specs=anywhere,
        out_shape=jax.ShapeDtypeStruct(x.shape, BF),
        scratch_shapes=[
            pltpu.VMEM((tiles, 4, n, c), BF),
            pltpu.VMEM((group_of(tiles, 3), 4, n, c), F32),
            pltpu.VMEM((2, tiles, n, 16, c), BF),
            pltpu.VMEM((n * 8, c), F32),
            pltpu.SemaphoreType.DMA((2, parts)),
            pltpu.SemaphoreType.DMA((2, parts)),
            pltpu.SemaphoreType.DMA((2,)),
        ],
        input_output_aliases={4: 0},
        compiler_params=params(),
        name="last_step",
    )(plan[0][0], recv, own, sums, x)


def group_of(tiles, want):
    return max(g for g in range(1, want + 1) if tiles % g == 0)


def tile_spec(group, *dims):
    return pl.BlockSpec((group,) + dims, lambda i: (i,) + (0,) * len(dims))


def whole_spec(shape):
    return pl.BlockSpec(shape, lambda i: (0,) * len(shape))


def enc_conv(x, rim, w, want):
    tiles, n, _, c = x.shape
    half, n_p = n // 2, up16(n)
    g = group_of(tiles, want)
    m = pair_chunks(n, ENC_PAIRS.get(n, 6))[0][1]
    args, specs = [x, w.reshape(9, c, c)], [tile_spec(g, n, n, c), whole_spec((9, c, c))]
    if rim is not None:
        args.append(rim.reshape(tiles, 4, n, c))
        specs.append(tile_spec(g, 4, n, c))
    y, sums, ring, s = pl.pallas_call(
        enc_kernel,
        grid=(tiles // g,),
        in_specs=specs,
        out_specs=[
            tile_spec(g, half, 2, n, c), tile_spec(g, 4, n, c), tile_spec(g, 4, n, c), tile_spec(g, half, half, c)
        ],
        out_shape=[
            jax.ShapeDtypeStruct((tiles, half, 2, n, c), BF),
            jax.ShapeDtypeStruct((tiles, 4, n, c), F32),
            jax.ShapeDtypeStruct((tiles, 4, n, c), BF),
            jax.ShapeDtypeStruct((tiles, half, half, c), BF),
        ],
        scratch_shapes=[
            pltpu.VMEM((half + 1, n_p, 768), BF),
            pltpu.VMEM((n * 8, 128), F32),
            pltpu.VMEM((m * n, 128), F32),
            pltpu.VMEM((2, n, 128), F32),
            pltpu.VMEM((1536, 256), BF),
        ],
        compiler_params=params(),
        cost_estimate=pl.CostEstimate(
            flops=tiles * n * n * 2 * 1536 * 128, bytes_accessed=tiles * n * n * 600, transcendentals=tiles * n * n * 128
        ),
        name="enc_conv",
    )(*args)
    strips = lambda a: a.reshape(tiles * 4, n, c)
    return y.reshape(tiles, n, n, c), strips(sums), strips(ring), s


def dec_conv(x, rim, u, urim, w, want):
    tiles, n, _, c = x.shape
    half, n_p = n // 2, up16(n)
    g = group_of(tiles, want)
    m = pair_chunks(n, DEC_PAIRS.get(n, 6))[0][1]
    args = [x, rim.reshape(tiles, 4, n, c), u]
    specs = [tile_spec(g, n, n, c), tile_spec(g, 4, n, c), tile_spec(g, half, half, c)]
    if urim is not None:
        args.append(urim.reshape(tiles, 4, half, c))
        specs.append(tile_spec(g, 4, half, c))
    args.append(w.reshape(9, 2 * c, c))
    specs.append(whole_spec((9, 2 * c, c)))
    rows = (half + 1, 2 * half, 384) if in_pairs(half) else (half + 2, up16(half), 384)

    def kernel(*refs):
        dec_kernel(urim is not None, *refs)

    y, sums = pl.pallas_call(
        kernel,
        grid=(tiles // g,),
        in_specs=specs,
        out_specs=[tile_spec(g, half, 2, n, c), tile_spec(g, 4, n, c)],
        out_shape=[
            jax.ShapeDtypeStruct((tiles, half, 2, n, c), BF),
            jax.ShapeDtypeStruct((tiles, 4, n, c), F32),
        ],
        scratch_shapes=[
            pltpu.VMEM((half + 1, n_p, 768), BF),
            pltpu.VMEM(rows, BF),
            pltpu.VMEM((n * 8, 128), F32),
            pltpu.VMEM((2, m, n_p, 128), F32),
            pltpu.VMEM((1536, 256), BF),
            pltpu.VMEM((2, 3, 256, 256), BF),
        ],
        compiler_params=params(),
        cost_estimate=pl.CostEstimate(
            flops=tiles * n * n * 2 * 2300 * 128, bytes_accessed=tiles * n * n * 600, transcendentals=tiles * n * n * 128
        ),
        name="dec_conv",
    )(*args)
    return y.reshape(x.shape), sums.reshape(tiles * 4, n, c)


def strips_of(field, ring=0):
    n = field.shape[1]
    far = n - 1 - ring
    out = jnp.stack([field[:, ring], field[:, :, far], field[:, far], field[:, :, ring]], axis=1)
    out = jnp.pad(out, ((0, 0), (0, 0), (0, strip_rows(n) - n), (0, 0)))
    return out.reshape(field.shape[0] * 4, strip_rows(n), field.shape[3])


def patched(field, rim):
    tiles, n, _, c = field.shape
    rim = rim.reshape(tiles, 4, -1, c)[:, :, :n]
    middle = jnp.concatenate(
        [rim[:, 3, 1 : n - 1, None], field[:, 1 : n - 1, 1 : n - 1], rim[:, 1, 1 : n - 1, None]], axis=2
    )
    return jnp.concatenate([rim[:, 0][:, None], middle, rim[:, 2][:, None]], axis=1)


def inner_sums(field, weight):
    return lax.conv_general_dilated(
        field,
        weight,
        (1, 1),
        ((1, 1), (1, 1)),
        dimension_numbers=("NHWC", "HWIO", "NHWC"),
        preferred_element_type=F32,
    )


def shrink(field):
    count, length, _, channels = field.shape
    blocks = field.astype(F32).reshape(count, length // 2, 2, length // 2, 2, channels)
    return (jnp.sum(blocks, axis=(2, 4)) * 0.25).astype(BF)


def enlarge(field):
    return jnp.repeat(jnp.repeat(field, 2, axis=1), 2, axis=2)


def per_device(features, edge_table, w_enc0, w_enc1, w_enc2, w_mid, w_dec2, w_dec1, w_dec0):
    tiles, n0 = features.shape[0], features.shape[1]
    devices = lax.axis_size("tile")
    position = lax.axis_index("tile")
    cap = pair_capacity(FACE_TILES, tiles)
    rows = devices * cap
    slot_row = send_slots(edge_table, position, tiles, cap)

    def trade(strips):
        out = lax.all_to_all(strips.reshape(devices, -1, 128), "tile", split_axis=0, concat_axis=0, tiled=True)
        return out.reshape(strips.shape)

    def step(n, *args, **kw):
        return rim_step(n, devices, cap, plan, *args, **kw)

    def after(value, token):
        return lax.optimization_barrier((value, token))[0]

    rim0, send = tile_rims(features, slot_row, rows)
    rim0 = rim0.reshape(tiles * 4, n0, 128)
    plan = receive_plan(after(edge_table, send), slot_row, position, tiles, cap, devices)
    recv = trade(send)
    enc0, sums, ring, x1 = enc_conv(features, None, w_enc0, 1)
    enc0_rim, x1_rim, send = step(n0, recv, rim0, sums, w=w_enc0, ring=ring)

    recv = trade(send)
    enc1, sums, ring, x2 = enc_conv(x1, x1_rim, w_enc1, 4)
    enc1_rim, x2_rim, send = step(n0 // 2, recv, x1_rim, sums, w=w_enc1, ring=ring)

    recv = trade(send)
    sums = inner_sums(patched(x2, x2_rim), w_enc2)
    enc2 = jax.nn.silu(sums).astype(BF)
    enc2_rim, x3_rim, send = step(
        n0 // 4, recv, x2_rim, strips_of(sums), w=w_enc2, ring=strips_of(enc2, 1)
    )

    recv = trade(send)
    sums = inner_sums(patched(shrink(enc2), x3_rim), w_mid)
    middle = jax.nn.silu(sums).astype(BF)
    skip2 = skip_step(n0 // 4, plan, enc2_rim, w_dec2)
    skip0 = skip_step(n0, plan, after(enc0_rim, x3_rim), w_dec0)
    sums, skip0 = lax.optimization_barrier((sums, skip0))
    mid_rim, own, send = step(
        n0 // 8, recv, x3_rim, strips_of(sums), w=w_mid,
        skip=skip2, wn=w_dec2,
    )

    recv = trade(send)
    joined = jnp.concatenate([enlarge(patched(middle, mid_rim)), patched(enc2, enc2_rim)], axis=3)
    sums = inner_sums(joined, w_dec2)
    dec2 = jax.nn.silu(sums).astype(BF)
    skip1 = skip_step(n0 // 2, plan, after(enc1_rim, mid_rim), w_dec1)
    dec2_rim, own, send = step(
        n0 // 4, recv, own, strips_of(sums), skip=skip1, wn=w_dec1
    )

    recv = trade(send)
    dec1, sums = dec_conv(enc1, enc1_rim, patched(dec2, dec2_rim), None, w_dec1, 4)
    dec1_rim, own, send = step(
        n0 // 2, recv, own, sums, skip=skip0, wn=w_dec0
    )

    recv = trade(send)
    dec0, sums = dec_conv(enc0, enc0_rim, dec1, dec1_rim, w_dec0, 1)
    return last_step(dec0, plan, recv, own, sums)


def solution(mesh):
    return jax.shard_map(
        per_device,
        mesh=mesh,
        in_specs=(P(("grp", "tile"), None, None, None), P(), P(), P(), P(), P(), P(), P(), P()),
        out_specs=P(("grp", "tile"), None, None, None),
        check_vma=False,
    )
```

```python
import jax
import jax.numpy as jnp
import numpy as np
from jax import lax
from jax.experimental import pallas as pl
from jax.experimental.pallas import tpu as pltpu
from jax.sharding import PartitionSpec as P

FACE_TILES = 8
RIM_TILES = 12
SIDE = 4
VMEM_LIMIT = 50 * 2**20
BF = jnp.bfloat16
F32 = jnp.float32


def cube_links(tiles_side):
    basis = np.eye(3, dtype=np.int64)
    frames = []
    for axis_id in range(3):
        for orient in (1, -1):
            frames.append(
                (orient * basis[axis_id], basis[(axis_id + 1) % 3], basis[(axis_id + 2) % 3])
            )
    per_face = tiles_side * tiles_side
    tile_total = 6 * per_face
    centres = np.zeros((tile_total, 3), np.int64)
    lookup = {}
    for face_id in range(6):
        normal, row_axis, col_axis = frames[face_id]
        for row_id in range(tiles_side):
            for col_id in range(tiles_side):
                slot_id = face_id * per_face + row_id * tiles_side + col_id
                centre = (
                    tiles_side * normal
                    + (2 * row_id + 1 - tiles_side) * row_axis
                    + (2 * col_id + 1 - tiles_side) * col_axis
                )
                centres[slot_id] = centre
                lookup[tuple((int(entry) for entry in centre))] = slot_id
    partner = np.zeros((tile_total, 4), np.int64)
    for slot_id in range(tile_total):
        normal, row_axis, col_axis = frames[slot_id // per_face]
        outward = (-row_axis, col_axis, row_axis, -col_axis)
        for edge_id in range(4):
            beyond = tuple((int(entry) for entry in centres[slot_id] + 2 * outward[edge_id]))
            if beyond in lookup:
                partner[slot_id, edge_id] = lookup[beyond]
            else:
                partner[slot_id, edge_id] = lookup[
                    tuple((int(entry) for entry in centres[slot_id] + outward[edge_id] - normal))
                ]
    return partner


def pair_capacity(tiles_side, tiles_here):
    partner = cube_links(tiles_side)
    tile_total = partner.shape[0]
    blocks = tile_total // tiles_here
    source = np.repeat(np.arange(tile_total) // tiles_here, 4)
    target = partner.reshape(-1) // tiles_here
    identity = np.eye(blocks, dtype=np.int64)
    shared = identity[source].T @ identity[target]
    shared = shared * (1 - identity)
    return max(int(shared.max()), 1)


def own_strips(edge_table, position, tiles_here):
    rows = lax.dynamic_slice_in_dim(edge_table, position * tiles_here, tiles_here, 0)
    rows = rows.reshape(tiles_here * 4, 2)
    return rows[:, 0], rows[:, 1] // 2, rows[:, 1] % 2


def send_slots(edge_table, position, tiles_here, slot_count):
    partner, _, _ = own_strips(edge_table, position, tiles_here)
    target = partner // tiles_here
    order = jnp.arange(tiles_here * 4, dtype=jnp.int32)
    earlier = (order[None, :] < order[:, None]) & (target[None, :] == target[:, None])
    slot_rank = jnp.sum(earlier.astype(jnp.int32), axis=1)
    return jnp.where(target != position, target * slot_count + slot_rank, -1)


def listed(mask):
    order = jnp.arange(mask.shape[0], dtype=jnp.int32)
    rank = jnp.sum((mask[None, :] & (order[None, :] < order[:, None])).astype(jnp.int32), axis=1)
    hit = mask[None, :] & (rank[None, :] == order[:, None])
    found = jnp.sum(jnp.where(hit, order[None, :], 0), axis=1)
    total = jnp.sum(mask.astype(jnp.int32), keepdims=True)
    found = jnp.where(order < total, found, mask.shape[0])
    return jnp.concatenate([found, jnp.full((3,), mask.shape[0], jnp.int32), total])


def receive_plan(edge_table, slot_row, position, tiles_here, slot_count, devices):
    strip_count = tiles_here * 4
    partner, matching, reversed_rows = own_strips(edge_table, position, tiles_here)
    target = partner // tiles_here
    order = jnp.arange(strip_count, dtype=jnp.int32)
    remote = target != position
    wanted = partner % tiles_here * 4 + matching
    toward_me = edge_table[:, :, 0].reshape(devices, strip_count) // tiles_here == position
    before = (order[:, None] < order[None, :]).astype(BF)
    ranks = jnp.dot(toward_me.astype(BF), before, preferred_element_type=F32).astype(BF)
    blocks = jnp.arange(devices, dtype=jnp.int32)
    from_target = (target[:, None] == blocks[None, :]).astype(BF)
    their_ranks = jnp.dot(from_target, ranks, preferred_element_type=F32)
    recv_rank = jnp.sum(jnp.where(wanted[:, None] == order[None, :], their_ranks, 0.0), axis=1).astype(jnp.int32)
    pick_row = lambda count: jnp.where(remote, target * count + recv_rank, devices * count + wanted)
    odd = (matching != (order + 2) % 4) | (reversed_rows == 1)
    one_more = lambda a: jnp.concatenate([a, jnp.zeros((1,), jnp.int32)])
    even = (slot_count + 1) // 2 * 2
    paired_slot = slot_row + target * (even - slot_count)
    shared = (one_more(reversed_rows), one_more(matching), listed(remote), listed(odd))
    return (pick_row(slot_count), pick_row(even)), (slot_row, paired_slot), shared


def up16(n):
    return (n + 15) // 16 * 16


def strip_rows(n):
    return {6: 8, 12: 16}.get(n, n)


def two_up(rows):
    return rows == 16


def send_shape(devices, cap, rows):
    return (devices * ((cap + 1) // 2), 24) if two_up(rows) else (devices * cap, rows)


def params():
    return pltpu.CompilerParams(vmem_limit_bytes=VMEM_LIMIT)


def rims_kernel(slot_ref, lo_ref, hi_ref, top_ref, bottom_ref, out_ref, send_ref, colbuf):
    group, n = lo_ref.shape[0], lo_ref.shape[1]
    first = pl.program_id(0) * group * 4
    for g in range(group):
        colbuf[...] = lo_ref[g, :, 0:8, :].astype(F32).reshape(n * 8, 128)
        left = colbuf[pl.ds(0, n, 8), :]
        colbuf[...] = hi_ref[g, :, 8:16, :].astype(F32).reshape(n * 8, 128)
        right = colbuf[pl.ds(7, n, 8), :]
        out_ref[g, 0] = top_ref[g, 0]
        out_ref[g, 1] = right.astype(BF)
        out_ref[g, 2] = bottom_ref[g, 0]
        out_ref[g, 3] = left.astype(BF)
    for g in range(group):
        for e in range(4):
            slot = slot_ref[first + g * 4 + e]

            @pl.when(slot >= 0)
            def _():
                send_ref[slot] = out_ref[g, e]


def tile_rims(x, slot_row, rows):
    tiles, n, _, c = x.shape
    g = group_of(tiles, RIM_TILES)
    last = n // 16 - 1
    return pl.pallas_call(
        rims_kernel,
        grid=(tiles // g,),
        in_specs=[
            pl.BlockSpec(memory_space=pltpu.SMEM),
            pl.BlockSpec((g, n, 16, c), lambda i: (i, 0, 0, 0)),
            pl.BlockSpec((g, n, 16, c), lambda i: (i, 0, last, 0)),
            pl.BlockSpec((g, 1, n, c), lambda i: (i, 0, 0, 0)),
            pl.BlockSpec((g, 1, n, c), lambda i: (i, n - 1, 0, 0)),
        ],
        out_specs=[tile_spec(g, 4, n, c), whole_spec((rows, n, c))],
        out_shape=[
            jax.ShapeDtypeStruct((tiles, 4, n, c), BF),
            jax.ShapeDtypeStruct((rows, n, c), BF),
        ],
        scratch_shapes=[pltpu.VMEM((n * 8, 128), F32)],
        compiler_params=params(),
        name="tile_rims",
    )(slot_row, x, x, x, x)


def silu(s):
    half = s * 0.5
    return half + half * jnp.tanh(half)


def strip_shifts(h, n):
    rows = h.shape[0]
    row = lax.broadcasted_iota(jnp.int32, h.shape, 0)
    half = h * 0.5
    down = jnp.where(row == 0, half, pltpu.roll(h, 1, 0))
    up = jnp.where(row == n - 1, half, pltpu.roll(h, rows - 1, 0))
    return down, up


def flip_matrices(rows, n):
    ri = lax.broadcasted_iota(jnp.int32, (rows, rows), 0)
    ci = lax.broadcasted_iota(jnp.int32, (rows, rows), 1)
    return (ri + ci == n - 1).astype(F32), (ri == ci).astype(F32)


def put_shifts(ref, index, lane, h, n):
    down, up = strip_shifts(h, n)
    for s, part in enumerate((down, h, up)):
        ref[index + (slice(None), slice(lane + s * 128, lane + s * 128 + 128))] = part.astype(ref.dtype)


def each_tile(tiles, body):
    side = group_of(tiles, SIDE)

    def step(i, carry):
        for k in range(side):
            body(i * side + k, k)
        return carry

    lax.fori_loop(0, tiles // side, step, 0)


def each_listed(list_ref, body):
    def step(j, carry):
        body(list_ref[j])
        return carry

    lax.fori_loop(0, list_ref[list_ref.shape[0] - 1], step, 0)


def each_four(list_ref, body):
    def step(j, carry):
        body([list_ref[j * 4 + k] for k in range(4)])
        return carry

    lax.fori_loop(0, (list_ref[list_ref.shape[0] - 1] + 3) // 4, step, 0)


def turned(rev_ref, i, h, flip, keep):
    order = jnp.where(rev_ref[i] == 1, flip, keep).astype(BF)
    return jnp.dot(order, h.astype(BF), preferred_element_type=F32)


def incoming(pick_ref, recv_ref, own_ref, i):
    paired = own_ref.shape[1] != recv_ref.shape[1]
    slots = recv_ref.shape[0] * (2 if paired else 1)
    pick = pick_ref[i]
    away = pick < slots
    slot = jnp.minimum(pick, slots - 1)
    b = own_ref[jnp.maximum(pick - slots, 0)].astype(F32)
    if not paired:
        return jnp.where(away, recv_ref[slot].astype(F32), b)
    a = recv_ref[slot >> 1].astype(F32)
    row = lax.broadcasted_iota(jnp.int32, (16, 128), 0)
    a = jnp.where(row < 12, jnp.where((slot & 1) == 1, pltpu.roll(a, 12, 0), a)[0:16], 0.0)
    return jnp.where(away, a, b)


def edge_taps(w_ref, e, lo):
    taps = ((0, 1, 2), (2, 5, 8), (6, 7, 8), (0, 3, 6))[e]
    return jnp.concatenate([w_ref[tap, lo : lo + 128, :] for tap in taps], axis=0)


def contributions(n, tiles, strip_of, w_ref, lo, rev_ref, edge_ref, odd_ref, lhs_ref, con_ref, taps_ref):
    lp = lhs_ref.shape[2]
    for e in range(4):
        taps_ref[e] = edge_taps(w_ref, e, lo)

    def fill(t, k):
        for f in range(4):
            put_shifts(lhs_ref, (f, t), 0, strip_of(f, t, k), n)

    each_tile(tiles, fill)
    for f in range(4):
        lhs = lhs_ref[f, 0:tiles].reshape(tiles * lp, 384).astype(BF)
        out = jnp.dot(lhs, taps_ref[(f + 2) % 4], preferred_element_type=F32)
        con_ref[f, 0:tiles] = out.reshape(tiles, lp, 128)
    flip, keep = flip_matrices(lp, n)

    def odd_ones(four):
        halos = [lhs_ref[i % 4, i // 4, :, 128:256] for i in four]
        halos = [turned(rev_ref, i, h, flip, keep) for i, h in zip(four, halos)]
        taps = [taps_ref[edge_ref[i]] for i in four]
        sums = []
        for h, tap in zip(halos, taps):
            down, up = strip_shifts(h, n)
            lhs = jnp.concatenate([down.astype(BF), h.astype(BF), up.astype(BF)], axis=1)
            sums.append(jnp.dot(lhs, tap, preferred_element_type=F32))
        for i, total in zip(four, sums):
            con_ref[i % 4, i // 4] = total

    each_four(odd_ref, odd_ones)


def skip_kernel(n, rev_ref, edge_ref, odd_ref, rim_ref, w_ref, out_ref, lhs_ref, con_ref, taps_ref):
    tiles = rim_ref.shape[0] // 4
    contributions(
        n, tiles, lambda f, t, k: rim_ref[t * 4 + f].astype(F32), w_ref, 128,
        rev_ref, edge_ref, odd_ref, lhs_ref, con_ref, taps_ref,
    )

    def put(t, k):
        for f in range(4):
            out_ref[t * 4 + f] = con_ref[f, t]

    each_tile(tiles, put)


def wide(rows):
    return BF if rows % 16 == 0 else F32


def skip_step(n, plan, rim, w):
    strips, lp, c = rim.shape
    smem = pl.BlockSpec(memory_space=pltpu.SMEM)
    vmem = pl.BlockSpec(memory_space=pltpu.VMEM)
    return pl.pallas_call(
        lambda *refs: skip_kernel(n, *refs),
        in_specs=[smem, smem, smem, vmem, vmem],
        out_specs=vmem,
        out_shape=jax.ShapeDtypeStruct((strips, lp, c), F32),
        scratch_shapes=[
            pltpu.VMEM((4, strips // 4 + 1, lp, 384), wide(lp)),
            pltpu.VMEM((4, strips // 4 + 1, lp, 128), F32),
            pltpu.VMEM((4, 384, 128), BF),
        ],
        compiler_params=params(),
        cost_estimate=pl.CostEstimate(flops=strips * lp * 2 * 384 * 256, bytes_accessed=strips * lp * 768, transcendentals=0),
        name="skip_step",
    )(plan[2][0], plan[2][1], plan[2][3], rim, w.reshape(9, -1, c))


def corners(end):
    return (
        (0, 0, 3, 0), (0, end, 1, 0), (2, 0, 3, end), (2, end, 1, end),
        (3, 0, 0, 0), (3, end, 2, 0), (1, 0, 0, end), (1, end, 2, end),
    )


def rim_kernel(n, strips_in, nxt, refs):
    it = iter(refs)
    pick_ref, rev_ref, slot_ref, edge_ref, remote_ref, odd_ref = [next(it) for _ in range(6)]
    recv_ref, own_ref, sum_ref = next(it), next(it), next(it)
    w_ref = next(it) if strips_in else None
    ring_ref = next(it) if nxt == "shrink" else None
    skip_ref, wn_ref = (next(it), next(it)) if nxt == "halo" else (None, None)
    rim_ref, next_ref, send_ref = next(it), next(it), next(it)
    lhs_ref, con_ref = next(it), next(it)
    edge_buf, ring_buf, sum_buf, out_buf = next(it), next(it), next(it), next(it)
    lhsn_ref, conn_ref, taps_ref, big_buf = [next(it) for _ in range(4)] if nxt == "halo" else [None] * 4

    strips, lp = own_ref.shape[0], own_ref.shape[1]
    tiles = strips // 4
    flip, keep = flip_matrices(lp, n)

    if strips_in:

        def fill(t, k):
            for e in range(4):
                put_shifts(lhs_ref, (e, t), 0, incoming(pick_ref, recv_ref, own_ref, t * 4 + e), n)

        each_tile(tiles, fill)

        def turn(four):
            halos = [lhs_ref[i % 4, i // 4, :, 128:256] for i in four]
            halos = [turned(rev_ref, i, h, flip, keep) for i, h in zip(four, halos)]
            for i, h in zip(four, halos):
                put_shifts(lhs_ref, (i % 4, i // 4), 0, h, n)

        each_four(odd_ref, turn)
        for e in range(4):
            lhs = lhs_ref[e, 0:tiles].reshape(tiles * lp, 384).astype(BF)
            out = jnp.dot(lhs, edge_taps(w_ref, e, 0), preferred_element_type=F32)
            con_ref[e] = out.reshape(tiles, lp, 128)

    end = n - 1
    joints = (
        (0, 0, 3, 1), (0, end, 1, 1), (2, 0, 3, end - 1), (2, end, 1, end - 1),
        (3, 0, 0, 1), (3, end, 2, 1), (1, 0, 0, end - 1), (1, end, 2, end - 1),
    )
    if nxt == "shrink":
        out_buf[...] = jnp.zeros_like(out_buf)

    def finish(t, k):
        if strips_in:
            con = [con_ref[e, t] for e in range(4)]
        else:
            con = [incoming(pick_ref, recv_ref, own_ref, t * 4 + e) for e in range(4)]
        for e in range(4):
            edge_buf[k, e] = sum_ref[t * 4 + e] + con[e]
        for e, cell, other, at in corners(end):
            cells = slice(cell, cell + 1)
            edge_buf[k, e, cells] = edge_buf[k, e, cells] + con[other][at : at + 1]
        for e in range(4):
            y = silu(edge_buf[k, e]).astype(BF)
            rim_ref[t * 4 + e] = y
            edge_buf[k, e] = y.astype(F32)
        if nxt == "shrink":
            for e in range(4):
                ring_buf[k, e] = ring_ref[t * 4 + e].astype(F32)
            for e, cell, other, at in joints:
                ring_buf[k, e, cell : cell + 1] = edge_buf[k, other, at : at + 1]
            for e in range(4):
                sum_buf[k, e] = edge_buf[k, e] + ring_buf[k, e]
                small = sum_buf[k, e, pl.ds(0, lp // 2, 2), :] + sum_buf[k, e, pl.ds(1, lp // 2, 2), :]
                out_buf[k, e, 0 : lp // 2] = small * 0.25
                next_ref[t * 4 + e] = out_buf[k, e].astype(BF)

    each_tile(tiles, finish)

    if nxt == "halo":
        half = big_buf.shape[2] // 2

        def enlarged(f, t, k):
            rim = rim_ref[t * 4 + f].astype(F32)[0:half]
            big_buf[k, f, pl.ds(0, half, 2), :] = rim
            big_buf[k, f, pl.ds(1, half, 2), :] = rim
            return big_buf[k, f]

        contributions(
            2 * n, tiles, enlarged, wn_ref, 0,
            rev_ref, edge_ref, odd_ref, lhsn_ref, conn_ref, taps_ref,
        )

        def put(t, k):
            for f in range(4):
                next_ref[t * 4 + f] = (conn_ref[f, t] + skip_ref[t * 4 + f]).astype(BF)

        each_tile(tiles, put)

    def send(i):
        slot = slot_ref[i]
        if next_ref.shape[1] == send_ref.shape[1]:
            send_ref[slot] = next_ref[i]
        else:
            block, second = slot >> 1, (slot & 1) == 1
            strip = jnp.concatenate([next_ref[i].astype(F32), jnp.zeros((8, 128), F32)], axis=0)
            row = lax.broadcasted_iota(jnp.int32, (24, 128), 0)
            held = send_ref[block].astype(F32)
            both = jnp.where(second, jnp.where(row < 12, held, pltpu.roll(strip, 12, 0)), jnp.where(row < 12, strip, held))
            send_ref[block] = both.astype(BF)

    each_listed(remote_ref, send)


def rim_step(n, devices, cap, plan, recv, own, sums, w=None, ring=None, skip=None, wn=None):
    strips, lp, c = own.shape
    tiles = strips // 4
    side = group_of(tiles, SIDE)
    nxt = "shrink" if ring is not None else "halo"
    smem = pl.BlockSpec(memory_space=pltpu.SMEM)
    vmem = pl.BlockSpec(memory_space=pltpu.VMEM)
    w = w if w is None else w.reshape(9, -1, c)
    wn = wn if wn is None else wn.reshape(9, -1, c)
    args = [recv, own, sums] + [a for a in (w, ring, skip, wn) if a is not None]
    lo = strip_rows(n // 2) if nxt == "shrink" else strip_rows(2 * n)
    outs = [
        jax.ShapeDtypeStruct((strips, lp, c), BF),
        jax.ShapeDtypeStruct((strips, lo, c), BF),
        jax.ShapeDtypeStruct(send_shape(devices, cap, lo) + (c,), BF),
    ]
    scratch = [
        pltpu.VMEM((4, tiles + 1, lp, 384), wide(lp)),
        pltpu.VMEM((4, tiles, lp, 128), F32),
        pltpu.VMEM((side, 4, lp, 128), F32),
        pltpu.VMEM((side, 4, lp, 128), F32),
        pltpu.VMEM((side, 4, lp, 128), F32),
        pltpu.VMEM((side, 4, lo, 128), F32),
    ]
    if nxt == "halo":
        scratch += [
            pltpu.VMEM((4, tiles + 1, lo, 384), wide(lo)),
            pltpu.VMEM((4, tiles + 1, lo, 128), F32),
            pltpu.VMEM((4, 384, 128), BF),
            pltpu.VMEM((side, 4, lo, 128), F32),
        ]

    def kernel(*refs):
        rim_kernel(n, w is not None, nxt, refs)

    return pl.pallas_call(
        kernel,
        in_specs=[smem] * 6 + [vmem] * len(args),
        out_specs=[vmem] * len(outs),
        out_shape=outs,
        scratch_shapes=scratch,
        compiler_params=params(),
        cost_estimate=pl.CostEstimate(flops=strips * lp * 2 * 384 * 512, bytes_accessed=strips * lp * 1500, transcendentals=0),
        name="rim_step",
    )(plan[0][int(two_up(lp))], plan[2][0], plan[1][int(two_up(lo))], *plan[2][1:], *args)


def spread_columns(strip, n, sublane, buf):
    buf[pl.ds(sublane, n, 8), :] = strip
    return buf[...].reshape(n, 8, 128)


def with_rims(x, rim, n, buf):
    sub = lax.broadcasted_iota(jnp.int32, (n, 8, 128), 1)
    head = jnp.where(sub == 0, spread_columns(rim[3], n, 0, buf), x[:, 0:8])
    tail = jnp.where(sub == 7, spread_columns(rim[1], n, 7, buf), x[:, n - 8 : n])
    x = jnp.concatenate([head, x[:, 8 : n - 8], tail], axis=1)
    return jnp.concatenate([rim[0][None], x[1 : n - 1], rim[2][None]], axis=0)


def column_shifts(x, n):
    sub = lax.broadcasted_iota(jnp.int32, (x.shape[0], 8, 128), 1)
    down = pltpu.roll(x, 1, 1)
    up = pltpu.roll(x, n - 1, 1)
    down = jnp.concatenate([jnp.where(sub == 0, 0.0, down[:, 0:8]), down[:, 8:n]], axis=1)
    up = jnp.concatenate([up[:, 0 : n - 8], jnp.where(sub == 7, 0.0, up[:, n - 8 : n])], axis=1)
    return down, x, up


def fill_pairs(y_ref, x, n):
    half, n_p = n // 2, y_ref.shape[1]
    zero = jnp.zeros((n_p, 384), BF)
    y_ref[0, :, 0:384] = zero
    y_ref[half, :, 384:768] = zero
    for s, body in enumerate(column_shifts(x, n)):
        b = body.astype(BF).reshape(half, 2, n, 128)
        y_ref[0:half, 0:n, 384 + s * 128 : 384 + s * 128 + 128] = b[:, 0]
        y_ref[1 : half + 1, 0:n, s * 128 : s * 128 + 128] = b[:, 1]


def in_pairs(n):
    return n % 16 == 8 and n % 2 == 0


def fill_row_pairs(u_ref, x, n):
    half = n // 2
    zero = jnp.zeros((n, 384), BF)
    u_ref[0, 0:n] = zero
    u_ref[half, n : 2 * n] = zero
    for s, body in enumerate(column_shifts(x, n)):
        b = body.astype(BF).reshape(half, 2, n, 128)
        lanes = slice(s * 128, s * 128 + 128)
        u_ref[0:half, n : 2 * n, lanes] = b[:, 0]
        u_ref[1 : half + 1, 0:n, lanes] = b[:, 1]
        u_ref[half + 1 : n + 1, 0:n, lanes] = b[:, 0]
        u_ref[half + 1 : n + 1, n : 2 * n, lanes] = b[:, 1]


def coarse_lhs(u_ref, n, start, m, lanes):
    if in_pairs(n):
        at = start // 2 if start % 2 == 0 else n // 2 + 1 + start // 2
        return u_ref[at : at + m // 2, :, lanes].reshape(m * n, 256), n
    return u_ref[start : start + m, :, lanes].reshape(m * u_ref.shape[1], 256), u_ref.shape[1]


def fill_rows(u_ref, x, n):
    zero = jnp.zeros((u_ref.shape[1], 384), BF)
    u_ref[0] = zero
    u_ref[n + 1] = zero
    for s, body in enumerate(column_shifts(x, n)):
        u_ref[1 : n + 1, 0:n, s * 128 : s * 128 + 128] = body.astype(BF)


def pair_sums(y_ref, w_ref, q0, m, extra):
    n_p = y_ref.shape[1]
    a = y_ref[q0 : q0 + m].reshape(m * n_p, 768)
    b = y_ref[q0 + 1 : q0 + 1 + m].reshape(m * n_p, 768)
    acc = jnp.dot(a, w_ref[0:768, :], preferred_element_type=F32)
    acc = acc + jnp.dot(b, w_ref[768:1536, :], preferred_element_type=F32)
    acc = acc.reshape(m, n_p, 256)
    return acc if extra is None else acc + extra


def pair_chunks(n, most):
    half = n // 2
    m = max(m for m in range(1, most + 1) if half % m == 0)
    return [(q, m) for q in range(0, half, m)]


ENC_PAIRS = {48: 24}
DEC_PAIRS = {48: 12}


def column_of(acc, m, lo, sublane, colbuf):
    rows = jnp.stack([acc[:, lo : lo + 8, 0:128], acc[:, lo : lo + 8, 128:256]], axis=1)
    colbuf[0 : 16 * m] = rows.reshape(16 * m, 128)
    return colbuf[pl.ds(sublane, 2 * m, 8), :]


def put_sums(acc, sums_ref, g, q0, m, n, colbuf):
    cells = slice(2 * q0, 2 * q0 + 2 * m)
    if q0 == 0:
        sums_ref[g, 0] = acc[0, 0:n, 0:128]
    if q0 + m == n // 2:
        sums_ref[g, 2] = acc[m - 1, 0:n, 128:256]
    sums_ref[g, 3, cells] = column_of(acc, m, 0, 0, colbuf)
    sums_ref[g, 1, cells] = column_of(acc, m, n - 8, 7, colbuf)


def fill_pair_weights(raw_ref, lo, w_ref):
    for p in range(4):
        for col in range(3):
            at = slice((p * 3 + col) * 128, (p * 3 + col) * 128 + 128)
            for out in range(2):
                row = p - out
                tap = raw_ref[row * 3 + col, lo : lo + 128, :] if 0 <= row <= 2 else jnp.zeros((128, 128), BF)
                w_ref[at, out * 128 : out * 128 + 128] = tap


def fill_coarse_weights(raw_ref, w_ref):
    along = (((0,), (1, 2), ()), ((), (0, 1), (2,)))
    for b in range(2):
        for k in range(3):
            for slot in range(2):
                cols = along[b][slot + b]
                for out in range(2):
                    taps = [raw_ref[r * 3 + col, 0:128, :].astype(F32) for r in along[out][k] for col in cols]
                    total = sum(taps[1:], taps[0]) if taps else jnp.zeros((128, 128), F32)
                    w_ref[b, k, slot * 128 : slot * 128 + 128, out * 128 : out * 128 + 128] = total.astype(BF)


def enc_kernel(*refs):
    it = iter(refs[:-5])
    x_ref, raw_ref = next(it), next(it)
    rest = list(it)
    rim_ref = rest.pop(0) if len(rest) == 5 else None
    y_ref, sums_ref, ring_ref, s_ref = rest
    pairs, colbuf, sumbuf, ringbuf, w_ref = refs[-5:]

    @pl.when(pl.program_id(0) == 0)
    def _():
        fill_pair_weights(raw_ref, 0, w_ref)

    group, n = x_ref.shape[0], x_ref.shape[1]
    half = n // 2

    for g in range(group):
        x = x_ref[g].astype(F32)
        if rim_ref is not None:
            x = with_rims(x, [rim_ref[g, e].astype(F32) for e in range(4)], n, colbuf)
        fill_pairs(pairs, x, n)
        for q0, m in pair_chunks(n, ENC_PAIRS.get(n, 6)):
            acc = pair_sums(pairs, w_ref, q0, m, None)
            put_sums(acc, sums_ref, g, q0, m, n, colbuf)
            out = silu(acc).astype(BF)[:, 0:n]
            y_ref[g, q0 : q0 + m, 0] = out[:, :, 0:128]
            y_ref[g, q0 : q0 + m, 1] = out[:, :, 128:256]
            wide = out.astype(F32)
            if q0 == 0:
                ring_ref[g, 0] = out[0, :, 128:256]
            if q0 + m == half:
                ring_ref[g, 2] = out[m - 1, :, 0:128]
            ringbuf[1, 2 * q0 : 2 * q0 + 2 * m] = column_of(wide, m, n - 8, 6, colbuf)
            ringbuf[0, 2 * q0 : 2 * q0 + 2 * m] = column_of(wide, m, 0, 1, colbuf)
            both = wide[:, :, 0:128] + wide[:, :, 128:256]
            sumbuf[...] = both.reshape(m * n, 128)
            small = sumbuf[pl.ds(0, m * half, 2), :] + sumbuf[pl.ds(1, m * half, 2), :]
            s_ref[g, q0 : q0 + m] = (small * 0.25).reshape(m, half, 128).astype(BF)
        ring_ref[g, 1] = ringbuf[1].astype(BF)
        ring_ref[g, 3] = ringbuf[0].astype(BF)


def dec_kernel(coarse_rims, *refs):
    refs = list(refs)
    x_ref, rim_ref, u_ref = refs.pop(0), refs.pop(0), refs.pop(0)
    urim_ref = refs.pop(0) if coarse_rims else None
    raw_ref = refs.pop(0)
    y_ref, sums_ref, pairs, rows, colbuf, acc_ref, w_ref, wu_ref = refs
    group, n = y_ref.shape[0], y_ref.shape[3]
    half = n // 2

    @pl.when(pl.program_id(0) == 0)
    def _():
        fill_pair_weights(raw_ref, 128, w_ref)
        fill_coarse_weights(raw_ref, wu_ref)

    for g in range(group):
        u = u_ref[g].astype(F32)
        if urim_ref is not None:
            u = with_rims(u, [urim_ref[g, e].astype(F32) for e in range(4)], half, colbuf.at[0 : half * 8])
        (fill_row_pairs if in_pairs(half) else fill_rows)(rows, u, half)
        x = with_rims(x_ref[g].astype(F32), [rim_ref[g, e].astype(F32) for e in range(4)], n, colbuf)
        fill_pairs(pairs, x, n)
        for q0, m in pair_chunks(n, DEC_PAIRS.get(n, 6)):
            for b in range(2):
                acc = None
                for k in range(3):
                    lhs, hp = coarse_lhs(rows, half, q0 + k, m, slice(b * 128, b * 128 + 256))
                    part = jnp.dot(lhs, wu_ref[b, k], preferred_element_type=F32)
                    acc = part if acc is None else acc + part
                acc = acc.reshape(m, hp, 256)
                for i in range(m):
                    for p in range(2):
                        acc_ref[p, i, pl.ds(b, half, 2), :] = acc[i, 0:half, p * 128 : p * 128 + 128]
            extra = jnp.concatenate([acc_ref[0], acc_ref[1]], axis=2)
            acc = pair_sums(pairs, w_ref, q0, m, extra)
            put_sums(acc, sums_ref, g, q0, m, n, colbuf)
            out = silu(acc).astype(BF)[:, 0:n]
            y_ref[g, q0 : q0 + m, 0] = out[:, :, 0:128]
            y_ref[g, q0 : q0 + m, 1] = out[:, :, 128:256]


def last_kernel(pick_ref, recv_ref, own_ref, sum_ref, x_ref, y_ref, *scratch):
    rim_ref, edge_buf, slab_ref, colbuf, in_sem, out_sem, row_sem = scratch
    del x_ref
    strips, n = own_ref.shape[0], own_ref.shape[1]
    tiles = strips // 4
    parts = in_sem.shape[1]
    span = tiles // parts

    def slab(side, part):
        return y_ref.at[pl.ds(part * span, span), :, pl.ds(side * (n - 16), 16), :]

    def held(side, part):
        return slab_ref.at[side, pl.ds(part * span, span)]

    reads = [
        [pltpu.make_async_copy(slab(side, p), held(side, p), in_sem.at[side, p]) for p in range(parts)]
        for side in range(2)
    ]
    for p in range(parts):
        for side in range(2):
            reads[side][p].start()

    end = n - 1

    def finish(t, k):
        con = [incoming(pick_ref, recv_ref, own_ref, t * 4 + e) for e in range(4)]
        for e in range(4):
            edge_buf[k, e] = sum_ref[t * 4 + e] + con[e]
        for e, cell, other, at in corners(end):
            cells = slice(cell, cell + 1)
            edge_buf[k, e, cells] = edge_buf[k, e, cells] + con[other][at : at + 1]
        for e in range(4):
            rim_ref[t, e] = silu(edge_buf[k, e]).astype(BF)

    each_tile(tiles, finish)

    rows = [
        pltpu.make_async_copy(
            rim_ref.at[:, e, pl.ds(16, n - 32), :], y_ref.at[:, row, pl.ds(16, n - 32), :], row_sem.at[j]
        )
        for j, (e, row) in enumerate(((0, 0), (2, n - 1)))
    ]
    for copy in rows:
        copy.start()

    sub = lax.broadcasted_iota(jnp.int32, (n, 8, 128), 1)

    def patch(side, t):
        lo = 0 if side == 0 else n - 16
        near = slice(0, 8) if side == 0 else slice(8, 16)
        far = slice(8, 16) if side == 0 else slice(0, 8)
        x = slab_ref[side, t].astype(F32)
        cells = spread_columns(rim_ref[t, 3 if side == 0 else 1].astype(F32), n, 0 if side == 0 else 7, colbuf)
        new = jnp.where(sub == (0 if side == 0 else 7), cells, x[:, near])
        both = [new, x[:, far]] if side == 0 else [x[:, far], new]
        slab_ref[side, t] = jnp.concatenate(both, axis=1).astype(BF)
        slab_ref[side, t, 0] = rim_ref[t, 0, lo : lo + 16]
        slab_ref[side, t, n - 1] = rim_ref[t, 2, lo : lo + 16]

    writes = []
    for p in range(parts):
        for side in range(2):
            reads[side][p].wait()

            def step(t, carry, side=side):
                patch(side, t)
                return carry

            lax.fori_loop(p * span, p * span + span, step, 0)
            copy = pltpu.make_async_copy(held(side, p), slab(side, p), out_sem.at[side, p])
            copy.start()
            writes.append(copy)
    for copy in writes + rows:
        copy.wait()


def last_step(x, plan, recv, own, sums):
    tiles, n, _, c = x.shape
    strips = own.shape[0]
    parts = 4 if tiles % 4 == 0 else 1
    smem = pl.BlockSpec(memory_space=pltpu.SMEM)
    vmem = pl.BlockSpec(memory_space=pltpu.VMEM)
    anywhere = pl.BlockSpec(memory_space=pl.ANY)
    return pl.pallas_call(
        last_kernel,
        in_specs=[smem, vmem, vmem, vmem, anywhere],
        out_specs=anywhere,
        out_shape=jax.ShapeDtypeStruct(x.shape, BF),
        scratch_shapes=[
            pltpu.VMEM((tiles, 4, n, c), BF),
            pltpu.VMEM((group_of(tiles, SIDE), 4, n, c), F32),
            pltpu.VMEM((2, tiles, n, 16, c), BF),
            pltpu.VMEM((n * 8, c), F32),
            pltpu.SemaphoreType.DMA((2, parts)),
            pltpu.SemaphoreType.DMA((2, parts)),
            pltpu.SemaphoreType.DMA((2,)),
        ],
        input_output_aliases={4: 0},
        compiler_params=params(),
        name="last_step",
    )(plan[0][0], recv, own, sums, x)


def group_of(tiles, want):
    return max(g for g in range(1, want + 1) if tiles % g == 0)


def tile_spec(group, *dims):
    return pl.BlockSpec((group,) + dims, lambda i: (i,) + (0,) * len(dims))


def whole_spec(shape):
    return pl.BlockSpec(shape, lambda i: (0,) * len(shape))


def enc_conv(x, rim, w, want):
    tiles, n, _, c = x.shape
    half, n_p = n // 2, up16(n)
    g = group_of(tiles, want)
    m = pair_chunks(n, ENC_PAIRS.get(n, 6))[0][1]
    args, specs = [x, w.reshape(9, c, c)], [tile_spec(g, n, n, c), whole_spec((9, c, c))]
    if rim is not None:
        args.append(rim.reshape(tiles, 4, n, c))
        specs.append(tile_spec(g, 4, n, c))
    y, sums, ring, s = pl.pallas_call(
        enc_kernel,
        grid=(tiles // g,),
        in_specs=specs,
        out_specs=[
            tile_spec(g, half, 2, n, c), tile_spec(g, 4, n, c), tile_spec(g, 4, n, c), tile_spec(g, half, half, c)
        ],
        out_shape=[
            jax.ShapeDtypeStruct((tiles, half, 2, n, c), BF),
            jax.ShapeDtypeStruct((tiles, 4, n, c), F32),
            jax.ShapeDtypeStruct((tiles, 4, n, c), BF),
            jax.ShapeDtypeStruct((tiles, half, half, c), BF),
        ],
        scratch_shapes=[
            pltpu.VMEM((half + 1, n_p, 768), BF),
            pltpu.VMEM((n * 8, 128), F32),
            pltpu.VMEM((m * n, 128), F32),
            pltpu.VMEM((2, n, 128), F32),
            pltpu.VMEM((1536, 256), BF),
        ],
        compiler_params=params(),
        cost_estimate=pl.CostEstimate(
            flops=tiles * n * n * 2 * 1536 * 128, bytes_accessed=tiles * n * n * 600, transcendentals=tiles * n * n * 128
        ),
        name="enc_conv",
    )(*args)
    strips = lambda a: a.reshape(tiles * 4, n, c)
    return y.reshape(tiles, n, n, c), strips(sums), strips(ring), s


def dec_conv(x, rim, u, urim, w, want):
    tiles, n, _, c = x.shape
    half, n_p = n // 2, up16(n)
    g = group_of(tiles, want)
    m = pair_chunks(n, DEC_PAIRS.get(n, 6))[0][1]
    args = [x, rim.reshape(tiles, 4, n, c), u]
    specs = [tile_spec(g, n, n, c), tile_spec(g, 4, n, c), tile_spec(g, half, half, c)]
    if urim is not None:
        args.append(urim.reshape(tiles, 4, half, c))
        specs.append(tile_spec(g, 4, half, c))
    args.append(w.reshape(9, 2 * c, c))
    specs.append(whole_spec((9, 2 * c, c)))
    rows = (half + 1, 2 * half, 384) if in_pairs(half) else (half + 2, up16(half), 384)

    def kernel(*refs):
        dec_kernel(urim is not None, *refs)

    y, sums = pl.pallas_call(
        kernel,
        grid=(tiles // g,),
        in_specs=specs,
        out_specs=[tile_spec(g, half, 2, n, c), tile_spec(g, 4, n, c)],
        out_shape=[
            jax.ShapeDtypeStruct((tiles, half, 2, n, c), BF),
            jax.ShapeDtypeStruct((tiles, 4, n, c), F32),
        ],
        scratch_shapes=[
            pltpu.VMEM((half + 1, n_p, 768), BF),
            pltpu.VMEM(rows, BF),
            pltpu.VMEM((n * 8, 128), F32),
            pltpu.VMEM((2, m, n_p, 128), F32),
            pltpu.VMEM((1536, 256), BF),
            pltpu.VMEM((2, 3, 256, 256), BF),
        ],
        compiler_params=params(),
        cost_estimate=pl.CostEstimate(
            flops=tiles * n * n * 2 * 2300 * 128, bytes_accessed=tiles * n * n * 600, transcendentals=tiles * n * n * 128
        ),
        name="dec_conv",
    )(*args)
    return y.reshape(x.shape), sums.reshape(tiles * 4, n, c)


def strips_of(field, ring=0):
    n = field.shape[1]
    far = n - 1 - ring
    out = jnp.stack([field[:, ring], field[:, :, far], field[:, far], field[:, :, ring]], axis=1)
    out = jnp.pad(out, ((0, 0), (0, 0), (0, strip_rows(n) - n), (0, 0)))
    return out.reshape(field.shape[0] * 4, strip_rows(n), field.shape[3])


def patched(field, rim):
    tiles, n, _, c = field.shape
    rim = rim.reshape(tiles, 4, -1, c)[:, :, :n]
    middle = jnp.concatenate(
        [rim[:, 3, 1 : n - 1, None], field[:, 1 : n - 1, 1 : n - 1], rim[:, 1, 1 : n - 1, None]], axis=2
    )
    return jnp.concatenate([rim[:, 0][:, None], middle, rim[:, 2][:, None]], axis=1)


def inner_sums(field, weight):
    return lax.conv_general_dilated(
        field,
        weight,
        (1, 1),
        ((1, 1), (1, 1)),
        dimension_numbers=("NHWC", "HWIO", "NHWC"),
        preferred_element_type=F32,
    )


def shrink(field):
    count, length, _, channels = field.shape
    blocks = field.astype(F32).reshape(count, length // 2, 2, length // 2, 2, channels)
    return (jnp.sum(blocks, axis=(2, 4)) * 0.25).astype(BF)


def enlarge(field):
    return jnp.repeat(jnp.repeat(field, 2, axis=1), 2, axis=2)


def per_device(features, edge_table, w_enc0, w_enc1, w_enc2, w_mid, w_dec2, w_dec1, w_dec0):
    tiles, n0 = features.shape[0], features.shape[1]
    devices = lax.axis_size("tile")
    position = lax.axis_index("tile")
    cap = pair_capacity(FACE_TILES, tiles)
    rows = devices * cap
    slot_row = send_slots(edge_table, position, tiles, cap)

    def trade(strips):
        out = lax.all_to_all(strips.reshape(devices, -1, 128), "tile", split_axis=0, concat_axis=0, tiled=True)
        return out.reshape(strips.shape)

    def step(n, *args, **kw):
        return rim_step(n, devices, cap, plan, *args, **kw)

    def after(value, token):
        return lax.optimization_barrier((value, token))[0]

    rim0, send = tile_rims(features, slot_row, rows)
    rim0 = rim0.reshape(tiles * 4, n0, 128)
    plan = receive_plan(after(edge_table, send), slot_row, position, tiles, cap, devices)
    recv = trade(send)
    enc0, sums, ring, x1 = enc_conv(features, None, w_enc0, 1)
    enc0_rim, x1_rim, send = step(n0, recv, rim0, sums, w=w_enc0, ring=ring)

    recv = trade(send)
    enc1, sums, ring, x2 = enc_conv(x1, x1_rim, w_enc1, 4)
    enc1_rim, x2_rim, send = step(n0 // 2, recv, x1_rim, sums, w=w_enc1, ring=ring)

    recv = trade(send)
    sums = inner_sums(patched(x2, x2_rim), w_enc2)
    enc2 = jax.nn.silu(sums).astype(BF)
    enc2_rim, x3_rim, send = step(
        n0 // 4, recv, x2_rim, strips_of(sums), w=w_enc2, ring=strips_of(enc2, 1)
    )

    recv = trade(send)
    sums = inner_sums(patched(shrink(enc2), x3_rim), w_mid)
    middle = jax.nn.silu(sums).astype(BF)
    skip2 = skip_step(n0 // 4, plan, enc2_rim, w_dec2)
    skip0 = skip_step(n0, plan, after(enc0_rim, x3_rim), w_dec0)
    sums, skip0 = lax.optimization_barrier((sums, skip0))
    mid_rim, own, send = step(
        n0 // 8, recv, x3_rim, strips_of(sums), w=w_mid,
        skip=skip2, wn=w_dec2,
    )

    recv = trade(send)
    joined = jnp.concatenate([enlarge(patched(middle, mid_rim)), patched(enc2, enc2_rim)], axis=3)
    sums = inner_sums(joined, w_dec2)
    dec2 = jax.nn.silu(sums).astype(BF)
    skip1 = skip_step(n0 // 2, plan, after(enc1_rim, mid_rim), w_dec1)
    dec2_rim, own, send = step(
        n0 // 4, recv, own, strips_of(sums), skip=skip1, wn=w_dec1
    )

    recv = trade(send)
    dec1, sums = dec_conv(enc1, enc1_rim, patched(dec2, dec2_rim), None, w_dec1, 4)
    dec1_rim, own, send = step(
        n0 // 2, recv, own, sums, skip=skip0, wn=w_dec0
    )

    recv = trade(send)
    dec0, sums = dec_conv(enc0, enc0_rim, dec1, dec1_rim, w_dec0, 1)
    return last_step(dec0, plan, recv, own, sums)


def solution(mesh):
    return jax.shard_map(
        per_device,
        mesh=mesh,
        in_specs=(P(("grp", "tile"), None, None, None), P(), P(), P(), P(), P(), P(), P(), P()),
        out_specs=P(("grp", "tile"), None, None, None),
        check_vma=False,
    )
```

```python
import jax
import jax.numpy as jnp
import numpy as np
from jax import lax
from jax.experimental import pallas as pl
from jax.experimental.pallas import tpu as pltpu
from jax.sharding import PartitionSpec as P

FACE_TILES = 8
RIM_TILES = 12
SIDE = 6
VMEM_LIMIT = 50 * 2**20
BF = jnp.bfloat16
F32 = jnp.float32


def cube_links(tiles_side):
    basis = np.eye(3, dtype=np.int64)
    frames = []
    for axis_id in range(3):
        for orient in (1, -1):
            frames.append(
                (orient * basis[axis_id], basis[(axis_id + 1) % 3], basis[(axis_id + 2) % 3])
            )
    per_face = tiles_side * tiles_side
    tile_total = 6 * per_face
    centres = np.zeros((tile_total, 3), np.int64)
    lookup = {}
    for face_id in range(6):
        normal, row_axis, col_axis = frames[face_id]
        for row_id in range(tiles_side):
            for col_id in range(tiles_side):
                slot_id = face_id * per_face + row_id * tiles_side + col_id
                centre = (
                    tiles_side * normal
                    + (2 * row_id + 1 - tiles_side) * row_axis
                    + (2 * col_id + 1 - tiles_side) * col_axis
                )
                centres[slot_id] = centre
                lookup[tuple((int(entry) for entry in centre))] = slot_id
    partner = np.zeros((tile_total, 4), np.int64)
    for slot_id in range(tile_total):
        normal, row_axis, col_axis = frames[slot_id // per_face]
        outward = (-row_axis, col_axis, row_axis, -col_axis)
        for edge_id in range(4):
            beyond = tuple((int(entry) for entry in centres[slot_id] + 2 * outward[edge_id]))
            if beyond in lookup:
                partner[slot_id, edge_id] = lookup[beyond]
            else:
                partner[slot_id, edge_id] = lookup[
                    tuple((int(entry) for entry in centres[slot_id] + outward[edge_id] - normal))
                ]
    return partner


def pair_capacity(tiles_side, tiles_here):
    partner = cube_links(tiles_side)
    tile_total = partner.shape[0]
    blocks = tile_total // tiles_here
    source = np.repeat(np.arange(tile_total) // tiles_here, 4)
    target = partner.reshape(-1) // tiles_here
    identity = np.eye(blocks, dtype=np.int64)
    shared = identity[source].T @ identity[target]
    shared = shared * (1 - identity)
    return max(int(shared.max()), 1)


def own_strips(edge_table, position, tiles_here):
    rows = lax.dynamic_slice_in_dim(edge_table, position * tiles_here, tiles_here, 0)
    rows = rows.reshape(tiles_here * 4, 2)
    return rows[:, 0], rows[:, 1] // 2, rows[:, 1] % 2


def send_slots(edge_table, position, tiles_here, slot_count):
    partner, _, _ = own_strips(edge_table, position, tiles_here)
    target = partner // tiles_here
    order = jnp.arange(tiles_here * 4, dtype=jnp.int32)
    earlier = (order[None, :] < order[:, None]) & (target[None, :] == target[:, None])
    slot_rank = jnp.sum(earlier.astype(jnp.int32), axis=1)
    return jnp.where(target != position, target * slot_count + slot_rank, -1)


def listed(mask):
    order = jnp.arange(mask.shape[0], dtype=jnp.int32)
    rank = jnp.sum((mask[None, :] & (order[None, :] < order[:, None])).astype(jnp.int32), axis=1)
    hit = mask[None, :] & (rank[None, :] == order[:, None])
    found = jnp.sum(jnp.where(hit, order[None, :], 0), axis=1)
    total = jnp.sum(mask.astype(jnp.int32), keepdims=True)
    found = jnp.where(order < total, found, mask.shape[0])
    return jnp.concatenate([found, jnp.full((3,), mask.shape[0], jnp.int32), total])


def receive_plan(edge_table, slot_row, position, tiles_here, slot_count, devices):
    strip_count = tiles_here * 4
    partner, matching, reversed_rows = own_strips(edge_table, position, tiles_here)
    target = partner // tiles_here
    order = jnp.arange(strip_count, dtype=jnp.int32)
    remote = target != position
    wanted = partner % tiles_here * 4 + matching
    toward_me = edge_table[:, :, 0].reshape(devices, strip_count) // tiles_here == position
    before = (order[:, None] < order[None, :]).astype(BF)
    ranks = jnp.dot(toward_me.astype(BF), before, preferred_element_type=F32).astype(BF)
    blocks = jnp.arange(devices, dtype=jnp.int32)
    from_target = (target[:, None] == blocks[None, :]).astype(BF)
    their_ranks = jnp.dot(from_target, ranks, preferred_element_type=F32)
    recv_rank = jnp.sum(jnp.where(wanted[:, None] == order[None, :], their_ranks, 0.0), axis=1).astype(jnp.int32)
    pick_row = lambda count: jnp.where(remote, target * count + recv_rank, devices * count + wanted)
    odd = (matching != (order + 2) % 4) | (reversed_rows == 1)
    one_more = lambda a: jnp.concatenate([a, jnp.zeros((1,), jnp.int32)])
    even = (slot_count + 1) // 2 * 2
    paired_slot = slot_row + target * (even - slot_count)
    shared = (one_more(reversed_rows), one_more(matching), listed(remote), listed(odd))
    return (pick_row(slot_count), pick_row(even)), (slot_row, paired_slot), shared


def up16(n):
    return (n + 15) // 16 * 16


def strip_rows(n):
    return {6: 8, 12: 16}.get(n, n)


def two_up(rows):
    return rows == 16


def send_shape(devices, cap, rows):
    return (devices * ((cap + 1) // 2), 24) if two_up(rows) else (devices * cap, rows)


def params():
    return pltpu.CompilerParams(vmem_limit_bytes=VMEM_LIMIT)


def rims_kernel(slot_ref, lo_ref, hi_ref, top_ref, bottom_ref, out_ref, send_ref, colbuf):
    group, n = lo_ref.shape[0], lo_ref.shape[1]
    first = pl.program_id(0) * group * 4
    for g in range(group):
        colbuf[...] = lo_ref[g, :, 0:8, :].astype(F32).reshape(n * 8, 128)
        left = colbuf[pl.ds(0, n, 8), :]
        colbuf[...] = hi_ref[g, :, 8:16, :].astype(F32).reshape(n * 8, 128)
        right = colbuf[pl.ds(7, n, 8), :]
        out_ref[g, 0] = top_ref[g, 0]
        out_ref[g, 1] = right.astype(BF)
        out_ref[g, 2] = bottom_ref[g, 0]
        out_ref[g, 3] = left.astype(BF)
    for g in range(group):
        for e in range(4):
            slot = slot_ref[first + g * 4 + e]

            @pl.when(slot >= 0)
            def _():
                send_ref[slot] = out_ref[g, e]


def tile_rims(x, slot_row, rows):
    tiles, n, _, c = x.shape
    g = group_of(tiles, RIM_TILES)
    last = n // 16 - 1
    return pl.pallas_call(
        rims_kernel,
        grid=(tiles // g,),
        in_specs=[
            pl.BlockSpec(memory_space=pltpu.SMEM),
            pl.BlockSpec((g, n, 16, c), lambda i: (i, 0, 0, 0)),
            pl.BlockSpec((g, n, 16, c), lambda i: (i, 0, last, 0)),
            pl.BlockSpec((g, 1, n, c), lambda i: (i, 0, 0, 0)),
            pl.BlockSpec((g, 1, n, c), lambda i: (i, n - 1, 0, 0)),
        ],
        out_specs=[tile_spec(g, 4, n, c), whole_spec((rows, n, c))],
        out_shape=[
            jax.ShapeDtypeStruct((tiles, 4, n, c), BF),
            jax.ShapeDtypeStruct((rows, n, c), BF),
        ],
        scratch_shapes=[pltpu.VMEM((n * 8, 128), F32)],
        compiler_params=params(),
        name="tile_rims",
    )(slot_row, x, x, x, x)


def silu(s):
    half = s * 0.5
    return half + half * jnp.tanh(half)


def strip_shifts(h, n):
    rows = h.shape[0]
    row = lax.broadcasted_iota(jnp.int32, h.shape, 0)
    half = h * 0.5
    down = jnp.where(row == 0, half, pltpu.roll(h, 1, 0))
    up = jnp.where(row == n - 1, half, pltpu.roll(h, rows - 1, 0))
    return down, up


def flip_matrices(rows, n):
    ri = lax.broadcasted_iota(jnp.int32, (rows, rows), 0)
    ci = lax.broadcasted_iota(jnp.int32, (rows, rows), 1)
    return (ri + ci == n - 1).astype(F32), (ri == ci).astype(F32)


def put_shifts(ref, index, lane, h, n):
    down, up = strip_shifts(h, n)
    for s, part in enumerate((down, h, up)):
        ref[index + (slice(None), slice(lane + s * 128, lane + s * 128 + 128))] = part.astype(ref.dtype)


def each_tile(tiles, body):
    side = group_of(tiles, SIDE)

    def step(i, carry):
        for k in range(side):
            body(i * side + k, k)
        return carry

    lax.fori_loop(0, tiles // side, step, 0)


def each_listed(list_ref, body):
    def step(j, carry):
        body(list_ref[j])
        return carry

    lax.fori_loop(0, list_ref[list_ref.shape[0] - 1], step, 0)


def each_four(list_ref, body):
    def step(j, carry):
        body([list_ref[j * 4 + k] for k in range(4)])
        return carry

    lax.fori_loop(0, (list_ref[list_ref.shape[0] - 1] + 3) // 4, step, 0)


def turned(rev_ref, i, h, flip, keep):
    order = jnp.where(rev_ref[i] == 1, flip, keep).astype(BF)
    return jnp.dot(order, h.astype(BF), preferred_element_type=F32)


def incoming(pick_ref, recv_ref, own_ref, i):
    paired = own_ref.shape[1] != recv_ref.shape[1]
    slots = recv_ref.shape[0] * (2 if paired else 1)
    pick = pick_ref[i]
    away = pick < slots
    slot = jnp.minimum(pick, slots - 1)
    b = own_ref[jnp.maximum(pick - slots, 0)].astype(F32)
    if not paired:
        return jnp.where(away, recv_ref[slot].astype(F32), b)
    a = recv_ref[slot >> 1].astype(F32)
    row = lax.broadcasted_iota(jnp.int32, (16, 128), 0)
    a = jnp.where(row < 12, jnp.where((slot & 1) == 1, pltpu.roll(a, 12, 0), a)[0:16], 0.0)
    return jnp.where(away, a, b)


def edge_taps(w_ref, e, lo):
    taps = ((0, 1, 2), (2, 5, 8), (6, 7, 8), (0, 3, 6))[e]
    return jnp.concatenate([w_ref[tap, lo : lo + 128, :] for tap in taps], axis=0)


def contributions(n, tiles, strip_of, w_ref, lo, rev_ref, edge_ref, odd_ref, lhs_ref, con_ref, taps_ref):
    lp = lhs_ref.shape[2]
    for e in range(4):
        taps_ref[e] = edge_taps(w_ref, e, lo)

    def fill(t, k):
        for f in range(4):
            put_shifts(lhs_ref, (f, t), 0, strip_of(f, t, k), n)

    each_tile(tiles, fill)
    for f in range(4):
        lhs = lhs_ref[f, 0:tiles].reshape(tiles * lp, 384).astype(BF)
        out = jnp.dot(lhs, taps_ref[(f + 2) % 4], preferred_element_type=F32)
        con_ref[f, 0:tiles] = out.reshape(tiles, lp, 128)
    flip, keep = flip_matrices(lp, n)

    def odd_ones(four):
        halos = [lhs_ref[i % 4, i // 4, :, 128:256] for i in four]
        halos = [turned(rev_ref, i, h, flip, keep) for i, h in zip(four, halos)]
        taps = [taps_ref[edge_ref[i]] for i in four]
        sums = []
        for h, tap in zip(halos, taps):
            down, up = strip_shifts(h, n)
            lhs = jnp.concatenate([down.astype(BF), h.astype(BF), up.astype(BF)], axis=1)
            sums.append(jnp.dot(lhs, tap, preferred_element_type=F32))
        for i, total in zip(four, sums):
            con_ref[i % 4, i // 4] = total

    each_four(odd_ref, odd_ones)


def skip_kernel(n, rev_ref, edge_ref, odd_ref, rim_ref, w_ref, out_ref, lhs_ref, con_ref, taps_ref):
    tiles = rim_ref.shape[0] // 4
    contributions(
        n, tiles, lambda f, t, k: rim_ref[t * 4 + f].astype(F32), w_ref, 128,
        rev_ref, edge_ref, odd_ref, lhs_ref, con_ref, taps_ref,
    )

    def put(t, k):
        for f in range(4):
            out_ref[t * 4 + f] = con_ref[f, t]

    each_tile(tiles, put)


def wide(rows):
    return BF if rows % 16 == 0 else F32


def skip_step(n, plan, rim, w):
    strips, lp, c = rim.shape
    smem = pl.BlockSpec(memory_space=pltpu.SMEM)
    vmem = pl.BlockSpec(memory_space=pltpu.VMEM)
    return pl.pallas_call(
        lambda *refs: skip_kernel(n, *refs),
        in_specs=[smem, smem, smem, vmem, vmem],
        out_specs=vmem,
        out_shape=jax.ShapeDtypeStruct((strips, lp, c), F32),
        scratch_shapes=[
            pltpu.VMEM((4, strips // 4 + 1, lp, 384), wide(lp)),
            pltpu.VMEM((4, strips // 4 + 1, lp, 128), F32),
            pltpu.VMEM((4, 384, 128), BF),
        ],
        compiler_params=params(),
        cost_estimate=pl.CostEstimate(flops=strips * lp * 2 * 384 * 256, bytes_accessed=strips * lp * 768, transcendentals=0),
        name="skip_step",
    )(plan[2][0], plan[2][1], plan[2][3], rim, w.reshape(9, -1, c))


def corners(end):
    return (
        (0, 0, 3, 0), (0, end, 1, 0), (2, 0, 3, end), (2, end, 1, end),
        (3, 0, 0, 0), (3, end, 2, 0), (1, 0, 0, end), (1, end, 2, end),
    )


def rim_kernel(n, strips_in, nxt, refs):
    it = iter(refs)
    pick_ref, rev_ref, slot_ref, edge_ref, remote_ref, odd_ref = [next(it) for _ in range(6)]
    recv_ref, own_ref, sum_ref = next(it), next(it), next(it)
    w_ref = next(it) if strips_in else None
    ring_ref = next(it) if nxt == "shrink" else None
    skip_ref, wn_ref = (next(it), next(it)) if nxt == "halo" else (None, None)
    rim_ref, next_ref, send_ref = next(it), next(it), next(it)
    lhs_ref, con_ref = next(it), next(it)
    edge_buf, ring_buf, sum_buf, out_buf = next(it), next(it), next(it), next(it)
    lhsn_ref, conn_ref, taps_ref, big_buf = [next(it) for _ in range(4)] if nxt == "halo" else [None] * 4

    strips, lp = own_ref.shape[0], own_ref.shape[1]
    tiles = strips // 4
    flip, keep = flip_matrices(lp, n)

    if strips_in:

        def fill(t, k):
            for e in range(4):
                put_shifts(lhs_ref, (e, t), 0, incoming(pick_ref, recv_ref, own_ref, t * 4 + e), n)

        each_tile(tiles, fill)

        def turn(four):
            halos = [lhs_ref[i % 4, i // 4, :, 128:256] for i in four]
            halos = [turned(rev_ref, i, h, flip, keep) for i, h in zip(four, halos)]
            for i, h in zip(four, halos):
                put_shifts(lhs_ref, (i % 4, i // 4), 0, h, n)

        each_four(odd_ref, turn)
        for e in range(4):
            lhs = lhs_ref[e, 0:tiles].reshape(tiles * lp, 384).astype(BF)
            out = jnp.dot(lhs, edge_taps(w_ref, e, 0), preferred_element_type=F32)
            con_ref[e] = out.reshape(tiles, lp, 128)

    end = n - 1
    joints = (
        (0, 0, 3, 1), (0, end, 1, 1), (2, 0, 3, end - 1), (2, end, 1, end - 1),
        (3, 0, 0, 1), (3, end, 2, 1), (1, 0, 0, end - 1), (1, end, 2, end - 1),
    )
    if nxt == "shrink":
        out_buf[...] = jnp.zeros_like(out_buf)

    def finish(t, k):
        if strips_in:
            con = [con_ref[e, t] for e in range(4)]
        else:
            con = [incoming(pick_ref, recv_ref, own_ref, t * 4 + e) for e in range(4)]
        for e in range(4):
            edge_buf[k, e] = sum_ref[t * 4 + e] + con[e]
        for e, cell, other, at in corners(end):
            cells = slice(cell, cell + 1)
            edge_buf[k, e, cells] = edge_buf[k, e, cells] + con[other][at : at + 1]
        for e in range(4):
            y = silu(edge_buf[k, e]).astype(BF)
            rim_ref[t * 4 + e] = y
            edge_buf[k, e] = y.astype(F32)
        if nxt == "shrink":
            for e in range(4):
                ring_buf[k, e] = ring_ref[t * 4 + e].astype(F32)
            for e, cell, other, at in joints:
                ring_buf[k, e, cell : cell + 1] = edge_buf[k, other, at : at + 1]
            for e in range(4):
                sum_buf[k, e] = edge_buf[k, e] + ring_buf[k, e]
                small = sum_buf[k, e, pl.ds(0, lp // 2, 2), :] + sum_buf[k, e, pl.ds(1, lp // 2, 2), :]
                out_buf[k, e, 0 : lp // 2] = small * 0.25
                next_ref[t * 4 + e] = out_buf[k, e].astype(BF)

    each_tile(tiles, finish)

    if nxt == "halo":
        half = big_buf.shape[2] // 2

        def enlarged(f, t, k):
            rim = rim_ref[t * 4 + f].astype(F32)[0:half]
            big_buf[k, f, pl.ds(0, half, 2), :] = rim
            big_buf[k, f, pl.ds(1, half, 2), :] = rim
            return big_buf[k, f]

        contributions(
            2 * n, tiles, enlarged, wn_ref, 0,
            rev_ref, edge_ref, odd_ref, lhsn_ref, conn_ref, taps_ref,
        )

        def put(t, k):
            for f in range(4):
                next_ref[t * 4 + f] = (conn_ref[f, t] + skip_ref[t * 4 + f]).astype(BF)

        each_tile(tiles, put)

    def send(i):
        slot = slot_ref[i]
        if next_ref.shape[1] == send_ref.shape[1]:
            send_ref[slot] = next_ref[i]
        else:
            block, second = slot >> 1, (slot & 1) == 1
            strip = jnp.concatenate([next_ref[i].astype(F32), jnp.zeros((8, 128), F32)], axis=0)
            row = lax.broadcasted_iota(jnp.int32, (24, 128), 0)
            held = send_ref[block].astype(F32)
            both = jnp.where(second, jnp.where(row < 12, held, pltpu.roll(strip, 12, 0)), jnp.where(row < 12, strip, held))
            send_ref[block] = both.astype(BF)

    each_listed(remote_ref, send)


def rim_step(n, devices, cap, plan, recv, own, sums, w=None, ring=None, skip=None, wn=None):
    strips, lp, c = own.shape
    tiles = strips // 4
    side = group_of(tiles, SIDE)
    nxt = "shrink" if ring is not None else "halo"
    smem = pl.BlockSpec(memory_space=pltpu.SMEM)
    vmem = pl.BlockSpec(memory_space=pltpu.VMEM)
    w = w if w is None else w.reshape(9, -1, c)
    wn = wn if wn is None else wn.reshape(9, -1, c)
    args = [recv, own, sums] + [a for a in (w, ring, skip, wn) if a is not None]
    lo = strip_rows(n // 2) if nxt == "shrink" else strip_rows(2 * n)
    outs = [
        jax.ShapeDtypeStruct((strips, lp, c), BF),
        jax.ShapeDtypeStruct((strips, lo, c), BF),
        jax.ShapeDtypeStruct(send_shape(devices, cap, lo) + (c,), BF),
    ]
    scratch = [
        pltpu.VMEM((4, tiles + 1, lp, 384), wide(lp)),
        pltpu.VMEM((4, tiles, lp, 128), F32),
        pltpu.VMEM((side, 4, lp, 128), F32),
        pltpu.VMEM((side, 4, lp, 128), F32),
        pltpu.VMEM((side, 4, lp, 128), F32),
        pltpu.VMEM((side, 4, lo, 128), F32),
    ]
    if nxt == "halo":
        scratch += [
            pltpu.VMEM((4, tiles + 1, lo, 384), wide(lo)),
            pltpu.VMEM((4, tiles + 1, lo, 128), F32),
            pltpu.VMEM((4, 384, 128), BF),
            pltpu.VMEM((side, 4, lo, 128), F32),
        ]

    def kernel(*refs):
        rim_kernel(n, w is not None, nxt, refs)

    return pl.pallas_call(
        kernel,
        in_specs=[smem] * 6 + [vmem] * len(args),
        out_specs=[vmem] * len(outs),
        out_shape=outs,
        scratch_shapes=scratch,
        compiler_params=params(),
        cost_estimate=pl.CostEstimate(flops=strips * lp * 2 * 384 * 512, bytes_accessed=strips * lp * 1500, transcendentals=0),
        name="rim_step",
    )(plan[0][int(two_up(lp))], plan[2][0], plan[1][int(two_up(lo))], *plan[2][1:], *args)


def spread_columns(strip, n, sublane, buf):
    buf[pl.ds(sublane, n, 8), :] = strip
    return buf[...].reshape(n, 8, 128)


def with_rims(x, rim, n, buf):
    sub = lax.broadcasted_iota(jnp.int32, (n, 8, 128), 1)
    head = jnp.where(sub == 0, spread_columns(rim[3], n, 0, buf), x[:, 0:8])
    tail = jnp.where(sub == 7, spread_columns(rim[1], n, 7, buf), x[:, n - 8 : n])
    x = jnp.concatenate([head, x[:, 8 : n - 8], tail], axis=1)
    return jnp.concatenate([rim[0][None], x[1 : n - 1], rim[2][None]], axis=0)


def column_shifts(x, n):
    sub = lax.broadcasted_iota(jnp.int32, (x.shape[0], 8, 128), 1)
    down = pltpu.roll(x, 1, 1)
    up = pltpu.roll(x, n - 1, 1)
    down = jnp.concatenate([jnp.where(sub == 0, 0.0, down[:, 0:8]), down[:, 8:n]], axis=1)
    up = jnp.concatenate([up[:, 0 : n - 8], jnp.where(sub == 7, 0.0, up[:, n - 8 : n])], axis=1)
    return down, x, up


def fill_pairs(y_ref, x, n):
    half, n_p = n // 2, y_ref.shape[1]
    zero = jnp.zeros((n_p, 384), BF)
    y_ref[0, :, 0:384] = zero
    y_ref[half, :, 384:768] = zero
    for s, body in enumerate(column_shifts(x, n)):
        b = body.astype(BF).reshape(half, 2, n, 128)
        y_ref[0:half, 0:n, 384 + s * 128 : 384 + s * 128 + 128] = b[:, 0]
        y_ref[1 : half + 1, 0:n, s * 128 : s * 128 + 128] = b[:, 1]


def in_pairs(n):
    return n % 16 == 8 and n % 2 == 0


def fill_row_pairs(u_ref, x, n):
    half = n // 2
    zero = jnp.zeros((n, 384), BF)
    u_ref[0, 0:n] = zero
    u_ref[half, n : 2 * n] = zero
    for s, body in enumerate(column_shifts(x, n)):
        b = body.astype(BF).reshape(half, 2, n, 128)
        lanes = slice(s * 128, s * 128 + 128)
        u_ref[0:half, n : 2 * n, lanes] = b[:, 0]
        u_ref[1 : half + 1, 0:n, lanes] = b[:, 1]
        u_ref[half + 1 : n + 1, 0:n, lanes] = b[:, 0]
        u_ref[half + 1 : n + 1, n : 2 * n, lanes] = b[:, 1]


def coarse_lhs(u_ref, n, start, m, lanes):
    if in_pairs(n):
        at = start // 2 if start % 2 == 0 else n // 2 + 1 + start // 2
        return u_ref[at : at + m // 2, :, lanes].reshape(m * n, 256), n
    return u_ref[start : start + m, :, lanes].reshape(m * u_ref.shape[1], 256), u_ref.shape[1]


def fill_rows(u_ref, x, n):
    zero = jnp.zeros((u_ref.shape[1], 384), BF)
    u_ref[0] = zero
    u_ref[n + 1] = zero
    for s, body in enumerate(column_shifts(x, n)):
        u_ref[1 : n + 1, 0:n, s * 128 : s * 128 + 128] = body.astype(BF)


def pair_sums(y_ref, w_ref, q0, m, extra):
    n_p = y_ref.shape[1]
    a = y_ref[q0 : q0 + m].reshape(m * n_p, 768)
    b = y_ref[q0 + 1 : q0 + 1 + m].reshape(m * n_p, 768)
    acc = jnp.dot(a, w_ref[0:768, :], preferred_element_type=F32)
    acc = acc + jnp.dot(b, w_ref[768:1536, :], preferred_element_type=F32)
    acc = acc.reshape(m, n_p, 256)
    return acc if extra is None else acc + extra


def pair_chunks(n, most):
    half = n // 2
    m = max(m for m in range(1, most + 1) if half % m == 0)
    return [(q, m) for q in range(0, half, m)]


ENC_PAIRS = {48: 24}
DEC_PAIRS = {48: 12}


def column_of(acc, m, lo, sublane, colbuf):
    rows = jnp.stack([acc[:, lo : lo + 8, 0:128], acc[:, lo : lo + 8, 128:256]], axis=1)
    colbuf[0 : 16 * m] = rows.reshape(16 * m, 128)
    return colbuf[pl.ds(sublane, 2 * m, 8), :]


def put_sums(acc, sums_ref, g, q0, m, n, colbuf):
    cells = slice(2 * q0, 2 * q0 + 2 * m)
    if q0 == 0:
        sums_ref[g, 0] = acc[0, 0:n, 0:128]
    if q0 + m == n // 2:
        sums_ref[g, 2] = acc[m - 1, 0:n, 128:256]
    sums_ref[g, 3, cells] = column_of(acc, m, 0, 0, colbuf)
    sums_ref[g, 1, cells] = column_of(acc, m, n - 8, 7, colbuf)


def fill_pair_weights(raw_ref, lo, w_ref):
    for p in range(4):
        for col in range(3):
            at = slice((p * 3 + col) * 128, (p * 3 + col) * 128 + 128)
            for out in range(2):
                row = p - out
                tap = raw_ref[row * 3 + col, lo : lo + 128, :] if 0 <= row <= 2 else jnp.zeros((128, 128), BF)
                w_ref[at, out * 128 : out * 128 + 128] = tap


def fill_coarse_weights(raw_ref, w_ref):
    along = (((0,), (1, 2), ()), ((), (0, 1), (2,)))
    for b in range(2):
        for k in range(3):
            for slot in range(2):
                cols = along[b][slot + b]
                for out in range(2):
                    taps = [raw_ref[r * 3 + col, 0:128, :].astype(F32) for r in along[out][k] for col in cols]
                    total = sum(taps[1:], taps[0]) if taps else jnp.zeros((128, 128), F32)
                    w_ref[b, k, slot * 128 : slot * 128 + 128, out * 128 : out * 128 + 128] = total.astype(BF)


def enc_kernel(*refs):
    it = iter(refs[:-5])
    x_ref, raw_ref = next(it), next(it)
    rest = list(it)
    rim_ref = rest.pop(0) if len(rest) == 5 else None
    y_ref, sums_ref, ring_ref, s_ref = rest
    pairs, colbuf, sumbuf, ringbuf, w_ref = refs[-5:]

    @pl.when(pl.program_id(0) == 0)
    def _():
        fill_pair_weights(raw_ref, 0, w_ref)

    group, n = x_ref.shape[0], x_ref.shape[1]
    half = n // 2

    for g in range(group):
        x = x_ref[g].astype(F32)
        if rim_ref is not None:
            x = with_rims(x, [rim_ref[g, e].astype(F32) for e in range(4)], n, colbuf)
        fill_pairs(pairs, x, n)
        for q0, m in pair_chunks(n, ENC_PAIRS.get(n, 6)):
            acc = pair_sums(pairs, w_ref, q0, m, None)
            put_sums(acc, sums_ref, g, q0, m, n, colbuf)
            out = silu(acc).astype(BF)[:, 0:n]
            y_ref[g, q0 : q0 + m, 0] = out[:, :, 0:128]
            y_ref[g, q0 : q0 + m, 1] = out[:, :, 128:256]
            wide = out.astype(F32)
            if q0 == 0:
                ring_ref[g, 0] = out[0, :, 128:256]
            if q0 + m == half:
                ring_ref[g, 2] = out[m - 1, :, 0:128]
            ringbuf[1, 2 * q0 : 2 * q0 + 2 * m] = column_of(wide, m, n - 8, 6, colbuf)
            ringbuf[0, 2 * q0 : 2 * q0 + 2 * m] = column_of(wide, m, 0, 1, colbuf)
            both = wide[:, :, 0:128] + wide[:, :, 128:256]
            sumbuf[...] = both.reshape(m * n, 128)
            small = sumbuf[pl.ds(0, m * half, 2), :] + sumbuf[pl.ds(1, m * half, 2), :]
            s_ref[g, q0 : q0 + m] = (small * 0.25).reshape(m, half, 128).astype(BF)
        ring_ref[g, 1] = ringbuf[1].astype(BF)
        ring_ref[g, 3] = ringbuf[0].astype(BF)


def dec_kernel(coarse_rims, *refs):
    refs = list(refs)
    x_ref, rim_ref, u_ref = refs.pop(0), refs.pop(0), refs.pop(0)
    urim_ref = refs.pop(0) if coarse_rims else None
    raw_ref = refs.pop(0)
    y_ref, sums_ref, pairs, rows, colbuf, acc_ref, w_ref, wu_ref = refs
    group, n = y_ref.shape[0], y_ref.shape[3]
    half = n // 2

    @pl.when(pl.program_id(0) == 0)
    def _():
        fill_pair_weights(raw_ref, 128, w_ref)
        fill_coarse_weights(raw_ref, wu_ref)

    for g in range(group):
        u = u_ref[g].astype(F32)
        if urim_ref is not None:
            u = with_rims(u, [urim_ref[g, e].astype(F32) for e in range(4)], half, colbuf.at[0 : half * 8])
        (fill_row_pairs if in_pairs(half) else fill_rows)(rows, u, half)
        x = with_rims(x_ref[g].astype(F32), [rim_ref[g, e].astype(F32) for e in range(4)], n, colbuf)
        fill_pairs(pairs, x, n)
        for q0, m in pair_chunks(n, DEC_PAIRS.get(n, 6)):
            for b in range(2):
                acc = None
                for k in range(3):
                    lhs, hp = coarse_lhs(rows, half, q0 + k, m, slice(b * 128, b * 128 + 256))
                    part = jnp.dot(lhs, wu_ref[b, k], preferred_element_type=F32)
                    acc = part if acc is None else acc + part
                acc = acc.reshape(m, hp, 256)
                for i in range(m):
                    for p in range(2):
                        acc_ref[p, i, pl.ds(b, half, 2), :] = acc[i, 0:half, p * 128 : p * 128 + 128]
            extra = jnp.concatenate([acc_ref[0], acc_ref[1]], axis=2)
            acc = pair_sums(pairs, w_ref, q0, m, extra)
            put_sums(acc, sums_ref, g, q0, m, n, colbuf)
            out = silu(acc).astype(BF)[:, 0:n]
            y_ref[g, q0 : q0 + m, 0] = out[:, :, 0:128]
            y_ref[g, q0 : q0 + m, 1] = out[:, :, 128:256]


def last_kernel(pick_ref, recv_ref, own_ref, sum_ref, x_ref, y_ref, *scratch):
    rim_ref, edge_buf, slab_ref, colbuf, in_sem, out_sem, row_sem = scratch
    del x_ref
    strips, n = own_ref.shape[0], own_ref.shape[1]
    tiles = strips // 4
    parts = in_sem.shape[1]
    span = tiles // parts

    def slab(side, part):
        return y_ref.at[pl.ds(part * span, span), :, pl.ds(side * (n - 16), 16), :]

    def held(side, part):
        return slab_ref.at[side, pl.ds(part * span, span)]

    reads = [
        [pltpu.make_async_copy(slab(side, p), held(side, p), in_sem.at[side, p]) for p in range(parts)]
        for side in range(2)
    ]
    for p in range(parts):
        for side in range(2):
            reads[side][p].start()

    end = n - 1

    def finish(t, k):
        con = [incoming(pick_ref, recv_ref, own_ref, t * 4 + e) for e in range(4)]
        for e in range(4):
            edge_buf[k, e] = sum_ref[t * 4 + e] + con[e]
        for e, cell, other, at in corners(end):
            cells = slice(cell, cell + 1)
            edge_buf[k, e, cells] = edge_buf[k, e, cells] + con[other][at : at + 1]
        for e in range(4):
            rim_ref[t, e] = silu(edge_buf[k, e]).astype(BF)

    each_tile(tiles, finish)

    rows = [
        pltpu.make_async_copy(
            rim_ref.at[:, e, pl.ds(16, n - 32), :], y_ref.at[:, row, pl.ds(16, n - 32), :], row_sem.at[j]
        )
        for j, (e, row) in enumerate(((0, 0), (2, n - 1)))
    ]
    for copy in rows:
        copy.start()

    sub = lax.broadcasted_iota(jnp.int32, (n, 8, 128), 1)

    def patch(side, t):
        lo = 0 if side == 0 else n - 16
        near = slice(0, 8) if side == 0 else slice(8, 16)
        far = slice(8, 16) if side == 0 else slice(0, 8)
        x = slab_ref[side, t].astype(F32)
        cells = spread_columns(rim_ref[t, 3 if side == 0 else 1].astype(F32), n, 0 if side == 0 else 7, colbuf)
        new = jnp.where(sub == (0 if side == 0 else 7), cells, x[:, near])
        both = [new, x[:, far]] if side == 0 else [x[:, far], new]
        slab_ref[side, t] = jnp.concatenate(both, axis=1).astype(BF)
        slab_ref[side, t, 0] = rim_ref[t, 0, lo : lo + 16]
        slab_ref[side, t, n - 1] = rim_ref[t, 2, lo : lo + 16]

    writes = []
    for p in range(parts):
        for side in range(2):
            reads[side][p].wait()

            def step(t, carry, side=side):
                patch(side, t)
                return carry

            lax.fori_loop(p * span, p * span + span, step, 0)
            copy = pltpu.make_async_copy(held(side, p), slab(side, p), out_sem.at[side, p])
            copy.start()
            writes.append(copy)
    for copy in writes + rows:
        copy.wait()


def last_step(x, plan, recv, own, sums):
    tiles, n, _, c = x.shape
    strips = own.shape[0]
    parts = 4 if tiles % 4 == 0 else 1
    smem = pl.BlockSpec(memory_space=pltpu.SMEM)
    vmem = pl.BlockSpec(memory_space=pltpu.VMEM)
    anywhere = pl.BlockSpec(memory_space=pl.ANY)
    return pl.pallas_call(
        last_kernel,
        in_specs=[smem, vmem, vmem, vmem, anywhere],
        out_specs=anywhere,
        out_shape=jax.ShapeDtypeStruct(x.shape, BF),
        scratch_shapes=[
            pltpu.VMEM((tiles, 4, n, c), BF),
            pltpu.VMEM((group_of(tiles, SIDE), 4, n, c), F32),
            pltpu.VMEM((2, tiles, n, 16, c), BF),
            pltpu.VMEM((n * 8, c), F32),
            pltpu.SemaphoreType.DMA((2, parts)),
            pltpu.SemaphoreType.DMA((2, parts)),
            pltpu.SemaphoreType.DMA((2,)),
        ],
        input_output_aliases={4: 0},
        compiler_params=params(),
        name="last_step",
    )(plan[0][0], recv, own, sums, x)


def group_of(tiles, want):
    return max(g for g in range(1, want + 1) if tiles % g == 0)


def tile_spec(group, *dims):
    return pl.BlockSpec((group,) + dims, lambda i: (i,) + (0,) * len(dims))


def whole_spec(shape):
    return pl.BlockSpec(shape, lambda i: (0,) * len(shape))


def enc_conv(x, rim, w, want):
    tiles, n, _, c = x.shape
    half, n_p = n // 2, up16(n)
    g = group_of(tiles, want)
    m = pair_chunks(n, ENC_PAIRS.get(n, 6))[0][1]
    args, specs = [x, w.reshape(9, c, c)], [tile_spec(g, n, n, c), whole_spec((9, c, c))]
    if rim is not None:
        args.append(rim.reshape(tiles, 4, n, c))
        specs.append(tile_spec(g, 4, n, c))
    y, sums, ring, s = pl.pallas_call(
        enc_kernel,
        grid=(tiles // g,),
        in_specs=specs,
        out_specs=[
            tile_spec(g, half, 2, n, c), tile_spec(g, 4, n, c), tile_spec(g, 4, n, c), tile_spec(g, half, half, c)
        ],
        out_shape=[
            jax.ShapeDtypeStruct((tiles, half, 2, n, c), BF),
            jax.ShapeDtypeStruct((tiles, 4, n, c), F32),
            jax.ShapeDtypeStruct((tiles, 4, n, c), BF),
            jax.ShapeDtypeStruct((tiles, half, half, c), BF),
        ],
        scratch_shapes=[
            pltpu.VMEM((half + 1, n_p, 768), BF),
            pltpu.VMEM((n * 8, 128), F32),
            pltpu.VMEM((m * n, 128), F32),
            pltpu.VMEM((2, n, 128), F32),
            pltpu.VMEM((1536, 256), BF),
        ],
        compiler_params=params(),
        cost_estimate=pl.CostEstimate(
            flops=tiles * n * n * 2 * 1536 * 128, bytes_accessed=tiles * n * n * 600, transcendentals=tiles * n * n * 128
        ),
        name="enc_conv",
    )(*args)
    strips = lambda a: a.reshape(tiles * 4, n, c)
    return y.reshape(tiles, n, n, c), strips(sums), strips(ring), s


def dec_conv(x, rim, u, urim, w, want):
    tiles, n, _, c = x.shape
    half, n_p = n // 2, up16(n)
    g = group_of(tiles, want)
    m = pair_chunks(n, DEC_PAIRS.get(n, 6))[0][1]
    args = [x, rim.reshape(tiles, 4, n, c), u]
    specs = [tile_spec(g, n, n, c), tile_spec(g, 4, n, c), tile_spec(g, half, half, c)]
    if urim is not None:
        args.append(urim.reshape(tiles, 4, half, c))
        specs.append(tile_spec(g, 4, half, c))
    args.append(w.reshape(9, 2 * c, c))
    specs.append(whole_spec((9, 2 * c, c)))
    rows = (half + 1, 2 * half, 384) if in_pairs(half) else (half + 2, up16(half), 384)

    def kernel(*refs):
        dec_kernel(urim is not None, *refs)

    y, sums = pl.pallas_call(
        kernel,
        grid=(tiles // g,),
        in_specs=specs,
        out_specs=[tile_spec(g, half, 2, n, c), tile_spec(g, 4, n, c)],
        out_shape=[
            jax.ShapeDtypeStruct((tiles, half, 2, n, c), BF),
            jax.ShapeDtypeStruct((tiles, 4, n, c), F32),
        ],
        scratch_shapes=[
            pltpu.VMEM((half + 1, n_p, 768), BF),
            pltpu.VMEM(rows, BF),
            pltpu.VMEM((n * 8, 128), F32),
            pltpu.VMEM((2, m, n_p, 128), F32),
            pltpu.VMEM((1536, 256), BF),
            pltpu.VMEM((2, 3, 256, 256), BF),
        ],
        compiler_params=params(),
        cost_estimate=pl.CostEstimate(
            flops=tiles * n * n * 2 * 2300 * 128, bytes_accessed=tiles * n * n * 600, transcendentals=tiles * n * n * 128
        ),
        name="dec_conv",
    )(*args)
    return y.reshape(x.shape), sums.reshape(tiles * 4, n, c)


def strips_of(field, ring=0):
    n = field.shape[1]
    far = n - 1 - ring
    out = jnp.stack([field[:, ring], field[:, :, far], field[:, far], field[:, :, ring]], axis=1)
    out = jnp.pad(out, ((0, 0), (0, 0), (0, strip_rows(n) - n), (0, 0)))
    return out.reshape(field.shape[0] * 4, strip_rows(n), field.shape[3])


def patched(field, rim):
    tiles, n, _, c = field.shape
    rim = rim.reshape(tiles, 4, -1, c)[:, :, :n]
    middle = jnp.concatenate(
        [rim[:, 3, 1 : n - 1, None], field[:, 1 : n - 1, 1 : n - 1], rim[:, 1, 1 : n - 1, None]], axis=2
    )
    return jnp.concatenate([rim[:, 0][:, None], middle, rim[:, 2][:, None]], axis=1)


def inner_sums(field, weight):
    return lax.conv_general_dilated(
        field,
        weight,
        (1, 1),
        ((1, 1), (1, 1)),
        dimension_numbers=("NHWC", "HWIO", "NHWC"),
        preferred_element_type=F32,
    )


def shrink(field):
    count, length, _, channels = field.shape
    blocks = field.astype(F32).reshape(count, length // 2, 2, length // 2, 2, channels)
    return (jnp.sum(blocks, axis=(2, 4)) * 0.25).astype(BF)


def enlarge(field):
    return jnp.repeat(jnp.repeat(field, 2, axis=1), 2, axis=2)


def per_device(features, edge_table, w_enc0, w_enc1, w_enc2, w_mid, w_dec2, w_dec1, w_dec0):
    tiles, n0 = features.shape[0], features.shape[1]
    devices = lax.axis_size("tile")
    position = lax.axis_index("tile")
    cap = pair_capacity(FACE_TILES, tiles)
    rows = devices * cap
    slot_row = send_slots(edge_table, position, tiles, cap)

    def trade(strips):
        out = lax.all_to_all(strips.reshape(devices, -1, 128), "tile", split_axis=0, concat_axis=0, tiled=True)
        return out.reshape(strips.shape)

    def step(n, *args, **kw):
        return rim_step(n, devices, cap, plan, *args, **kw)

    def after(value, token):
        return lax.optimization_barrier((value, token))[0]

    rim0, send = tile_rims(features, slot_row, rows)
    rim0 = rim0.reshape(tiles * 4, n0, 128)
    plan = receive_plan(after(edge_table, send), slot_row, position, tiles, cap, devices)
    recv = trade(send)
    enc0, sums, ring, x1 = enc_conv(features, None, w_enc0, 1)
    enc0_rim, x1_rim, send = step(n0, recv, rim0, sums, w=w_enc0, ring=ring)

    recv = trade(send)
    enc1, sums, ring, x2 = enc_conv(x1, x1_rim, w_enc1, 4)
    enc1_rim, x2_rim, send = step(n0 // 2, recv, x1_rim, sums, w=w_enc1, ring=ring)

    recv = trade(send)
    sums = inner_sums(patched(x2, x2_rim), w_enc2)
    enc2 = jax.nn.silu(sums).astype(BF)
    enc2_rim, x3_rim, send = step(
        n0 // 4, recv, x2_rim, strips_of(sums), w=w_enc2, ring=strips_of(enc2, 1)
    )

    recv = trade(send)
    sums = inner_sums(patched(shrink(enc2), x3_rim), w_mid)
    middle = jax.nn.silu(sums).astype(BF)
    skip2 = skip_step(n0 // 4, plan, enc2_rim, w_dec2)
    skip0 = skip_step(n0, plan, after(enc0_rim, x3_rim), w_dec0)
    sums, skip0 = lax.optimization_barrier((sums, skip0))
    mid_rim, own, send = step(
        n0 // 8, recv, x3_rim, strips_of(sums), w=w_mid,
        skip=skip2, wn=w_dec2,
    )

    recv = trade(send)
    joined = jnp.concatenate([enlarge(patched(middle, mid_rim)), patched(enc2, enc2_rim)], axis=3)
    sums = inner_sums(joined, w_dec2)
    dec2 = jax.nn.silu(sums).astype(BF)
    skip1 = skip_step(n0 // 2, plan, after(enc1_rim, mid_rim), w_dec1)
    dec2_rim, own, send = step(
        n0 // 4, recv, own, strips_of(sums), skip=skip1, wn=w_dec1
    )

    recv = trade(send)
    dec1, sums = dec_conv(enc1, enc1_rim, patched(dec2, dec2_rim), None, w_dec1, 4)
    dec1_rim, own, send = step(
        n0 // 2, recv, own, sums, skip=skip0, wn=w_dec0
    )

    recv = trade(send)
    dec0, sums = dec_conv(enc0, enc0_rim, dec1, dec1_rim, w_dec0, 1)
    return last_step(dec0, plan, recv, own, sums)


def solution(mesh):
    return jax.shard_map(
        per_device,
        mesh=mesh,
        in_specs=(P(("grp", "tile"), None, None, None), P(), P(), P(), P(), P(), P(), P(), P()),
        out_specs=P(("grp", "tile"), None, None, None),
        check_vma=False,
    )
```
